32 devices in a mesh: rows: 2 (over core), seq: 16 (over z, y, x).
Axes of the slice: x: 2, y: 2, z: 4, core: 2. Of those that a mesh axis runs over, the one named last changes fastest.
Arguments:
- tokens: bfloat16 [2, 4096, 768], P('rows', 'seq'), may hold values from -6 to 6
- cotangent: bfloat16 [2, 4096, 768], P('rows', 'seq'), may hold values from -6 to 6
- w_query: bfloat16 [768, 768], replicated, may hold values from -0.21875 to 0.21875
- w_key: bfloat16 [768, 768], replicated, may hold values from -0.21875 to 0.21875
- w_value: bfloat16 [768, 768], replicated, may hold values from -0.21875 to 0.21875
- w_output: bfloat16 [768, 768], replicated, may hold values from -1.75 to 1.75
- w_inner: bfloat16 [768, 3072], replicated, may hold values from -0.21875 to 0.21875
- w_outer: bfloat16 [3072, 768], replicated, may hold values from -0.109375 to 0.109375
- rel_table: bfloat16 [512, 768], replicated, may hold values from -6 to 6
- mid_gain: float32 [768], replicated, may hold values from 0.1 to 1.9
- mid_bias: float32 [768], replicated, may hold values from -3 to 3
- end_gain: float32 [768], replicated, may hold values from 0.1 to 1.9
- end_bias: float32 [768], replicated, may hold values from -3 to 3
- seq_lengths: int32 [2, 4], P('rows'), may hold values from 1 to 4093, as said below
- pad_mask: int32 [2, 4096], P('rows'), may hold values 0 or 1
- rel_buckets: int32 [512], replicated, may hold values from -256 to 255
Outputs:
- layer_out: bfloat16 [2, 4096, 768], P('rows', 'seq')
- tokens_grad: bfloat16 [2, 4096, 768], P('rows', 'seq')
- w_query_grad: float32 [768, 768], replicated
- w_key_grad: float32 [768, 768], replicated
- w_value_grad: float32 [768, 768], replicated
- w_output_grad: float32 [768, 768], replicated
- w_inner_grad: float32 [768, 3072], replicated
- w_outer_grad: float32 [3072, 768], replicated
- rel_table_grad: float32 [512, 768], replicated
- mid_gain_grad: float32 [768], replicated
- mid_bias_grad: float32 [768], replicated
- end_gain_grad: float32 [768], replicated
- end_bias_grad: float32 [768], replicated
The draws below stay inside these ranges and needn't reach their ends.
Inputs may be any that keep to these rules, and one draw needn't show every extreme that they name: `seq_lengths`: in each row the 4 lengths sum to 4096; all but one are at most 64, and in one row those are all 1.
All inputs are finite; a program needn't handle non-finite values. No bound on the sum of `pad_mask` on one device may be relied on, other than what follows from the above.
Results may differ from the reference program's by a relative error of at most 0.02.
Values may be sent and summed in bfloat16 or wider, within the bound.
A program may use at most 256 MiB of HBM per device.

```python
import math
import jax
import jax.numpy as jnp
from jax import lax

D = 768
H = 12
DH = 64
FF = 3072
SPAN = 256
NSEG = 4
BLOCK = 256
ROWS = 2
ROW_LEN = 4096


def draw_seq_lengths(key, part):
    key = jax.random.fold_in(key, 11)
    key_short, key_slot, key_row = jax.random.split(key, 3)
    short_len = jax.random.randint(key_short, (ROWS, NSEG), 1, BLOCK // 4 + 1)
    long_slot = jax.random.randint(key_slot, (ROWS, 1), 0, NSEG)
    ones_row = jax.random.randint(key_row, (1, 1), 0, ROWS)
    row_ids = jnp.arange(ROWS)[:, None]
    short_len = jnp.where(row_ids == ones_row, 1, short_len)
    is_long = jnp.arange(NSEG)[None, :] == long_slot
    others = jnp.sum(jnp.where(is_long, 0, short_len), axis=1, keepdims=True)
    return jnp.where(is_long, ROW_LEN - others, short_len).astype(jnp.int32)


def set_ends(result, rng, low, top_value):
    spot = [jax.random.randint(jax.random.fold_in(rng, axis), (), 0, length) for axis, length in enumerate(result.shape)]
    longest = result.shape.index(max(result.shape))
    next_to = spot[:longest] + [(spot[longest] + 1) % result.shape[longest]] + spot[longest + 1:]
    return result.at[tuple(spot)].set(low).at[tuple(next_to)].set(top_value)


def block_scale(rng, shape, shards, least, high):
    gain = 1.0
    for position, parts in shards:
        heights = jax.random.uniform(jax.random.fold_in(jax.random.fold_in(rng, 6), position), (parts,), jnp.float32, least / len(shards), high / len(shards))
        gain = gain * jnp.repeat(jnp.exp(heights), shape[position] // parts).reshape((-1,) + (1,) * (len(shape) - 1 - position))
    return gain


def centred(own_key, extent, scale, limit, shards=(), kind=jnp.bfloat16):
    drawn = jax.random.normal(own_key, extent, jnp.float32) * scale
    if len(shards) > 0:
        drawn = block_scale(own_key, extent, shards, -0.22, 0.18) * drawn
    return jnp.clip(drawn, min=-limit, max=limit).astype(kind)


def setup_inputs(seed: int = 0) -> dict:
    key_of = jax.random.split(jax.random.key(seed), 17)
    return {
        "tokens": centred(key_of[0], (ROWS, ROW_LEN, D), 1.0, 6.0, ((0, 2), (1, 16))),
        "cotangent": centred(key_of[1], (ROWS, ROW_LEN, D), 1.0, 6.0, ((0, 2), (1, 16))),
        "w_query": centred(key_of[2], (D, D), D ** -0.5, 0.21875),
        "w_key": centred(key_of[3], (D, D), D ** -0.5, 0.21875),
        "w_value": centred(key_of[4], (D, D), D ** -0.5, 0.21875),
        "w_output": centred(key_of[5], (D, D), (D // 64) ** -0.5, 1.75),
        "w_inner": centred(key_of[6], (D, FF), D ** -0.5, 0.21875),
        "w_outer": centred(key_of[7], (FF, D), FF ** -0.5, 0.109375),
        "rel_table": centred(key_of[8], (2 * SPAN, D), 1.0, 6.0),
        "mid_gain": jnp.clip(1.0 + 0.18 * jax.random.normal(key_of[9], (D,), jnp.float32), 0.1, 1.9),
        "mid_bias": centred(key_of[10], (D,), 0.5, 3.0, (), jnp.float32),
        "end_gain": jnp.clip(1.0 + 0.18 * jax.random.normal(key_of[11], (D,), jnp.float32), 0.1, 1.9),
        "end_bias": centred(key_of[12], (D,), 0.5, 3.0, (), jnp.float32),
        "seq_lengths": draw_seq_lengths(jax.random.fold_in(key_of[16], 71), 0),
        "pad_mask": set_ends((jax.random.randint(key_of[14], (ROWS, ROW_LEN), 0, 8) < 7).astype(jnp.int32), jax.random.fold_in(key_of[14], 1), 0, 1),
        "rel_buckets": set_ends(jax.random.randint(key_of[15], (2 * SPAN,), -SPAN, SPAN), jax.random.fold_in(key_of[15], 1), -SPAN, SPAN - 1).astype(jnp.int32),
    }


@jax.custom_vjp
def low(v):
    return lax.optimization_barrier(v.astype(jnp.bfloat16)).astype(jnp.float32)

@jax.custom_vjp
def low_back(v):
    return v

def low_keep(v):
    return (low(v), None)

def low_pass(kept, grad):
    return (grad,)

def back_keep(v):
    return (v, None)

def back_low(kept, grad):
    return (low(grad),)
low.defvjp(low_keep, low_pass)
low_back.defvjp(back_keep, back_low)
norm_eps = 1e-07
masked_score = -1e+30
highest = lax.Precision.HIGHEST

def layer_norm(values, norm_gain, norm_bias):
    centre = values - lax.optimization_barrier(jnp.mean(values, axis=-1, keepdims=True))
    spread = lax.optimization_barrier(jnp.mean(centre * centre, axis=-1, keepdims=True))
    return centre * lax.rsqrt(spread + norm_eps) * norm_gain + norm_bias

def matmul(left, right):
    return jnp.einsum('rtd,de->rte', left, right, precision=highest)

def relative_indices(rel_buckets):
    ext_len = BLOCK + 2 * SPAN
    query_pos = jnp.arange(BLOCK, dtype=jnp.int32)[:, None]
    key_pos = jnp.arange(ext_len, dtype=jnp.int32)[None, :]
    offset = jnp.clip(query_pos - key_pos + 2 * SPAN, 0, 2 * SPAN - 1).astype(jnp.int32)
    bucket = jnp.take(rel_buckets, offset).astype(jnp.int32)
    to_index = jnp.clip(bucket + SPAN, 0, 2 * SPAN - 1).astype(jnp.int32)
    from_index = jnp.clip(SPAN - bucket, 0, 2 * SPAN - 1).astype(jnp.int32)
    inside = jnp.abs(query_pos - key_pos + SPAN) < SPAN
    diagonal = key_pos == query_pos + SPAN
    return (to_index, from_index, inside, diagonal)

def block_attention(query_block_rows, key_blk, value_blk, seg_query, seg_key, keep_key, rel_key, rel_query, to_index, from_index, inside, diagonal):
    score_scale = 1.0 / math.sqrt(3 * DH)
    content = jnp.einsum('ihd,jhd->hij', query_block_rows, key_blk, precision=highest)
    to_table = low_back(jnp.einsum('ihd,rhd->hir', query_block_rows, rel_key, precision=highest))
    from_table = low_back(jnp.einsum('rhd,jhd->hrj', rel_query, key_blk, precision=highest))
    full_shape = (query_block_rows.shape[1],) + to_index.shape
    to_term = jnp.take_along_axis(to_table, jnp.broadcast_to(to_index, full_shape), axis=2)
    from_term = jnp.take_along_axis(from_table, jnp.broadcast_to(from_index, full_shape), axis=1)
    scores = low_back((content + to_term + from_term) * score_scale)
    allowed = (seg_query[:, None] == seg_key[None, :]) & inside & ((keep_key[None, :] == 1) | diagonal)
    prob_vals = jax.nn.softmax(jnp.where(allowed[None], scores, masked_score), axis=-1)
    return jnp.einsum('hij,jhd->ihd', low(prob_vals), value_blk, precision=highest)

def layer_forward(tokens, w_query, w_key, w_value, w_output, w_inner, w_outer, rel_table, mid_gain, mid_bias, end_gain, end_bias, seq_lengths, pad_mask, rel_buckets):
    row_total, row_len, model_width = tokens.shape
    blocks = row_len // BLOCK
    ext_len = BLOCK + 2 * SPAN
    query_all = low_back(low(matmul(tokens, w_query)))
    key_all = low_back(low(matmul(tokens, w_key)))
    value_all = low_back(low(matmul(tokens, w_value)))
    rel_key = low_back(low(jnp.dot(rel_table, w_key, precision=highest))).reshape(2 * SPAN, H, DH)
    rel_query = low_back(low(jnp.dot(rel_table, w_query, precision=highest))).reshape(2 * SPAN, H, DH)
    seq_ends = jnp.cumsum(seq_lengths, axis=1).astype(jnp.int32)
    slot_ids = jnp.arange(row_len, dtype=jnp.int32)
    segment = lax.optimization_barrier(jnp.sum((slot_ids[None, :, None] >= seq_ends[:, None, :]).astype(jnp.int32), axis=2)).astype(jnp.int32)
    window_length = (jnp.arange(blocks, dtype=jnp.int32)[:, None] * BLOCK + jnp.arange(ext_len, dtype=jnp.int32)[None, :]).astype(jnp.int32)

    def extend(values, fill_value):
        widths = ((0, 0), (SPAN, SPAN)) + ((0, 0),) * (values.ndim - 2)
        padded = jnp.pad(values, widths, constant_values=fill_value)
        return padded[:, window_length]
    key_ext = extend(key_all, 0.0).reshape(row_total * blocks, ext_len, H, DH)
    value_ext = extend(value_all, 0.0).reshape(row_total * blocks, ext_len, H, DH)
    seg_key = extend(segment, -1).reshape(row_total * blocks, ext_len)
    keep_key = extend(pad_mask, 0).reshape(row_total * blocks, ext_len)
    query_blocks = query_all.reshape(row_total * blocks, BLOCK, H, DH)
    seg_query = segment.reshape(row_total * blocks, BLOCK)
    to_index, from_index, inside, diagonal = relative_indices(rel_buckets)
    checked = jax.checkpoint(block_attention)

    def one_block(block_items):
        return checked(*block_items, rel_key, rel_query, to_index, from_index, inside, diagonal)
    attn = lax.map(one_block, (query_blocks, key_ext, value_ext, seg_query, seg_key, keep_key))
    attn = low_back(low(attn.reshape(row_total, row_len, model_width)))
    mixed_out = low_back(matmul(attn, w_output))
    hidden = layer_norm(tokens + mixed_out, mid_gain, mid_bias)
    inner_pre = low_back(matmul(low(hidden), w_inner))
    active = low(jax.nn.gelu(inner_pre, approximate=False))
    outer_out = low_back(matmul(active, w_outer))
    return layer_norm(hidden + outer_out, end_gain, end_bias)

def reference(tokens, cotangent, w_query, w_key, w_value, w_output, w_inner, w_outer, rel_table, mid_gain, mid_bias, end_gain, end_bias, seq_lengths, pad_mask, rel_buckets):
    floats = [arr.astype(jnp.float32) for arr in (tokens, w_query, w_key, w_value, w_output, w_inner, w_outer, rel_table, mid_gain, mid_bias, end_gain, end_bias)]

    def forward(*values):
        return layer_forward(*values, seq_lengths, pad_mask, rel_buckets)
    forward_out, pull_back = jax.vjp(forward, *floats)
    gradients = pull_back(cotangent.astype(jnp.float32))
    return (forward_out.astype(jnp.bfloat16), gradients[0].astype(jnp.bfloat16), gradients[1], gradients[2], gradients[3], gradients[4], gradients[5], gradients[6], gradients[7], gradients[8], gradients[9], gradients[10], gradients[11])
```

```python
import functools
import math

import jax
import jax.numpy as jnp
from jax import lax
from jax.experimental import pallas as pl
from jax.experimental.pallas import tpu as pltpu
from jax.sharding import PartitionSpec as P

H = 12
DH = 64
SPAN = 256
TILE = 128
REACH = 640
PAIR = 128
score_scale = 1.0 / math.sqrt(3 * DH)


def nt(left, right):
    return lax.dot_general(left, right, (((1,), (1,)), ((), ())), preferred_element_type=jnp.float32)


def nn(left, right):
    return lax.dot_general(left, right, (((1,), (0,)), ((), ())), preferred_element_type=jnp.float32)


def head_lanes(values, head):
    lane = lax.broadcasted_iota(jnp.int32, values.shape, 1)
    mine = (lane < DH) if head == 0 else (lane >= DH)
    return jnp.where(mine, values, jnp.zeros_like(values))


def unit(reverse):
    row = lax.broadcasted_iota(jnp.int32, (TILE, TILE), 0)
    col = lax.broadcasted_iota(jnp.int32, (TILE, TILE), 1)
    hit = (row + col == TILE - 1) if reverse else (row == col)
    return jnp.where(hit, 1.0, 0.0).astype(jnp.bfloat16)


def attend_kernel(q_ref, k_ref, vt_ref, relk_ref, relq_ref, bias_ref, attn_ref, prob_ref, score_ref):
    eye = unit(False)
    log_two = score_scale * math.log2(math.e)
    tiles = q_ref.shape[0] // TILE
    for tile in range(tiles):
        first = tile * TILE
        q_tile = q_ref[pl.ds(first, TILE), :]
        for head in range(2):
            q_head = head_lanes(q_tile, head)
            band = nt(q_head, relk_ref[...])
            band = jnp.concatenate([band, jnp.zeros((TILE, REACH - 2 * SPAN), jnp.float32)], axis=1)
            to_term = pltpu.roll(band, 0, 1, stride=1, stride_axis=0).astype(jnp.bfloat16)
            for part in range(REACH // TILE):
                at = first + part * TILE
                k_part = k_ref[pl.ds(at, TILE), :]
                window = relq_ref[pl.ds((REACH // TILE - 1 - part) * TILE, 2 * TILE), :]
                from_band = nt(head_lanes(k_part, head), window)
                from_term = pltpu.roll(from_band, TILE + 1, 1, stride=1, stride_axis=0)[:, :TILE]
                left = jnp.concatenate([k_part, eye], axis=1)
                right = jnp.concatenate(
                    [q_head, to_term[:, part * TILE : (part + 1) * TILE]], axis=1
                )
                score_ref[pl.ds(part * TILE, TILE), :] = (
                    nt(left, right) + from_term + bias_ref[pl.ds(at, TILE), pl.ds(first, TILE)]
                )
            scores = score_ref[...]
            top = jnp.max(scores, axis=0, keepdims=True)
            weights = jnp.exp2((scores - top) * log_two)
            total = jnp.sum(weights, axis=0, keepdims=True)
            probs = (weights * (1.0 / total)).astype(jnp.bfloat16)
            prob_ref[head, tile] = probs
            out = nn(vt_ref[pl.ds(head * DH, DH), pl.ds(first, REACH)], probs)
            attn_ref[pl.ds(head * DH, DH), pl.ds(first, TILE)] = out.astype(attn_ref.dtype)


def attend(query, key_ext, value_ext_t, relk, relq, bias):
    block_len, width = query.shape
    ext_len = key_ext.shape[0]
    tiles = block_len // TILE
    pairs = width // PAIR
    return pl.pallas_call(
        attend_kernel,
        grid=(pairs,),
        in_specs=[
            pl.BlockSpec((block_len, PAIR), lambda p: (0, p)),
            pl.BlockSpec((ext_len, PAIR), lambda p: (0, p)),
            pl.BlockSpec((PAIR, ext_len), lambda p: (p, 0)),
            pl.BlockSpec((2 * SPAN, PAIR), lambda p: (0, p)),
            pl.BlockSpec((2 * SPAN + 2 * TILE, PAIR), lambda p: (0, p)),
            pl.BlockSpec((ext_len, block_len), lambda p: (0, 0)),
        ],
        out_specs=[
            pl.BlockSpec((PAIR, block_len), lambda p: (p, 0)),
            pl.BlockSpec((2, tiles, REACH, TILE), lambda p: (p, 0, 0, 0)),
        ],
        out_shape=[
            jax.ShapeDtypeStruct((width, block_len), jnp.bfloat16),
            jax.ShapeDtypeStruct((2 * pairs, tiles, REACH, TILE), jnp.bfloat16),
        ],
        scratch_shapes=[pltpu.VMEM((REACH, TILE), jnp.float32)],
        compiler_params=pltpu.CompilerParams(vmem_limit_bytes=48 * 2**20),
        name="attend",
    )(query, key_ext, value_ext_t, relk, relq, bias)


def attend_back_kernel(
    q_ref, k_ref, v_ref, grad_ref, prob_ref, relk_ref, relq_ref,
    dq_ref, dk_ref, dv_ref, drelk_ref, drelq_ref, qt_ref, kt_ref,
):
    swap = unit(True)
    for source, result in ((q_ref, qt_ref), (k_ref, kt_ref)):
        for at in range(0, source.shape[0], TILE):
            flipped = nn(swap, source[pl.ds(at, TILE), :])
            result[:, pl.ds(at, TILE)] = flipped.T.astype(jnp.bfloat16)
    row = lax.broadcasted_iota(jnp.int32, (TILE, TILE), 0)
    col = lax.broadcasted_iota(jnp.int32, (TILE, TILE), 1)
    parts = REACH // TILE
    tiles = q_ref.shape[0] // TILE
    dk_ref[...] = jnp.zeros_like(dk_ref)
    dv_ref[...] = jnp.zeros_like(dv_ref)
    drelk_ref[...] = jnp.zeros_like(drelk_ref)
    drelq_ref[...] = jnp.zeros_like(drelq_ref)
    for tile in range(tiles):
        first = tile * TILE
        q_tile = q_ref[pl.ds(first, TILE), :]
        grad_tile = grad_ref[pl.ds(first, TILE), :]
        v_tile = v_ref[pl.ds(first, REACH), :]
        q_heads = [head_lanes(q_tile, head) for head in range(2)]
        grad_heads = [head_lanes(grad_tile, head) for head in range(2)]
        dq_heads = []
        lefts = [[] for _ in range(parts)]
        for head in range(2):
            lanes = pl.ds(head * DH, DH)
            probs = prob_ref[head, tile].astype(jnp.float32)
            weighted = probs * nt(v_tile, grad_heads[head])
            delta = jnp.sum(weighted, axis=0, keepdims=True)
            dscore = ((weighted - probs * delta) * score_scale).astype(jnp.bfloat16)
            turned = nt(swap, dscore)
            dband = pltpu.roll(turned, REACH - TILE + 1, 1, stride=1, stride_axis=0)
            dband = dband[:, : 2 * SPAN].astype(jnp.bfloat16)
            dq_heads.append(
                nn(turned.astype(jnp.bfloat16), k_ref[pl.ds(first, REACH), :])
                + nn(dband, relk_ref[...])
            )
            drelk_ref[lanes, :] += nn(qt_ref[lanes, pl.ds(first, TILE)], dband)
            for part in range(parts):
                flipped = nn(swap, dscore[part * TILE : (part + 1) * TILE, :])
                spun = pltpu.roll(flipped, 0, 1, stride=1, stride_axis=0)
                low = jnp.where(col >= row, spun, 0.0)
                dfrom = jnp.concatenate([low, spun - low], axis=1).astype(jnp.bfloat16)
                window = pl.ds((parts - 1 - part) * TILE, 2 * TILE)
                drelq_ref[lanes, window] += nn(kt_ref[lanes, pl.ds(first + part * TILE, TILE)], dfrom)
                lefts[part] += [flipped.astype(jnp.bfloat16), dfrom]
        dq_turned = jnp.where(col < DH, dq_heads[0], dq_heads[1]).astype(jnp.bfloat16)
        dq_ref[pl.ds(first, TILE), :] = nn(swap, dq_turned).astype(dq_ref.dtype)
        dv_ref[pl.ds(first, REACH), :] += nn(
            jnp.concatenate([prob_ref[0, tile], prob_ref[1, tile]], axis=1),
            jnp.concatenate(grad_heads, axis=0),
        )
        for part in range(parts):
            window = relq_ref[pl.ds((parts - 1 - part) * TILE, 2 * TILE), :]
            right = jnp.concatenate(
                [q_heads[0], head_lanes(window, 0), q_heads[1], head_lanes(window, 1)], axis=0
            )
            dk_ref[pl.ds(first + part * TILE, TILE), :] += nn(
                jnp.concatenate(lefts[part], axis=1), right
            )


def attend_back(query, key_ext, value_ext, grad, probs, relk, relq):
    block_len, width = query.shape
    ext_len = key_ext.shape[0]
    tiles = block_len // TILE
    pairs = width // PAIR
    table = 2 * SPAN
    cols = lambda n: pl.BlockSpec((n, PAIR), lambda p: (0, p))
    rows = lambda n: pl.BlockSpec((PAIR, n), lambda p: (p, 0))
    f32 = lambda *s: jax.ShapeDtypeStruct(s, jnp.float32)
    return pl.pallas_call(
        attend_back_kernel,
        grid=(pairs,),
        in_specs=[
            cols(block_len), cols(ext_len), cols(ext_len), cols(block_len),
            pl.BlockSpec((2, tiles, REACH, TILE), lambda p: (p, 0, 0, 0)),
            cols(table), cols(table + 2 * TILE),
        ],
        out_specs=[cols(block_len), cols(ext_len), cols(ext_len), rows(table), rows(table + 2 * TILE)],
        out_shape=[
            jax.ShapeDtypeStruct((block_len, width), jnp.bfloat16),
            f32(ext_len, width), f32(ext_len, width), f32(width, table), f32(width, table + 2 * TILE),
        ],
        scratch_shapes=[
            pltpu.VMEM((PAIR, block_len), jnp.bfloat16), pltpu.VMEM((PAIR, ext_len), jnp.bfloat16),
        ],
        compiler_params=pltpu.CompilerParams(vmem_limit_bytes=48 * 2**20),
        name="attend_back",
    )(query, key_ext, value_ext, grad, probs, relk, relq)


norm_eps = 1e-07
masked_score = -1e30


def shifted(shard, axis, by):
    count = lax.axis_size(axis)
    pairs = [(i, i + by) for i in range(count) if 0 <= i + by < count]
    return lax.ppermute(shard, axis, pairs)


def layer_norm(values, norm_gain, norm_bias):
    centre = values - jnp.mean(values, axis=-1, keepdims=True)
    spread = jnp.mean(centre * centre, axis=-1, keepdims=True)
    return centre * lax.rsqrt(spread + norm_eps) * norm_gain + norm_bias


def f32dot(spec, left, right):
    return jnp.einsum(spec, left, right, preferred_element_type=jnp.float32)


def segment_of(slot_ids, seq_ends):
    return jnp.sum((slot_ids[:, None] >= seq_ends[None, :]).astype(jnp.int32), axis=1)


def mask_bias(seq_lengths, pad_mask, block_len, seq_count):
    ext_len = block_len + 2 * SPAN
    seq_place = lax.axis_index("seq")
    row_len = block_len * seq_count
    seg_ids = jnp.arange(seq_lengths.shape[0], dtype=jnp.int32)
    seq_ends = jnp.sum(
        jnp.where(seg_ids[None, :] <= seg_ids[:, None], seq_lengths[None, :], 0), axis=1
    )
    query_slots = seq_place * block_len + jnp.arange(block_len, dtype=jnp.int32)
    key_slots = seq_place * block_len - SPAN + jnp.arange(ext_len, dtype=jnp.int32)
    seg_query = segment_of(query_slots, seq_ends)
    in_row = (key_slots >= 0) & (key_slots < row_len)
    seg_key = jnp.where(in_row, segment_of(key_slots, seq_ends), -1)
    keep_key = lax.dynamic_slice_in_dim(
        jnp.pad(pad_mask, (SPAN, SPAN)), seq_place * block_len, ext_len, 0
    )
    apart = key_slots[:, None] - query_slots[None, :]
    allowed = (
        (seg_key[:, None] == seg_query[None, :])
        & (jnp.abs(apart) < SPAN)
        & ((keep_key[:, None] == 1) | (apart == 0))
    )
    return jnp.where(allowed, 0.0, masked_score).astype(jnp.float32)


def band_tables(rel_buckets):
    span_ids = jnp.arange(2 * SPAN, dtype=jnp.int32)[None, :]
    back = rel_buckets[::-1]
    to_bucket = jnp.concatenate([back[:1], back[:-1]])
    from_bucket = jnp.concatenate([rel_buckets[1:], rel_buckets[-1:]])
    to_pos = jnp.clip(to_bucket + SPAN, 0, 2 * SPAN - 1)
    from_pos = jnp.clip(SPAN - from_bucket, 0, 2 * SPAN - 1)
    to_hot = (to_pos[:, None] == span_ids).astype(jnp.bfloat16)
    from_hot = (from_pos[:, None] == span_ids).astype(jnp.bfloat16)
    return to_hot, from_hot


def low(values):
    return values.astype(jnp.bfloat16)


def shards(
    tokens, cotangent, w_query, w_key, w_value, w_output, w_inner, w_outer, rel_table,
    mid_gain, mid_bias, end_gain, end_bias, seq_lengths, pad_mask, rel_buckets,
):
    tokens, cotangent = tokens[0], cotangent[0]
    block_len, width = tokens.shape
    seq_count = lax.axis_size("seq")
    prev = shifted(tokens, "seq", 1)
    following = shifted(tokens, "seq", -1)
    bias = mask_bias(seq_lengths[0], pad_mask[0], block_len, seq_count)
    to_hot, from_hot = band_tables(rel_buckets)
    to_table = low(f32dot("mr,re->me", to_hot, rel_table))
    from_table = low(f32dot("mr,re->me", from_hot, rel_table))
    relk = low(f32dot("me,ed->md", to_table, w_key))
    relq = low(f32dot("me,ed->md", from_table, w_query))
    relq = jnp.pad(relq, ((TILE, TILE), (0, 0)))
    query = low(f32dot("te,ed->td", tokens, w_query))
    tokens_ext = jnp.concatenate([prev, tokens, following], axis=0)
    key_ext = low(f32dot("te,ed->td", tokens_ext, w_key))
    value_ext = low(f32dot("te,ed->td", tokens_ext, w_value))
    attn_t, probs = attend(query, key_ext, value_ext.T, relk, relq, bias)

    mixed = f32dot("dt,de->te", attn_t, w_output)
    hidden, mid_back = jax.vjp(layer_norm, tokens.astype(jnp.float32) + mixed, mid_gain, mid_bias)
    hidden_low = low(hidden)
    inner = f32dot("td,df->tf", hidden_low, w_inner)
    active, gelu_back = jax.vjp(functools.partial(jax.nn.gelu, approximate=False), inner)
    active_low = low(active)
    outer = f32dot("tf,fd->td", active_low, w_outer)
    final, end_back = jax.vjp(layer_norm, hidden + outer, end_gain, end_bias)
    layer_out = low(final)
    sum_grad, end_gain_part, end_bias_part = end_back(cotangent.astype(jnp.float32))
    outer_low = low(sum_grad)
    outer_part = low(f32dot("tf,td->fd", active_low, outer_low))
    inner_low = low(gelu_back(f32dot("td,fd->tf", outer_low, w_outer))[0])
    inner_part = low(f32dot("td,tf->df", hidden_low, inner_low))
    hidden_grad = sum_grad + f32dot("tf,df->td", inner_low, w_inner)
    resid_grad, mid_gain_part, mid_bias_part = mid_back(hidden_grad)
    mixed_low = low(resid_grad)
    output_part = low(f32dot("dt,te->de", attn_t, mixed_low))
    attn_grad = low(f32dot("te,de->td", mixed_low, w_output))

    dquery, dkey, dvalue, drelk, drelq = attend_back(
        query, key_ext, value_ext, attn_grad, probs, relk, relq
    )
    pair = jnp.concatenate([dkey, dvalue], axis=1)
    from_next = shifted(low(pair[:SPAN]), "seq", -1).astype(jnp.float32)
    from_prev = shifted(low(pair[SPAN + block_len :]), "seq", 1).astype(jnp.float32)
    pair = low(pair[SPAN : SPAN + block_len] + from_prev + from_next)
    swap = unit(True)
    dkey = low(
        f32dot("ab,nbd->nad", swap, pair[:, :width].reshape(-1, TILE, width))
    ).reshape(block_len, width)
    dvalue = pair[:, width:]
    drelk = low(drelk)
    drelq = low(drelq[:, TILE : TILE + 2 * SPAN])
    query_part = low(f32dot("te,td->ed", tokens, dquery) + f32dot("me,dm->ed", from_table, drelq))
    key_part = low(f32dot("te,td->ed", tokens, dkey) + f32dot("me,dm->ed", to_table, drelk))
    value_part = low(f32dot("te,td->ed", tokens, dvalue))
    table_part = low(
        f32dot("mr,me->re", to_hot, low(f32dot("dm,ed->me", drelk, w_key)))
        + f32dot("mr,me->re", from_hot, low(f32dot("dm,ed->me", drelq, w_query)))
    )
    tokens_grad = low(
        resid_grad
        + f32dot("td,ed->te", dquery, w_query)
        + f32dot("td,ed->te", dkey, w_key)
        + f32dot("td,ed->te", dvalue, w_value)
    )
    norm_parts = lax.psum(
        (mid_gain_part, mid_bias_part, end_gain_part, end_bias_part), ("rows", "seq")
    )
    groups = (
        (outer_part,),
        tuple(inner_part[:, at : at + width] for at in range(0, inner_part.shape[1], width)),
        (query_part, key_part, value_part, output_part, table_part),
    )
    outs = []
    for group in groups:
        packed = jnp.concatenate(group, axis=0)
        share = lax.psum_scatter(packed, ("rows", "seq"), scatter_dimension=0, tiled=True)
        whole = lax.all_gather(share, ("rows", "seq"), axis=0, tiled=True).astype(jnp.float32)
        pieces, at = [], 0
        for piece in group:
            pieces.append(whole[at : at + piece.shape[0]])
            at += piece.shape[0]
        outs.append(pieces)
    (outer_w,), inner_w, (query_w, key_w, value_w, output_w, table_w) = outs
    inner_w = jnp.concatenate(inner_w, axis=1)
    return (
        layer_out[None], tokens_grad[None], query_w, key_w, value_w, output_w, inner_w, outer_w,
        table_w, *norm_parts,
    )


def solution(mesh):
    split = P("rows", "seq", None)
    return jax.shard_map(
        shards,
        mesh=mesh,
        in_specs=(split, split) + (P(),) * 11 + (P("rows", None), P("rows", None), P()),
        out_specs=(split, split) + (P(),) * 11,
        check_vma=False,
    )
```

```python
import functools
import math

import jax
import jax.numpy as jnp
from jax import lax
from jax.experimental import pallas as pl
from jax.experimental.pallas import tpu as pltpu
from jax.sharding import PartitionSpec as P

H = 12
DH = 64
SPAN = 256
TILE = 128
REACH = 640
PAIR = 128
score_scale = 1.0 / math.sqrt(3 * DH)


def nt(left, right):
    return lax.dot_general(left, right, (((1,), (1,)), ((), ())), preferred_element_type=jnp.float32)


def nn(left, right):
    return lax.dot_general(left, right, (((1,), (0,)), ((), ())), preferred_element_type=jnp.float32)


def head_lanes(values, head):
    lane = lax.broadcasted_iota(jnp.int32, values.shape, 1)
    mine = (lane < DH) if head == 0 else (lane >= DH)
    return jnp.where(mine, values, jnp.zeros_like(values))


def unit(reverse):
    row = lax.broadcasted_iota(jnp.int32, (TILE, TILE), 0)
    col = lax.broadcasted_iota(jnp.int32, (TILE, TILE), 1)
    hit = (row + col == TILE - 1) if reverse else (row == col)
    return jnp.where(hit, 1.0, 0.0).astype(jnp.bfloat16)


def attend_kernel(q_ref, k_ref, vt_ref, relk_ref, relq_ref, bias_ref, attn_ref, prob_ref, score_ref):
    eye = unit(False)
    log_two = score_scale * math.log2(math.e)
    tiles = q_ref.shape[0] // TILE
    for tile in range(tiles):
        first = tile * TILE
        q_tile = q_ref[pl.ds(first, TILE), :]
        for head in range(2):
            q_head = head_lanes(q_tile, head)
            band = nt(q_head, relk_ref[...])
            band = jnp.concatenate([band, jnp.zeros((TILE, REACH - 2 * SPAN), jnp.float32)], axis=1)
            to_term = pltpu.roll(band, 0, 1, stride=1, stride_axis=0).astype(jnp.bfloat16)
            for part in range(REACH // TILE):
                at = first + part * TILE
                k_part = k_ref[pl.ds(at, TILE), :]
                window = relq_ref[pl.ds((REACH // TILE - 1 - part) * TILE, 2 * TILE), :]
                from_band = nt(head_lanes(k_part, head), window)
                from_term = pltpu.roll(from_band, TILE + 1, 1, stride=1, stride_axis=0)[:, :TILE]
                left = jnp.concatenate([k_part, eye], axis=1)
                right = jnp.concatenate(
                    [q_head, to_term[:, part * TILE : (part + 1) * TILE]], axis=1
                )
                score_ref[pl.ds(part * TILE, TILE), :] = (
                    nt(left, right) + from_term + bias_ref[pl.ds(at, TILE), pl.ds(first, TILE)]
                )
            scores = score_ref[...]
            top = jnp.max(scores, axis=0, keepdims=True)
            weights = jnp.exp2((scores - top) * log_two)
            total = jnp.sum(weights, axis=0, keepdims=True)
            probs = (weights * (1.0 / total)).astype(jnp.bfloat16)
            prob_ref[head, tile] = probs
            out = nn(vt_ref[pl.ds(head * DH, DH), pl.ds(first, REACH)], probs)
            attn_ref[pl.ds(head * DH, DH), pl.ds(first, TILE)] = out.astype(attn_ref.dtype)


def attend(query, key_ext, value_ext_t, relk, relq, bias):
    block_len, width = query.shape
    ext_len = key_ext.shape[0]
    tiles = block_len // TILE
    pairs = width // PAIR
    return pl.pallas_call(
        attend_kernel,
        grid=(pairs,),
        in_specs=[
            pl.BlockSpec((block_len, PAIR), lambda p: (0, p)),
            pl.BlockSpec((ext_len, PAIR), lambda p: (0, p)),
            pl.BlockSpec((PAIR, ext_len), lambda p: (p, 0)),
            pl.BlockSpec((2 * SPAN, PAIR), lambda p: (0, p)),
            pl.BlockSpec((2 * SPAN + 2 * TILE, PAIR), lambda p: (0, p)),
            pl.BlockSpec((ext_len, block_len), lambda p: (0, 0)),
        ],
        out_specs=[
            pl.BlockSpec((PAIR, block_len), lambda p: (p, 0)),
            pl.BlockSpec((2, tiles, REACH, TILE), lambda p: (p, 0, 0, 0)),
        ],
        out_shape=[
            jax.ShapeDtypeStruct((width, block_len), jnp.bfloat16),
            jax.ShapeDtypeStruct((2 * pairs, tiles, REACH, TILE), jnp.bfloat16),
        ],
        scratch_shapes=[pltpu.VMEM((REACH, TILE), jnp.float32)],
        compiler_params=pltpu.CompilerParams(vmem_limit_bytes=48 * 2**20),
        name="attend",
    )(query, key_ext, value_ext_t, relk, relq, bias)


def attend_back_kernel(
    q_ref, k_ref, v_ref, grad_ref, prob_ref, relk_ref, relq_ref,
    dq_ref, dk_ref, dv_ref, drelk_ref, drelq_ref, qt_ref, kt_ref,
):
    swap = unit(True)
    for source, result in ((q_ref, qt_ref), (k_ref, kt_ref)):
        for at in range(0, source.shape[0], TILE):
            flipped = nn(swap, source[pl.ds(at, TILE), :])
            result[:, pl.ds(at, TILE)] = flipped.T.astype(jnp.bfloat16)
    row = lax.broadcasted_iota(jnp.int32, (TILE, TILE), 0)
    col = lax.broadcasted_iota(jnp.int32, (TILE, TILE), 1)
    parts = REACH // TILE
    tiles = q_ref.shape[0] // TILE
    dk_ref[...] = jnp.zeros_like(dk_ref)
    dv_ref[...] = jnp.zeros_like(dv_ref)
    drelk_ref[...] = jnp.zeros_like(drelk_ref)
    drelq_ref[...] = jnp.zeros_like(drelq_ref)
    for tile in range(tiles):
        first = tile * TILE
        q_tile = q_ref[pl.ds(first, TILE), :]
        grad_tile = grad_ref[pl.ds(first, TILE), :]
        v_tile = v_ref[pl.ds(first, REACH), :]
        q_heads = [head_lanes(q_tile, head) for head in range(2)]
        grad_heads = [head_lanes(grad_tile, head) for head in range(2)]
        dq_heads = []
        lefts = [[] for _ in range(parts)]
        for head in range(2):
            lanes = pl.ds(head * DH, DH)
            probs = prob_ref[head, tile].astype(jnp.float32)
            weighted = probs * nt(v_tile, grad_heads[head])
            delta = jnp.sum(weighted, axis=0, keepdims=True)
            dscore = ((weighted - probs * delta) * score_scale).astype(jnp.bfloat16)
            turned = nt(swap, dscore)
            dband = pltpu.roll(turned, REACH - TILE + 1, 1, stride=1, stride_axis=0)
            dband = dband[:, : 2 * SPAN].astype(jnp.bfloat16)
            dq_heads.append(
                nn(turned.astype(jnp.bfloat16), k_ref[pl.ds(first, REACH), :])
                + nn(dband, relk_ref[...])
            )
            drelk_ref[lanes, :] += nn(qt_ref[lanes, pl.ds(first, TILE)], dband)
            for part in range(parts):
                flipped = nn(swap, dscore[part * TILE : (part + 1) * TILE, :])
                spun = pltpu.roll(flipped, 0, 1, stride=1, stride_axis=0)
                low = jnp.where(col >= row, spun, 0.0)
                dfrom = jnp.concatenate([low, spun - low], axis=1).astype(jnp.bfloat16)
                window = pl.ds((parts - 1 - part) * TILE, 2 * TILE)
                drelq_ref[lanes, window] += nn(kt_ref[lanes, pl.ds(first + part * TILE, TILE)], dfrom)
                lefts[part] += [flipped.astype(jnp.bfloat16), dfrom]
        dq_turned = jnp.where(col < DH, dq_heads[0], dq_heads[1]).astype(jnp.bfloat16)
        dq_ref[pl.ds(first, TILE), :] = nn(swap, dq_turned).astype(dq_ref.dtype)
        dv_ref[pl.ds(first, REACH), :] += nn(
            jnp.concatenate([prob_ref[0, tile], prob_ref[1, tile]], axis=1),
            jnp.concatenate(grad_heads, axis=0),
        )
        for part in range(parts):
            window = relq_ref[pl.ds((parts - 1 - part) * TILE, 2 * TILE), :]
            right = jnp.concatenate(
                [q_heads[0], head_lanes(window, 0), q_heads[1], head_lanes(window, 1)], axis=0
            )
            dk_ref[pl.ds(first + part * TILE, TILE), :] += nn(
                jnp.concatenate(lefts[part], axis=1), right
            )


def attend_back(query, key_ext, value_ext, grad, probs, relk, relq):
    block_len, width = query.shape
    ext_len = key_ext.shape[0]
    tiles = block_len // TILE
    pairs = width // PAIR
    table = 2 * SPAN
    cols = lambda n: pl.BlockSpec((n, PAIR), lambda p: (0, p))
    rows = lambda n: pl.BlockSpec((PAIR, n), lambda p: (p, 0))
    f32 = lambda *s: jax.ShapeDtypeStruct(s, jnp.float32)
    return pl.pallas_call(
        attend_back_kernel,
        grid=(pairs,),
        in_specs=[
            cols(block_len), cols(ext_len), cols(ext_len), cols(block_len),
            pl.BlockSpec((2, tiles, REACH, TILE), lambda p: (p, 0, 0, 0)),
            cols(table), cols(table + 2 * TILE),
        ],
        out_specs=[cols(block_len), cols(ext_len), cols(ext_len), rows(table), rows(table + 2 * TILE)],
        out_shape=[
            jax.ShapeDtypeStruct((block_len, width), jnp.bfloat16),
            f32(ext_len, width), f32(ext_len, width), f32(width, table), f32(width, table + 2 * TILE),
        ],
        scratch_shapes=[
            pltpu.VMEM((PAIR, block_len), jnp.bfloat16), pltpu.VMEM((PAIR, ext_len), jnp.bfloat16),
        ],
        compiler_params=pltpu.CompilerParams(vmem_limit_bytes=48 * 2**20),
        name="attend_back",
    )(query, key_ext, value_ext, grad, probs, relk, relq)


MESH = pl.DeviceIdType.MESH
PACK = 16


def axes_of(seq_count):
    row, place = lax.axis_index("rows"), lax.axis_index("seq")
    first, second, third = place % 2, (place // 2) % 2, place // 4
    near = (first + row * (second - first), 1 + row, 2)
    cross = (second + row * (first - second), 2 - row, 2)
    far = (third, 4, seq_count // 4)
    return row, place, near, cross, far


class Line:
    def __init__(self, at, step, count):
        self.at, self.step, self.count = at, step, count

    def peers(self, row, place):
        for ahead in range(1, self.count):
            there = lax.rem(self.at + ahead, self.count)
            yield ahead - 1, there, {"rows": row, "seq": place + (there - self.at) * self.step}


class CoreLine(Line):
    def peers(self, row, place):
        yield 0, 1 - row, {"rows": 1 - row, "seq": place}


def add_rows(target, at, sources, rows, out=None, out_at=None):
    out, out_at = (target, at) if out is None else (out, out_at)
    step = 48 if rows % 48 == 0 else (32 if rows % 32 == 0 else PACK)

    def body(i, carry):
        here = pl.multiple_of(i * step, PACK)
        total = target[pl.ds(pl.multiple_of(at + here, PACK), step), :].astype(jnp.float32)
        for source in sources:
            total = total + source[pl.ds(here, step), :].astype(jnp.float32)
        out[pl.ds(pl.multiple_of(out_at + here, PACK), step), :] = total.astype(out.dtype)
        return carry

    lax.fori_loop(0, rows // step, body, 0)


class Chunk:
    def __init__(self, index, base, half, take, put, far_first):
        self.index, self.base, self.half = index, base, half
        self.take, self.put, self.far_first = take, put, far_first


def sum_plan(chunks, seq_count):
    plan = []
    for chunk in chunks:
        far = seq_count // 4
        counts = (2, far, 2, 2) if chunk.far_first else (2, 2, 2, far)
        rows, phases = 2 * chunk.half, []
        for count in counts:
            rows //= count
            phases.append((count, rows))
        plan.append(phases)
    return plan


def sum_kernel(chunks, seq_count, stride, *refs):
    n_in = len(SOURCES)
    ins, vec_in = refs[:n_in], refs[n_in]
    outs, vec_out = refs[n_in + 1 : 2 * n_in + 1], refs[2 * n_in + 1]
    acc, gat, recv, vec_acc, vec_recv, load_sem, send_sem, recv_sem, vec_send, vec_got, store_sem = refs[
        2 * n_in + 2 :
    ]
    row, place, near, cross, far = axes_of(seq_count)
    core = CoreLine(row, 0, 2)
    lines_a = (core, Line(*near), Line(*cross), Line(*far))
    lines_c = (core, Line(*far), Line(*near), Line(*cross))
    plan = sum_plan(chunks, seq_count)

    barrier = pltpu.get_barrier_semaphore()
    greeted = 0
    for line in lines_a:
        for _, _, device in line.peers(row, place):
            pl.semaphore_signal(barrier, inc=1, device_id=device, device_id_type=MESH)
            greeted += 1
    pl.semaphore_wait(barrier, greeted)

    def remote(source, target, sems, device):
        return pltpu.make_async_remote_copy(
            src_ref=source, dst_ref=target, send_sem=send_sem.at[sems], recv_sem=recv_sem.at[sems],
            device_id=device, device_id_type=MESH,
        )

    acc_at, recv_at, sem_at = [], [], []
    acc_rows = recv_rows = sems = 0
    for phases in plan:
        acc_at.append(acc_rows)
        acc_rows += phases[0][1]
        recv_at.append([])
        sem_at.append([])
        for count, rows in phases:
            recv_at[-1].append(recv_rows)
            recv_rows += (count - 1) * rows
            sem_at[-1].append((sems, sems + count - 1))
            sems += 2 * (count - 1)

    def lines_of(chunk):
        return lines_c if chunk.far_first else lines_a

    def offset(chunk, phase):
        at = 0
        for line, (count, rows) in list(zip(lines_of(chunk), plan[chunk.index]))[1 : phase + 1]:
            at = at + line.at * rows
        return at

    in_flight = {}

    def start_reduce(chunk, phase):
        c = chunk.index
        count, rows = plan[c][phase]
        line = lines_of(chunk)[phase]
        copies = []
        for slot, there, device in line.peers(row, place):
            if phase == 0:
                source = chunk.take(ins, there)
            else:
                at = acc_at[c] + offset(chunk, phase - 1) + there * rows
                source = acc.at[pl.ds(pl.multiple_of(at, PACK), rows)]
            target = recv.at[pl.ds(recv_at[c][phase] + slot * rows, rows)]
            copy = remote(source, target, sem_at[c][phase][0] + slot, device)
            copy.start()
            copies.append(copy)
        if phase == 0:
            load = pltpu.make_async_copy(
                chunk.take(ins, row), acc.at[pl.ds(acc_at[c], rows)], load_sem.at[c]
            )
            load.start()
            copies.append(load)
        in_flight[c] = copies

    def end_reduce(chunk, phase):
        c = chunk.index
        count, rows = plan[c][phase]
        for copy in in_flight.pop(c):
            copy.wait()
        sources = [
            recv.at[pl.ds(recv_at[c][phase] + slot * rows, rows)] for slot in range(count - 1)
        ]
        at = acc_at[c] + offset(chunk, phase)
        if phase == 3:
            home = chunk.base + row * chunk.half + offset(chunk, 3)
            add_rows(acc, at, sources, rows, gat, home)
        else:
            add_rows(acc, at, sources, rows)

    def start_gather(chunk, phase):
        c = chunk.index
        count, rows = plan[c][phase]
        line = lines_of(chunk)[phase]
        home = chunk.base + row * chunk.half + offset(chunk, phase)
        mine = gat.at[pl.ds(pl.multiple_of(home, PACK), rows)]
        copies = []
        for slot, there, device in line.peers(row, place):
            copy = remote(mine, mine, sem_at[c][phase][1] + slot, device)
            copy.start()
            copies.append(copy)
        in_flight[c] = copies

    def end_gather(chunk, phase):
        for copy in in_flight.pop(chunk.index):
            copy.wait()

    stores = []

    def store(chunk):
        for number, (source, target) in enumerate(chunk.put(gat, outs)):
            copy = pltpu.make_async_copy(source, target, store_sem.at[chunk.index, number])
            copy.start()
            stores.append(copy)

    def step(chunk, stage):
        if stage == 0:
            start_reduce(chunk, 0)
        elif stage < 4:
            end_reduce(chunk, stage - 1)
            start_reduce(chunk, stage)
        elif stage == 4:
            end_reduce(chunk, 3)
            start_gather(chunk, 3)
        elif stage < 8:
            end_gather(chunk, 8 - stage)
            start_gather(chunk, 7 - stage)
        else:
            end_gather(chunk, 0)
            store(chunk)

    vec_sems = [0]

    def vec_stage(stage):
        if stage == 0:
            vec_acc[...] = vec_in[...]
        else:
            first = vec_sems[0]
            copies = []
            for slot, _, device in lines_a[stage - 1].peers(row, place):
                copy = pltpu.make_async_remote_copy(
                    src_ref=vec_acc, dst_ref=vec_recv.at[first + slot], send_sem=vec_send.at[first + slot],
                    recv_sem=vec_got.at[first + slot], device_id=device, device_id_type=MESH,
                )
                copy.start()
                copies.append(copy)
            for copy in copies:
                copy.wait()
            vec_sems[0] += len(copies)
            for slot in range(len(copies)):
                vec_acc[...] += vec_recv[first + slot]

    events = sorted(
        (stride * chunk.index + stage, -stage, chunk.index) for chunk in chunks for stage in range(9)
    )
    vec_stage(0)
    next_vec = 1
    for slot, minus, c in events:
        step(chunks[c], -minus)
        if c == 0 and next_vec <= 4:
            vec_stage(next_vec)
            next_vec += 1
    vec_out[...] = vec_acc[...]
    for copy in stores:
        copy.wait()


SOURCES = ("outer", "inner", "rest")


def cut_rows(which, start, base, half):
    def take(refs, side):
        return refs[which].at[pl.ds(pl.multiple_of(start + side * half, PACK), half)]

    def put(gat, refs):
        return [(gat.at[pl.ds(base, 2 * half)], refs[which].at[pl.ds(start, 2 * half)])]

    return take, put


def cut_cols(which, start, base, half):
    def take(refs, side):
        return refs[which].at[:, pl.ds(pl.multiple_of(start + side * half, PAIR), half)]

    def put(gat, refs):
        return [
            (gat.at[pl.ds(base + side * half, half)], refs[which].at[:, pl.ds(start + side * half, half)])
            for side in range(2)
        ]

    return take, put


def chunks_of(outer, inner, rest, devices):
    unit = PACK * devices
    chunks, base = [], 0

    def add(cut, which, start, half, far_first=False):
        nonlocal base
        chunks.append(Chunk(len(chunks), base, half, *cut(which, start, base, half), far_first))
        base += 2 * half

    def split(which, total, parts):
        start, left = 0, total // unit
        for part in range(parts):
            units = -(-left // (parts - part))
            add(cut_rows, which, start, units * unit // 2)
            start, left = start + units * unit, left - units

    split(0, outer.shape[0], 2)
    width = inner.shape[0]
    for start in range(0, inner.shape[1], 2 * width):
        add(cut_cols, 1, start, width)
    split(2, rest.shape[0], 3)
    return chunks, base


def sum_over_devices(outer, inner, rest, vectors, seq_count):
    chunks, total = chunks_of(outer, inner, rest, 2 * seq_count)
    plan = sum_plan(chunks, seq_count)
    width = rest.shape[1]
    recv_rows = sum((count - 1) * rows for phases in plan for count, rows in phases)
    sems = sum(2 * (count - 1) for phases in plan for count, _ in phases)
    vec_slots = sum(count - 1 for count, _ in plan[0])
    any_spec = pl.BlockSpec(memory_space=pl.ANY)
    vmem = pl.BlockSpec(memory_space=pltpu.VMEM)
    return pl.pallas_call(
        functools.partial(sum_kernel, chunks, seq_count, 1),
        in_specs=[any_spec] * 3 + [vmem],
        out_specs=[any_spec] * 3 + [vmem],
        out_shape=[jax.ShapeDtypeStruct(a.shape, a.dtype) for a in (outer, inner, rest, vectors)],
        scratch_shapes=[
            pltpu.VMEM((total // 2, width), jnp.bfloat16),
            pltpu.VMEM((total, width), jnp.bfloat16),
            pltpu.VMEM((recv_rows, width), jnp.bfloat16),
            pltpu.VMEM(vectors.shape, jnp.float32),
            pltpu.VMEM((vec_slots,) + vectors.shape, jnp.float32),
            pltpu.SemaphoreType.DMA((len(chunks),)),
            pltpu.SemaphoreType.DMA((sems,)),
            pltpu.SemaphoreType.DMA((sems,)),
            pltpu.SemaphoreType.DMA((vec_slots,)),
            pltpu.SemaphoreType.DMA((vec_slots,)),
            pltpu.SemaphoreType.DMA((len(chunks), 2)),
        ],
        compiler_params=pltpu.CompilerParams(
            collective_id=0, has_side_effects=True, vmem_limit_bytes=56 * 2**20
        ),
        name="sum_over_devices",
    )(outer, inner, rest, vectors)


def total_of(outer, inner, rest, vectors):
    seq_count, rows_count = lax.axis_size("seq"), lax.axis_size("rows")
    unit = PACK * seq_count * rows_count
    if rows_count == 2 and seq_count % 4 == 0 and all(
        part.shape[0] % unit == 0 for part in (outer, rest)
    ) and inner.shape[0] % (unit // 2) == 0:
        return sum_over_devices(outer, inner, rest, vectors, seq_count)
    both = ("rows", "seq")
    sums = [
        lax.all_gather(
            lax.psum_scatter(part, both, scatter_dimension=0, tiled=True), both, axis=0, tiled=True
        )
        for part in (outer, inner, rest)
    ]
    return (*sums, lax.psum(vectors, both))


norm_eps = 1e-07
masked_score = -1e30


def shifted(shard, axis, by):
    count = lax.axis_size(axis)
    pairs = [(i, i + by) for i in range(count) if 0 <= i + by < count]
    return lax.ppermute(shard, axis, pairs)


def layer_norm(values, norm_gain, norm_bias):
    centre = values - jnp.mean(values, axis=-1, keepdims=True)
    spread = jnp.mean(centre * centre, axis=-1, keepdims=True)
    return centre * lax.rsqrt(spread + norm_eps) * norm_gain + norm_bias


def f32dot(spec, left, right):
    return jnp.einsum(spec, left, right, preferred_element_type=jnp.float32)


def segment_of(slot_ids, seq_ends):
    return jnp.sum((slot_ids[:, None] >= seq_ends[None, :]).astype(jnp.int32), axis=1)


def mask_bias(seq_lengths, pad_mask, block_len, seq_count):
    ext_len = block_len + 2 * SPAN
    seq_place = lax.axis_index("seq")
    row_len = block_len * seq_count
    seg_ids = jnp.arange(seq_lengths.shape[0], dtype=jnp.int32)
    seq_ends = jnp.sum(
        jnp.where(seg_ids[None, :] <= seg_ids[:, None], seq_lengths[None, :], 0), axis=1
    )
    query_slots = seq_place * block_len + jnp.arange(block_len, dtype=jnp.int32)
    key_slots = seq_place * block_len - SPAN + jnp.arange(ext_len, dtype=jnp.int32)
    seg_query = segment_of(query_slots, seq_ends)
    in_row = (key_slots >= 0) & (key_slots < row_len)
    seg_key = jnp.where(in_row, segment_of(key_slots, seq_ends), -1)
    keep_key = lax.dynamic_slice_in_dim(
        jnp.pad(pad_mask, (SPAN, SPAN)), seq_place * block_len, ext_len, 0
    )
    apart = key_slots[:, None] - query_slots[None, :]
    allowed = (
        (seg_key[:, None] == seg_query[None, :])
        & (jnp.abs(apart) < SPAN)
        & ((keep_key[:, None] == 1) | (apart == 0))
    )
    return jnp.where(allowed, 0.0, masked_score).astype(jnp.float32)


def band_tables(rel_buckets):
    span_ids = jnp.arange(2 * SPAN, dtype=jnp.int32)[None, :]
    back = rel_buckets[::-1]
    to_bucket = jnp.concatenate([back[:1], back[:-1]])
    from_bucket = jnp.concatenate([rel_buckets[1:], rel_buckets[-1:]])
    to_pos = jnp.clip(to_bucket + SPAN, 0, 2 * SPAN - 1)
    from_pos = jnp.clip(SPAN - from_bucket, 0, 2 * SPAN - 1)
    to_hot = (to_pos[:, None] == span_ids).astype(jnp.bfloat16)
    from_hot = (from_pos[:, None] == span_ids).astype(jnp.bfloat16)
    return to_hot, from_hot


def low(values):
    return values.astype(jnp.bfloat16)


def shards(
    tokens, cotangent, w_query, w_key, w_value, w_output, w_inner, w_outer, rel_table,
    mid_gain, mid_bias, end_gain, end_bias, seq_lengths, pad_mask, rel_buckets,
):
    tokens, cotangent = tokens[0], cotangent[0]
    block_len, width = tokens.shape
    seq_count = lax.axis_size("seq")
    prev = shifted(tokens, "seq", 1)
    following = shifted(tokens, "seq", -1)
    bias = mask_bias(seq_lengths[0], pad_mask[0], block_len, seq_count)
    to_hot, from_hot = band_tables(rel_buckets)
    to_table = low(f32dot("mr,re->me", to_hot, rel_table))
    from_table = low(f32dot("mr,re->me", from_hot, rel_table))
    relk = low(f32dot("me,ed->md", to_table, w_key))
    relq = low(f32dot("me,ed->md", from_table, w_query))
    relq = jnp.pad(relq, ((TILE, TILE), (0, 0)))
    query = low(f32dot("te,ed->td", tokens, w_query))
    tokens_ext = jnp.concatenate([prev, tokens, following], axis=0)
    key_ext = low(f32dot("te,ed->td", tokens_ext, w_key))
    value_ext = low(f32dot("te,ed->td", tokens_ext, w_value))
    attn_t, probs = attend(query, key_ext, value_ext.T, relk, relq, bias)

    mixed = f32dot("dt,de->te", attn_t, w_output)
    hidden, mid_back = jax.vjp(layer_norm, tokens.astype(jnp.float32) + mixed, mid_gain, mid_bias)
    hidden_low = low(hidden)
    inner = f32dot("td,df->tf", hidden_low, w_inner)
    active, gelu_back = jax.vjp(functools.partial(jax.nn.gelu, approximate=False), inner)
    active_low = low(active)
    outer = f32dot("tf,fd->td", active_low, w_outer)
    final, end_back = jax.vjp(layer_norm, hidden + outer, end_gain, end_bias)
    layer_out = low(final)
    sum_grad, end_gain_part, end_bias_part = end_back(cotangent.astype(jnp.float32))
    outer_low = low(sum_grad)
    outer_part = low(f32dot("tf,td->fd", active_low, outer_low))
    inner_low = low(gelu_back(f32dot("td,fd->tf", outer_low, w_outer))[0])
    inner_part = low(f32dot("td,tf->df", hidden_low, inner_low))
    hidden_grad = sum_grad + f32dot("tf,df->td", inner_low, w_inner)
    resid_grad, mid_gain_part, mid_bias_part = mid_back(hidden_grad)
    mixed_low = low(resid_grad)
    output_part = low(f32dot("dt,te->de", attn_t, mixed_low))
    attn_grad = low(f32dot("te,de->td", mixed_low, w_output))

    dquery, dkey, dvalue, drelk, drelq = attend_back(
        query, key_ext, value_ext, attn_grad, probs, relk, relq
    )
    pair = jnp.concatenate([dkey, dvalue], axis=1)
    from_next = shifted(low(pair[:SPAN]), "seq", -1).astype(jnp.float32)
    from_prev = shifted(low(pair[SPAN + block_len :]), "seq", 1).astype(jnp.float32)
    pair = low(pair[SPAN : SPAN + block_len] + from_prev + from_next)
    swap = unit(True)
    dkey = low(
        f32dot("ab,nbd->nad", swap, pair[:, :width].reshape(-1, TILE, width))
    ).reshape(block_len, width)
    dvalue = pair[:, width:]
    drelk = low(drelk)
    drelq = low(drelq[:, TILE : TILE + 2 * SPAN])
    query_part = low(f32dot("te,td->ed", tokens, dquery) + f32dot("me,dm->ed", from_table, drelq))
    key_part = low(f32dot("te,td->ed", tokens, dkey) + f32dot("me,dm->ed", to_table, drelk))
    value_part = low(f32dot("te,td->ed", tokens, dvalue))
    table_part = low(
        f32dot("mr,me->re", to_hot, low(f32dot("dm,ed->me", drelk, w_key)))
        + f32dot("mr,me->re", from_hot, low(f32dot("dm,ed->me", drelq, w_query)))
    )
    tokens_grad = low(
        resid_grad
        + f32dot("td,ed->te", dquery, w_query)
        + f32dot("td,ed->te", dkey, w_key)
        + f32dot("td,ed->te", dvalue, w_value)
    )
    vectors = jnp.concatenate(
        [mid_gain_part, mid_bias_part, end_gain_part, end_bias_part, jnp.zeros_like(mid_gain_part)] * 2
    ).reshape(-1, width)[:8]
    rest_part = jnp.concatenate([query_part, key_part, value_part, output_part, table_part], axis=0)
    outer_w, inner_w, rest_w, norm_parts = total_of(outer_part, inner_part, rest_part, vectors)
    query_w, key_w, value_w, output_w = (rest_w[at * width : (at + 1) * width] for at in range(4))
    table_w = rest_w[4 * width :]
    return (
        layer_out[None], tokens_grad[None],
        *(w.astype(jnp.float32) for w in (query_w, key_w, value_w, output_w, inner_w, outer_w, table_w)),
        *(norm_parts[at] for at in range(4)),
    )


def solution(mesh):
    split = P("rows", "seq", None)
    return jax.shard_map(
        shards,
        mesh=mesh,
        in_specs=(split, split) + (P(),) * 11 + (P("rows", None), P("rows", None), P()),
        out_specs=(split, split) + (P(),) * 11,
        check_vma=False,
    )
```

```python
import functools
import math

import jax
import jax.numpy as jnp
from jax import lax
from jax.experimental import pallas as pl
from jax.experimental.pallas import tpu as pltpu
from jax.sharding import PartitionSpec as P

H = 12
DH = 64
SPAN = 256
TILE = 128
REACH = 640
PAIR = 128
score_scale = 1.0 / math.sqrt(3 * DH)


def nt(left, right):
    return lax.dot_general(left, right, (((1,), (1,)), ((), ())), preferred_element_type=jnp.float32)


def nn(left, right):
    return lax.dot_general(left, right, (((1,), (0,)), ((), ())), preferred_element_type=jnp.float32)


def head_lanes(values, head):
    lane = lax.broadcasted_iota(jnp.int32, values.shape, 1)
    mine = (lane < DH) if head == 0 else (lane >= DH)
    return jnp.where(mine, values, jnp.zeros_like(values))


def unit(reverse):
    row = lax.broadcasted_iota(jnp.int32, (TILE, TILE), 0)
    col = lax.broadcasted_iota(jnp.int32, (TILE, TILE), 1)
    hit = (row + col == TILE - 1) if reverse else (row == col)
    return jnp.where(hit, 1.0, 0.0).astype(jnp.bfloat16)


def attend_kernel(q_ref, k_ref, vt_ref, relk_ref, relq_ref, bias_ref, attn_ref, prob_ref, score_ref):
    eye = unit(False)
    log_two = score_scale * math.log2(math.e)
    tiles = q_ref.shape[0] // TILE
    for tile in range(tiles):
        first = tile * TILE
        q_tile = q_ref[pl.ds(first, TILE), :]
        for head in range(2):
            q_head = head_lanes(q_tile, head)
            band = nt(q_head, relk_ref[...])
            band = jnp.concatenate([band, jnp.zeros((TILE, REACH - 2 * SPAN), jnp.float32)], axis=1)
            to_term = pltpu.roll(band, 0, 1, stride=1, stride_axis=0).astype(jnp.bfloat16)
            for part in range(REACH // TILE):
                at = first + part * TILE
                k_part = k_ref[pl.ds(at, TILE), :]
                window = relq_ref[pl.ds((REACH // TILE - 1 - part) * TILE, 2 * TILE), :]
                from_band = nt(head_lanes(k_part, head), window)
                from_term = pltpu.roll(from_band, TILE + 1, 1, stride=1, stride_axis=0)[:, :TILE]
                left = jnp.concatenate([k_part, eye], axis=1)
                right = jnp.concatenate(
                    [q_head, to_term[:, part * TILE : (part + 1) * TILE]], axis=1
                )
                score_ref[pl.ds(part * TILE, TILE), :] = (
                    nt(left, right) + from_term + bias_ref[pl.ds(at, TILE), pl.ds(first, TILE)]
                )
            scores = score_ref[...]
            top = jnp.max(scores, axis=0, keepdims=True)
            weights = jnp.exp2((scores - top) * log_two)
            total = jnp.sum(weights, axis=0, keepdims=True)
            probs = (weights * (1.0 / total)).astype(jnp.bfloat16)
            prob_ref[head, tile] = probs
            out = nn(vt_ref[pl.ds(head * DH, DH), pl.ds(first, REACH)], probs)
            attn_ref[pl.ds(head * DH, DH), pl.ds(first, TILE)] = out.astype(attn_ref.dtype)


def attend(query, key_ext, value_ext_t, relk, relq, bias):
    block_len, width = query.shape
    ext_len = key_ext.shape[0]
    tiles = block_len // TILE
    pairs = width // PAIR
    return pl.pallas_call(
        attend_kernel,
        grid=(pairs,),
        in_specs=[
            pl.BlockSpec((block_len, PAIR), lambda p: (0, p)),
            pl.BlockSpec((ext_len, PAIR), lambda p: (0, p)),
            pl.BlockSpec((PAIR, ext_len), lambda p: (p, 0)),
            pl.BlockSpec((2 * SPAN, PAIR), lambda p: (0, p)),
            pl.BlockSpec((2 * SPAN + 2 * TILE, PAIR), lambda p: (0, p)),
            pl.BlockSpec((ext_len, block_len), lambda p: (0, 0)),
        ],
        out_specs=[
            pl.BlockSpec((PAIR, block_len), lambda p: (p, 0)),
            pl.BlockSpec((2, tiles, REACH, TILE), lambda p: (p, 0, 0, 0)),
        ],
        out_shape=[
            jax.ShapeDtypeStruct((width, block_len), jnp.bfloat16),
            jax.ShapeDtypeStruct((2 * pairs, tiles, REACH, TILE), jnp.bfloat16),
        ],
        scratch_shapes=[pltpu.VMEM((REACH, TILE), jnp.float32)],
        compiler_params=pltpu.CompilerParams(vmem_limit_bytes=48 * 2**20),
        name="attend",
    )(query, key_ext, value_ext_t, relk, relq, bias)


def attend_back_kernel(
    q_ref, k_ref, v_ref, grad_ref, prob_ref, relk_ref, relq_ref,
    dq_ref, dk_ref, dv_ref, drelk_ref, drelq_ref, qt_ref, kt_ref,
):
    swap = unit(True)
    for source, result in ((q_ref, qt_ref), (k_ref, kt_ref)):
        for at in range(0, source.shape[0], TILE):
            flipped = nn(swap, source[pl.ds(at, TILE), :])
            result[:, pl.ds(at, TILE)] = flipped.T.astype(jnp.bfloat16)
    row = lax.broadcasted_iota(jnp.int32, (TILE, TILE), 0)
    col = lax.broadcasted_iota(jnp.int32, (TILE, TILE), 1)
    parts = REACH // TILE
    tiles = q_ref.shape[0] // TILE
    dk_ref[...] = jnp.zeros_like(dk_ref)
    dv_ref[...] = jnp.zeros_like(dv_ref)
    drelk_ref[...] = jnp.zeros_like(drelk_ref)
    drelq_ref[...] = jnp.zeros_like(drelq_ref)
    for tile in range(tiles):
        first = tile * TILE
        q_tile = q_ref[pl.ds(first, TILE), :]
        grad_tile = grad_ref[pl.ds(first, TILE), :]
        v_tile = v_ref[pl.ds(first, REACH), :]
        q_heads = [head_lanes(q_tile, head) for head in range(2)]
        grad_heads = [head_lanes(grad_tile, head) for head in range(2)]
        dq_heads = []
        lefts = [[] for _ in range(parts)]
        for head in range(2):
            lanes = pl.ds(head * DH, DH)
            probs = prob_ref[head, tile].astype(jnp.float32)
            weighted = probs * nt(v_tile, grad_heads[head])
            delta = jnp.sum(weighted, axis=0, keepdims=True)
            dscore = ((weighted - probs * delta) * score_scale).astype(jnp.bfloat16)
            turned = nt(swap, dscore)
            dband = pltpu.roll(turned, REACH - TILE + 1, 1, stride=1, stride_axis=0)
            dband = dband[:, : 2 * SPAN].astype(jnp.bfloat16)
            dq_heads.append(
                nn(turned.astype(jnp.bfloat16), k_ref[pl.ds(first, REACH), :])
                + nn(dband, relk_ref[...])
            )
            drelk_ref[lanes, :] += nn(qt_ref[lanes, pl.ds(first, TILE)], dband)
            for part in range(parts):
                flipped = nn(swap, dscore[part * TILE : (part + 1) * TILE, :])
                spun = pltpu.roll(flipped, 0, 1, stride=1, stride_axis=0)
                low = jnp.where(col >= row, spun, 0.0)
                dfrom = jnp.concatenate([low, spun - low], axis=1).astype(jnp.bfloat16)
                window = pl.ds((parts - 1 - part) * TILE, 2 * TILE)
                drelq_ref[lanes, window] += nn(kt_ref[lanes, pl.ds(first + part * TILE, TILE)], dfrom)
                lefts[part] += [flipped.astype(jnp.bfloat16), dfrom]
        dq_turned = jnp.where(col < DH, dq_heads[0], dq_heads[1]).astype(jnp.bfloat16)
        dq_ref[pl.ds(first, TILE), :] = nn(swap, dq_turned).astype(dq_ref.dtype)
        dv_ref[pl.ds(first, REACH), :] += nn(
            jnp.concatenate([prob_ref[0, tile], prob_ref[1, tile]], axis=1),
            jnp.concatenate(grad_heads, axis=0),
        )
        for part in range(parts):
            window = relq_ref[pl.ds((parts - 1 - part) * TILE, 2 * TILE), :]
            right = jnp.concatenate(
                [q_heads[0], head_lanes(window, 0), q_heads[1], head_lanes(window, 1)], axis=0
            )
            dk_ref[pl.ds(first + part * TILE, TILE), :] += nn(
                jnp.concatenate(lefts[part], axis=1), right
            )


def attend_back(query, key_ext, value_ext, grad, probs, relk, relq):
    block_len, width = query.shape
    ext_len = key_ext.shape[0]
    tiles = block_len // TILE
    pairs = width // PAIR
    table = 2 * SPAN
    cols = lambda n: pl.BlockSpec((n, PAIR), lambda p: (0, p))
    rows = lambda n: pl.BlockSpec((PAIR, n), lambda p: (p, 0))
    f32 = lambda *s: jax.ShapeDtypeStruct(s, jnp.float32)
    return pl.pallas_call(
        attend_back_kernel,
        grid=(pairs,),
        in_specs=[
            cols(block_len), cols(ext_len), cols(ext_len), cols(block_len),
            pl.BlockSpec((2, tiles, REACH, TILE), lambda p: (p, 0, 0, 0)),
            cols(table), cols(table + 2 * TILE),
        ],
        out_specs=[cols(block_len), cols(ext_len), cols(ext_len), rows(table), rows(table + 2 * TILE)],
        out_shape=[
            jax.ShapeDtypeStruct((block_len, width), jnp.bfloat16),
            f32(ext_len, width), f32(ext_len, width), f32(width, table), f32(width, table + 2 * TILE),
        ],
        scratch_shapes=[
            pltpu.VMEM((PAIR, block_len), jnp.bfloat16), pltpu.VMEM((PAIR, ext_len), jnp.bfloat16),
        ],
        compiler_params=pltpu.CompilerParams(vmem_limit_bytes=48 * 2**20),
        name="attend_back",
    )(query, key_ext, value_ext, grad, probs, relk, relq)


MESH = pl.DeviceIdType.MESH
PACK = 16


def axes_of(seq_count):
    row, place = lax.axis_index("rows"), lax.axis_index("seq")
    first, second, third = place % 2, (place // 2) % 2, place // 4
    near = (first + row * (second - first), 1 + row, 2)
    cross = (second + row * (first - second), 2 - row, 2)
    far = (third, 4, seq_count // 4)
    return row, place, near, cross, far


class Line:
    def __init__(self, at, step, count):
        self.at, self.step, self.count = at, step, count

    def peers(self, row, place):
        for ahead in range(1, self.count):
            there = lax.rem(self.at + ahead, self.count)
            yield ahead - 1, there, {"rows": row, "seq": place + (there - self.at) * self.step}


class CoreLine(Line):
    def peers(self, row, place):
        yield 0, 1 - row, {"rows": 1 - row, "seq": place}


def add_rows(target, at, sources, rows, out, out_at):
    step = next(s for s in (48, 32, PACK) if rows % s == 0)

    def body(i, carry):
        here = pl.multiple_of(i * step, PACK)
        total = target[pl.ds(pl.multiple_of(at + here, PACK), step), :].astype(jnp.float32)
        for source in sources:
            total = total + source[pl.ds(here, step), :].astype(jnp.float32)
        out[pl.ds(pl.multiple_of(out_at + here, PACK), step), :] = total.astype(out.dtype)
        return carry

    lax.fori_loop(0, rows // step, body, 0)


class Chunk:
    def __init__(self, index, which, start, half, base, width):
        self.index, self.which, self.start, self.half, self.base, self.width = (
            index, which, start, half, base, width,
        )

    def part(self, refs, side):
        if self.which == "inner":
            block, low_row = (self.start // 2) // self.width, (self.start // 2) % self.width
            col = (2 * block + side) * self.width
            return refs["inner"].at[pl.ds(low_row, self.half), pl.ds(pl.multiple_of(col, PAIR), self.width)]
        first = pl.multiple_of(self.start + side * self.half, PACK)
        return refs[self.which].at[pl.ds(first, self.half)]


def chunks_of(spec, unit, width):
    chunks, starts, base = [], {}, 0
    for which, units in spec:
        half = units * unit // 2
        start = starts.get(which, 0)
        chunks.append(Chunk(len(chunks), which, start, half, base, width))
        starts[which] = start + 2 * half
        base += half
    return chunks, base


def phases_of(chunk, seq_count):
    rows, phases = 2 * chunk.half, []
    for count in (2, 2, 2, seq_count // 4):
        rows //= count
        phases.append((count, rows))
    return phases


class Sum:
    last = 8

    def __init__(self, chunks, seq_count, ins, outs, acc, gat, recv, own_sem, send_sem, recv_sem):
        self.chunks, self.ins, self.outs = chunks, ins, outs
        self.acc, self.gat, self.recv = acc, gat, recv
        self.own_sem, self.send_sem, self.recv_sem = own_sem, send_sem, recv_sem
        self.row, self.place, near, cross, far = axes_of(seq_count)
        self.lines = (CoreLine(self.row, 0, 2), Line(*near), Line(*cross), Line(*far))
        self.phases = [phases_of(chunk, seq_count) for chunk in chunks]
        self.recv_at, self.sem_at = [], []
        recv_rows = sems = 0
        for phases in self.phases:
            self.recv_at.append([])
            self.sem_at.append([])
            for count, rows in phases:
                self.recv_at[-1].append(recv_rows)
                recv_rows += (count - 1) * rows
                self.sem_at[-1].append((sems, sems + count - 1))
                sems += 2 * (count - 1)

    def greet(self, more):
        barrier = pltpu.get_barrier_semaphore()
        devices = [d for line in self.lines for _, _, d in line.peers(self.row, self.place)] + more
        for device in devices:
            pl.semaphore_signal(barrier, inc=1, device_id=device, device_id_type=MESH)
        pl.semaphore_wait(barrier, len(devices))

    def remote(self, source, target, sem, device):
        return pltpu.make_async_remote_copy(
            src_ref=source, dst_ref=target, send_sem=self.send_sem.at[sem], recv_sem=self.recv_sem.at[sem],
            device_id=device, device_id_type=MESH,
        )

    def offset(self, c, phase):
        at = 0
        for line, (count, rows) in list(zip(self.lines, self.phases[c]))[1 : phase + 1]:
            at = at + line.at * rows
        return at

    def received(self, c, phase):
        count, rows = self.phases[c][phase]
        return [
            self.recv.at[pl.ds(self.recv_at[c][phase] + slot * rows, rows)] for slot in range(count - 1)
        ]

    def reduce_copies(self, chunk, phase):
        c = chunk.index
        count, rows = self.phases[c][phase]
        copies = []
        for slot, there, device in self.lines[phase].peers(self.row, self.place):
            if phase == 0:
                source = chunk.part(self.ins, there)
            else:
                at = chunk.base + self.offset(c, phase - 1) + there * rows
                source = self.acc.at[pl.ds(pl.multiple_of(at, PACK), rows)]
            copies.append(
                self.remote(source, self.received(c, phase)[slot], self.sem_at[c][phase][0] + slot, device)
            )
        if phase == 0:
            copies.append(
                pltpu.make_async_copy(
                    chunk.part(self.ins, self.row), self.acc.at[pl.ds(chunk.base, rows)], self.own_sem.at[c]
                )
            )
        return copies

    def gather_copies(self, chunk, phase):
        c = chunk.index
        home = pl.multiple_of(chunk.base + self.offset(c, phase), PACK)
        mine = self.gat.at[pl.ds(home, self.phases[c][phase][1])]
        copies = []
        for slot, there, device in self.lines[phase].peers(self.row, self.place):
            target = chunk.part(self.outs, self.row) if phase == 0 else mine
            copies.append(self.remote(mine, target, self.sem_at[c][phase][1] + slot, device))
        if phase == 0:
            copies.append(
                pltpu.make_async_copy(mine, chunk.part(self.outs, self.row), self.own_sem.at[c])
            )
        return copies

    def copies(self, chunk, stage):
        return self.reduce_copies(chunk, stage) if stage < 4 else self.gather_copies(chunk, 7 - stage)

    def step(self, c, stage):
        chunk = self.chunks[c]
        if stage > 0:
            for copy in self.copies(chunk, stage - 1):
                copy.wait()
        if 0 < stage <= 4:
            at = chunk.base + self.offset(c, stage - 1)
            add_rows(
                self.acc, at, self.received(c, stage - 1), self.phases[c][stage - 1][1],
                self.gat if stage == 4 else self.acc, at,
            )
        if stage < self.last:
            for copy in self.copies(chunk, stage):
                copy.start()


class VectorSum:
    def __init__(self, total, acc, recv, send_sem, recv_sem):
        self.total, self.acc, self.recv, self.send_sem, self.recv_sem = total, acc, recv, send_sem, recv_sem

    def copies(self, phase):
        first = sum(line.count - 1 for line in self.total.lines[:phase])
        for slot, _, device in self.total.lines[phase].peers(self.total.row, self.total.place):
            yield first + slot, pltpu.make_async_remote_copy(
                src_ref=self.acc.at[phase], dst_ref=self.recv.at[first + slot],
                send_sem=self.send_sem.at[first + slot], recv_sem=self.recv_sem.at[first + slot],
                device_id=device, device_id_type=MESH,
            )

    def start(self, phase):
        for _, copy in self.copies(phase):
            copy.start()

    def end(self, phase):
        whole = self.acc[phase]
        for slot, copy in self.copies(phase):
            copy.wait()
            whole = whole + self.recv[slot]
        self.acc[phase + 1] = whole


def back_of_pair(pair, buf, r):
    swap = unit(True)
    lanes_at = pl.multiple_of(pair * PAIR, PAIR)
    lanes_here = pl.ds(lanes_at, PAIR)
    row = lax.broadcasted_iota(jnp.int32, (TILE, TILE), 0)
    col = lax.broadcasted_iota(jnp.int32, (TILE, TILE), 1)
    parts = REACH // TILE
    block_len, ext_len = r["q"].shape[0], r["k"].shape[0]
    tiles = block_len // TILE
    qt_ref, kt_ref, dk_ref, dv_ref, drelk_ref, drelq_ref = (
        r[name] for name in ("qt", "kt", "dk_pair", "dv_pair", "drelk_t", "drelq_t")
    )
    for source, result in ((r["q"], qt_ref), (r["k"], kt_ref)):
        for at in range(0, source.shape[0], TILE):
            flipped = nn(swap, source[pl.ds(at, TILE), lanes_here])
            result[:, pl.ds(at, TILE)] = flipped.T.astype(jnp.bfloat16)
    dk_ref[...] = jnp.zeros_like(dk_ref)
    dv_ref[...] = jnp.zeros_like(dv_ref)
    drelk_ref[...] = jnp.zeros_like(drelk_ref)
    drelq_ref[...] = jnp.zeros_like(drelq_ref)
    for tile in range(tiles):
        first = tile * TILE
        q_tile = r["q"][pl.ds(first, TILE), lanes_here]
        grad_tile = r["grad"][pl.ds(first, TILE), lanes_here]
        v_tile = r["v"][pl.ds(first, REACH), lanes_here]
        q_heads = [head_lanes(q_tile, head) for head in range(2)]
        grad_heads = [head_lanes(grad_tile, head) for head in range(2)]
        dq_heads = []
        lefts = [[] for _ in range(parts)]
        for head in range(2):
            lanes = pl.ds(head * DH, DH)
            probs = r["probs"][buf, head, tile].astype(jnp.float32)
            weighted = probs * nt(v_tile, grad_heads[head])
            delta = jnp.sum(weighted, axis=0, keepdims=True)
            dscore = ((weighted - probs * delta) * score_scale).astype(jnp.bfloat16)
            turned = nt(swap, dscore)
            dband = pltpu.roll(turned, REACH - TILE + 1, 1, stride=1, stride_axis=0)
            dband = dband[:, : 2 * SPAN].astype(jnp.bfloat16)
            dq_heads.append(
                nn(turned.astype(jnp.bfloat16), r["k"][pl.ds(first, REACH), lanes_here])
                + nn(dband, r["relk"][:, lanes_here])
            )
            drelk_ref[lanes, :] += nn(qt_ref[lanes, pl.ds(first, TILE)], dband)
            for part in range(parts):
                flipped = nn(swap, dscore[part * TILE : (part + 1) * TILE, :])
                spun = pltpu.roll(flipped, 0, 1, stride=1, stride_axis=0)
                near = jnp.where(col >= row, spun, 0.0)
                dfrom = jnp.concatenate([near, spun - near], axis=1).astype(jnp.bfloat16)
                window = pl.ds((parts - 1 - part) * TILE, 2 * TILE)
                drelq_ref[lanes, window] += nn(kt_ref[lanes, pl.ds(first + part * TILE, TILE)], dfrom)
                lefts[part] += [flipped.astype(jnp.bfloat16), dfrom]
        dq_turned = jnp.where(col < DH, dq_heads[0], dq_heads[1]).astype(jnp.bfloat16)
        r["dq"][pl.ds(first, TILE), lanes_here] = nn(swap, dq_turned).astype(jnp.bfloat16)
        dv_ref[pl.ds(first, REACH), :] += nn(
            jnp.concatenate([r["probs"][buf, 0, tile], r["probs"][buf, 1, tile]], axis=1),
            jnp.concatenate(grad_heads, axis=0),
        )
        for part in range(parts):
            window = r["relq"][pl.ds((parts - 1 - part) * TILE, 2 * TILE), lanes_here]
            right = jnp.concatenate(
                [q_heads[0], head_lanes(window, 0), q_heads[1], head_lanes(window, 1)], axis=0
            )
            dk_ref[pl.ds(first + part * TILE, TILE), :] += nn(
                jnp.concatenate(lefts[part], axis=1), right
            )
    r["dv"][:, lanes_here] = dv_ref[...].astype(jnp.bfloat16)
    for at in range(0, ext_len, TILE):
        r["dk"][pl.ds(at, TILE), lanes_here] = nn(
            swap, dk_ref[pl.ds(at, TILE), :].astype(jnp.bfloat16)
        ).astype(jnp.bfloat16)
    r["dk"][pl.ds(ext_len, 2 * SPAN), lanes_here] = drelk_ref[...].T.astype(jnp.bfloat16)
    r["dq"][pl.ds(block_len, 2 * SPAN), lanes_here] = (
        drelq_ref[:, pl.ds(TILE, 2 * SPAN)].T.astype(jnp.bfloat16)
    )


def by_rows(rows, step, body):
    def one(i, carry):
        body(pl.ds(pl.multiple_of(i * step, step), step))
        return carry

    lax.fori_loop(0, rows // step, one, 0)


FINISH_IN = (
    "q", "k", "v", "grad", "relk", "relq", "xt_key", "xt_query", "w_query", "w_key", "w_value",
    "hot", "resid", "vectors", "outer", "inner", "output", "probs_in",
)
FINISH_OUT = ("outer", "inner", "rest", "vectors", "tokens_grad")
FINISH_SCRATCH = (
    "probs", "qt", "kt", "dk_pair", "dv_pair", "drelk_t", "drelq_t", "dq", "dk", "dv", "rest", "table",
    "halo", "halo_got", "acc", "gat", "recv", "vec_acc", "vec_recv", "own_sem", "send_sem", "recv_sem",
    "vec_send", "vec_got", "probs_sem", "halo_send", "halo_recv",
)


def finish_kernel(chunks, seq_count, *refs):
    r = dict(zip(FINISH_IN, refs))
    outs = dict(zip(FINISH_OUT, refs[len(FINISH_IN) :]))
    r.update(zip(FINISH_SCRATCH, refs[len(FINISH_IN) + len(FINISH_OUT) :]))
    block_len, width = r["q"].shape
    ext_len = r["k"].shape[0]
    pairs = width // PAIR
    total = Sum(
        chunks, seq_count, r, outs, r["acc"], r["gat"], r["recv"], r["own_sem"], r["send_sem"], r["recv_sem"]
    )
    row, place = total.row, total.place
    before = {"rows": row, "seq": lax.rem(place + seq_count - 1, seq_count)}
    after = {"rows": row, "seq": lax.rem(place + 1, seq_count)}
    total.greet([before, after])
    vec = VectorSum(total, r["vec_acc"], r["vec_recv"], r["vec_send"], r["vec_got"])
    vec.acc[0] = r["vectors"][...]

    early = [c for c, chunk in enumerate(chunks) if chunk.which != "rest"]
    late = [c for c, chunk in enumerate(chunks) if chunk.which == "rest"]
    for c in early:
        total.step(c, 0)

    def probs_copy(pair, buf):
        return pltpu.make_async_copy(
            r["probs_in"].at[pl.ds(2 * pair, 2)], r["probs"].at[buf], r["probs_sem"].at[buf]
        )

    probs_copy(0, 0).start()
    done = {c: 0 for c in early}

    def move(*steps):
        for c, stage in steps:
            total.step(c, stage)
            done[c] = stage

    def between(pair):
        if pair == 0:
            move((0, 1), (1, 1))
            vec.start(0)
        elif pair == 1:
            move((2, 1), (3, 1))
            vec.end(0)
            vec.start(1)
        elif pair == 2:
            move((0, 2))
            vec.end(1)
            vec.start(2)
        elif pair == 3:
            move((1, 2), (0, 3))
            vec.end(2)
            vec.start(3)
        elif pair == 4:
            move((1, 3), (0, 4))
            vec.end(3)
        else:
            move((2, 2), (1, 4), (0, 5))

    def one_pair(pair, carry):
        buf = lax.rem(pair, 2)

        @pl.when(pair + 1 < pairs)
        def _():
            probs_copy(pair + 1, 1 - buf).start()

        probs_copy(pair, buf).wait()
        back_of_pair(pair, buf, r)
        for at in range(pairs):
            pl.when(pair == at)(functools.partial(between, at))
        return carry

    lax.fori_loop(0, pairs, one_pair, 0)

    def query_rows(rows):
        r["rest"][rows, :] = nn(r["xt_query"][rows, :], r["dq"][...]).astype(jnp.bfloat16)

    def key_rows(rows):
        at = pl.ds(pl.multiple_of(width + rows.start, PACK), rows.size)
        r["rest"][at, :] = nn(r["xt_key"][rows, :], r["dk"][...]).astype(jnp.bfloat16)

    def value_rows(rows):
        at = pl.ds(pl.multiple_of(2 * width + rows.start, PACK), rows.size)
        r["rest"][at, :] = nn(r["xt_key"][rows, pl.ds(0, ext_len)], r["dv"][...]).astype(jnp.bfloat16)

    def table_rows(rows):
        key_at = pl.ds(pl.multiple_of(ext_len + rows.start, PACK), rows.size)
        query_at = pl.ds(pl.multiple_of(block_len + rows.start, PACK), rows.size)
        other = pl.ds(pl.multiple_of(2 * SPAN + rows.start, PACK), rows.size)
        r["table"][rows, :] = nt(r["dk"][key_at, :], r["w_key"][...]).astype(jnp.bfloat16)
        r["table"][other, :] = nt(r["dq"][query_at, :], r["w_query"][...]).astype(jnp.bfloat16)

    def bucket_rows(rows):
        at = pl.ds(pl.multiple_of(4 * width + rows.start, PACK), rows.size)
        r["rest"][at, :] = nn(r["hot"][rows, :], r["table"][...]).astype(jnp.bfloat16)

    def token_rows(rows):
        grad = nt(r["dk"][rows, :], r["w_key"][...]) + nt(r["dv"][rows, :], r["w_value"][...])
        r["halo"][rows, :] = grad.astype(jnp.bfloat16)

    output_copy = pltpu.make_async_copy(
        r["output"], r["rest"].at[pl.ds(3 * width, width)], r["own_sem"].at[len(chunks)]
    )
    output_copy.start()
    by_rows(width, 128, query_rows)
    move((3, 2))
    by_rows(width, 128, key_rows)
    move((late[0], 0), (2, 3), (0, 6))
    by_rows(width, 128, value_rows)
    output_copy.wait()
    move((late[1], 0), (late[0], 1), (3, 3), (2, 4), (1, 5))
    by_rows(2 * SPAN, 128, table_rows)
    by_rows(2 * SPAN, 128, bucket_rows)
    move((late[2], 0), (late[1], 1), (late[0], 2), (3, 4), (2, 5), (1, 6), (0, 7))
    by_rows(ext_len, 128, token_rows)
    halos = []
    for number, (at, device) in enumerate(((0, before), (ext_len - SPAN, after))):
        copy = pltpu.make_async_remote_copy(
            src_ref=r["halo"].at[pl.ds(at, SPAN)], dst_ref=r["halo_got"].at[number],
            send_sem=r["halo_send"].at[number], recv_sem=r["halo_recv"].at[number],
            device_id=device, device_id_type=MESH,
        )
        copy.start()
        halos.append(copy)

    def finish_tokens():
        for copy in halos:
            copy.wait()

        def own_rows(rows):
            mid = pl.ds(pl.multiple_of(SPAN + rows.start, PACK), rows.size)
            grad = r["resid"][rows, :] + nt(r["dq"][rows, :], r["w_query"][...])
            grad = grad + nt(r["dk"][mid, :], r["w_key"][...]) + nt(r["dv"][mid, :], r["w_value"][...])
            for number in range(2):
                grad = grad + r["halo_got"][number, rows, :].astype(jnp.float32)
            outs["tokens_grad"][rows, :] = grad.astype(jnp.bfloat16)

        by_rows(block_len, 128, own_rows)

    left = [c for c in done if done[c] < total.last]
    order = sorted(
        (stage - done[c], stage, c) for c in left for stage in range(done[c] + 1, total.last + 1)
    )
    last_slot = 0
    tokens_done = False
    for slot, stage, c in order:
        if slot == 3 and not tokens_done:
            finish_tokens()
            tokens_done = True
        total.step(c, stage)
    outs["vectors"][...] = vec.acc[len(total.lines)]


def finish(inputs, seq_count):
    unit_rows = PACK * 2 * seq_count
    width = inputs["q"].shape[1]
    block_len, ext_len = inputs["q"].shape[0], inputs["k"].shape[0]
    spec = (("outer", 3), ("outer", 3), ("inner", 3), ("inner", 3), ("rest", 3), ("rest", 2), ("rest", 2))
    chunks, rows = chunks_of(spec, unit_rows, width)
    phases = [phases_of(chunk, seq_count) for chunk in chunks]
    recv_rows = sum((count - 1) * high for chunk in phases for count, high in chunk)
    sems = sum(2 * (count - 1) for chunk in phases for count, _ in chunk)
    vec_slots = sum(count - 1 for count, _ in phases[0])
    rest_rows = 4 * width + 2 * SPAN
    bf = lambda *shape: pltpu.VMEM(shape, jnp.bfloat16)
    f32 = lambda *shape: pltpu.VMEM(shape, jnp.float32)
    dma = pltpu.SemaphoreType.DMA
    vec_shape = inputs["vectors"].shape
    in_hbm = ("outer", "inner", "output", "probs_in")
    any_spec = pl.BlockSpec(memory_space=pl.ANY)
    vmem = pl.BlockSpec(memory_space=pltpu.VMEM)
    tiles = block_len // TILE
    return pl.pallas_call(
        functools.partial(finish_kernel, chunks, seq_count),
        in_specs=[any_spec if name in in_hbm else vmem for name in FINISH_IN],
        out_specs=[any_spec] * 3 + [vmem] * 2,
        out_shape=[
            jax.ShapeDtypeStruct(inputs["outer"].shape, jnp.bfloat16),
            jax.ShapeDtypeStruct(inputs["inner"].shape, jnp.bfloat16),
            jax.ShapeDtypeStruct((rest_rows, width), jnp.bfloat16),
            jax.ShapeDtypeStruct(vec_shape, jnp.float32),
            jax.ShapeDtypeStruct((block_len, width), jnp.bfloat16),
        ],
        scratch_shapes=[
            bf(2, 2, tiles, REACH, TILE), bf(PAIR, block_len), bf(PAIR, ext_len),
            f32(ext_len, PAIR), f32(ext_len, PAIR), f32(PAIR, 2 * SPAN), f32(PAIR, 2 * SPAN + 2 * TILE),
            bf(block_len + 2 * SPAN, width), bf(ext_len + 2 * SPAN, width), bf(ext_len, width),
            bf(rest_rows, width), bf(4 * SPAN, width), bf(ext_len, width), bf(2, SPAN, width),
            bf(rows, width), bf(rows, width), bf(recv_rows, width),
            f32(5, *vec_shape), f32(vec_slots, *vec_shape),
            dma((len(chunks) + 1,)), dma((sems,)), dma((sems,)), dma((vec_slots,)), dma((vec_slots,)),
            dma((2,)), dma((2,)), dma((2,)),
        ],
        compiler_params=pltpu.CompilerParams(
            collective_id=0, has_side_effects=True, vmem_limit_bytes=60 * 2**20
        ),
        name="finish",
    )(*(inputs[name] for name in FINISH_IN))

norm_eps = 1e-07
masked_score = -1e30


def shifted(shard, axis, by):
    count = lax.axis_size(axis)
    pairs = [(i, i + by) for i in range(count) if 0 <= i + by < count]
    return lax.ppermute(shard, axis, pairs)


def layer_norm(values, norm_gain, norm_bias):
    centre = values - jnp.mean(values, axis=-1, keepdims=True)
    spread = jnp.mean(centre * centre, axis=-1, keepdims=True)
    return centre * lax.rsqrt(spread + norm_eps) * norm_gain + norm_bias


def f32dot(spec, left, right):
    return jnp.einsum(spec, left, right, preferred_element_type=jnp.float32)


def segment_of(slot_ids, seq_ends):
    return jnp.sum((slot_ids[:, None] >= seq_ends[None, :]).astype(jnp.int32), axis=1)


def mask_bias(seq_lengths, pad_mask, block_len, seq_count):
    ext_len = block_len + 2 * SPAN
    seq_place = lax.axis_index("seq")
    row_len = block_len * seq_count
    seg_ids = jnp.arange(seq_lengths.shape[0], dtype=jnp.int32)
    seq_ends = jnp.sum(
        jnp.where(seg_ids[None, :] <= seg_ids[:, None], seq_lengths[None, :], 0), axis=1
    )
    query_slots = seq_place * block_len + jnp.arange(block_len, dtype=jnp.int32)
    key_slots = seq_place * block_len - SPAN + jnp.arange(ext_len, dtype=jnp.int32)
    seg_query = segment_of(query_slots, seq_ends)
    in_row = (key_slots >= 0) & (key_slots < row_len)
    seg_key = jnp.where(in_row, segment_of(key_slots, seq_ends), -1)
    keep_key = lax.dynamic_slice_in_dim(
        jnp.pad(pad_mask, (SPAN, SPAN)), seq_place * block_len, ext_len, 0
    )
    apart = key_slots[:, None] - query_slots[None, :]
    allowed = (
        (seg_key[:, None] == seg_query[None, :])
        & (jnp.abs(apart) < SPAN)
        & ((keep_key[:, None] == 1) | (apart == 0))
    )
    return jnp.where(allowed, 0.0, masked_score).astype(jnp.float32)


def band_tables(rel_buckets):
    span_ids = jnp.arange(2 * SPAN, dtype=jnp.int32)[None, :]
    back = rel_buckets[::-1]
    to_bucket = jnp.concatenate([back[:1], back[:-1]])
    from_bucket = jnp.concatenate([rel_buckets[1:], rel_buckets[-1:]])
    to_pos = jnp.clip(to_bucket + SPAN, 0, 2 * SPAN - 1)
    from_pos = jnp.clip(SPAN - from_bucket, 0, 2 * SPAN - 1)
    to_hot = (to_pos[:, None] == span_ids).astype(jnp.bfloat16)
    from_hot = (from_pos[:, None] == span_ids).astype(jnp.bfloat16)
    return to_hot, from_hot


def low(values):
    return values.astype(jnp.bfloat16)

def finish_plain(inputs):
    query, key_ext, value_ext = inputs["q"], inputs["k"], inputs["v"]
    block_len, width = query.shape
    w_query, w_key, w_value, hot = (inputs[name] for name in ("w_query", "w_key", "w_value", "hot"))
    dquery, dkey, dvalue, drelk, drelq = attend_back(
        query, key_ext, value_ext, inputs["grad"], inputs["probs_in"], inputs["relk"], inputs["relq"]
    )
    dkey = low(f32dot("ab,nbd->nad", unit(True), low(dkey).reshape(-1, TILE, width))).reshape(-1, width)
    dvalue = low(dvalue)
    drelk = low(drelk).T
    drelq = low(drelq[:, TILE : TILE + 2 * SPAN]).T
    query_part = f32dot("em,md->ed", inputs["xt_query"], jnp.concatenate([dquery, drelq]))
    key_part = f32dot("em,md->ed", inputs["xt_key"], jnp.concatenate([dkey, drelk]))
    value_part = f32dot("em,md->ed", inputs["xt_key"][:, : key_ext.shape[0]], dvalue)
    table = jnp.concatenate(
        [low(f32dot("md,ed->me", drelk, w_key)), low(f32dot("md,ed->me", drelq, w_query))]
    )
    table_part = f32dot("rm,me->re", hot, table)
    rest = jnp.concatenate(
        [low(query_part), low(key_part), low(value_part), inputs["output"], low(table_part)]
    )
    ext_grad = f32dot("td,ed->te", dkey, w_key) + f32dot("td,ed->te", dvalue, w_value)
    tokens_grad = (
        inputs["resid"]
        + f32dot("td,ed->te", dquery, w_query)
        + ext_grad[SPAN : SPAN + block_len]
        + shifted(low(ext_grad[:SPAN]), "seq", -1).astype(jnp.float32)
        + shifted(low(ext_grad[SPAN + block_len :]), "seq", 1).astype(jnp.float32)
    )
    both = ("rows", "seq")
    sums = [
        lax.all_gather(
            lax.psum_scatter(part, both, scatter_dimension=0, tiled=True), both, axis=0, tiled=True
        )
        for part in (inputs["outer"], inputs["inner"], rest)
    ]
    return (*sums, lax.psum(inputs["vectors"], both), low(tokens_grad))


def finish_of(inputs):
    seq_count, rows_count = lax.axis_size("seq"), lax.axis_size("rows")
    if rows_count == 2 and seq_count == 16:
        return finish(inputs, seq_count)
    return finish_plain(inputs)


def shards(
    tokens, cotangent, w_query, w_key, w_value, w_output, w_inner, w_outer, rel_table,
    mid_gain, mid_bias, end_gain, end_bias, seq_lengths, pad_mask, rel_buckets,
):
    tokens, cotangent = tokens[0], cotangent[0]
    block_len, width = tokens.shape
    seq_count = lax.axis_size("seq")
    prev = shifted(tokens, "seq", 1)
    following = shifted(tokens, "seq", -1)
    bias = mask_bias(seq_lengths[0], pad_mask[0], block_len, seq_count)
    to_hot, from_hot = band_tables(rel_buckets)
    to_table = low(f32dot("mr,re->me", to_hot, rel_table))
    from_table = low(f32dot("mr,re->me", from_hot, rel_table))
    to_table_t = low(f32dot("mr,re->em", to_hot, rel_table))
    from_table_t = low(f32dot("mr,re->em", from_hot, rel_table))
    relk = low(f32dot("me,ed->md", to_table, w_key))
    relq = low(f32dot("me,ed->md", from_table, w_query))
    relq = jnp.pad(relq, ((TILE, TILE), (0, 0)))
    query = low(f32dot("te,ed->td", tokens, w_query))
    tokens_ext = jnp.concatenate([prev, tokens, following], axis=0)
    key_ext = low(f32dot("te,ed->td", tokens_ext, w_key))
    value_ext = low(f32dot("te,ed->td", tokens_ext, w_value))
    attn_t, probs = attend(query, key_ext, value_ext.T, relk, relq, bias)

    mixed = f32dot("dt,de->te", attn_t, w_output)
    hidden, mid_back = jax.vjp(layer_norm, tokens.astype(jnp.float32) + mixed, mid_gain, mid_bias)
    hidden_low = low(hidden)
    inner = f32dot("td,df->tf", hidden_low, w_inner)
    active, gelu_back = jax.vjp(functools.partial(jax.nn.gelu, approximate=False), inner)
    active_low = low(active)
    outer = f32dot("tf,fd->td", active_low, w_outer)
    final, end_back = jax.vjp(layer_norm, hidden + outer, end_gain, end_bias)
    layer_out = low(final)
    sum_grad, end_gain_part, end_bias_part = end_back(cotangent.astype(jnp.float32))
    outer_low = low(sum_grad)
    outer_part = low(f32dot("tf,td->fd", active_low, outer_low))
    inner_low = low(gelu_back(f32dot("td,fd->tf", outer_low, w_outer))[0])
    inner_part = low(f32dot("td,tf->df", hidden_low, inner_low))
    hidden_grad = sum_grad + f32dot("tf,df->td", inner_low, w_inner)
    resid_grad, mid_gain_part, mid_bias_part = mid_back(hidden_grad)
    mixed_low = low(resid_grad)
    output_part = low(f32dot("dt,te->de", attn_t, mixed_low))
    attn_grad = low(f32dot("te,de->td", mixed_low, w_output))

    inputs = {
        "q": query, "k": key_ext, "v": value_ext, "grad": attn_grad, "relk": relk, "relq": relq,
        "xt_key": jnp.concatenate([tokens_ext.T, to_table_t], axis=1),
        "xt_query": jnp.concatenate([tokens.T, from_table_t], axis=1),
        "w_query": w_query, "w_key": w_key, "w_value": w_value,
        "hot": jnp.concatenate([to_hot.T, from_hot.T], axis=1), "resid": resid_grad,
        "vectors": jnp.concatenate(
            [mid_gain_part, mid_bias_part, end_gain_part, end_bias_part] * 2
        ).reshape(8, width),
        "outer": outer_part, "inner": inner_part, "output": output_part, "probs_in": probs,
    }
    outer_w, inner_w, rest_w, norm_parts, tokens_grad = finish_of(inputs)
    query_w, key_w, value_w, output_w = (rest_w[at * width : (at + 1) * width] for at in range(4))
    table_w = rest_w[4 * width :]
    return (
        layer_out[None], tokens_grad[None],
        *(w.astype(jnp.float32) for w in (query_w, key_w, value_w, output_w, inner_w, outer_w, table_w)),
        *(norm_parts[at] for at in range(4)),
    )


def solution(mesh):
    split = P("rows", "seq", None)
    return jax.shard_map(
        shards,
        mesh=mesh,
        in_specs=(split, split) + (P(),) * 11 + (P("rows", None), P("rows", None), P()),
        out_specs=(split, split) + (P(),) * 11,
        check_vma=False,
    )
```

```python
import functools
import math

import jax
import jax.numpy as jnp
from jax import lax
from jax.experimental import pallas as pl
from jax.experimental.pallas import tpu as pltpu
from jax.sharding import PartitionSpec as P

H = 12
DH = 64
SPAN = 256
TILE = 128
REACH = 640
PAIR = 128
score_scale = 1.0 / math.sqrt(3 * DH)


def nt(left, right):
    return lax.dot_general(left, right, (((1,), (1,)), ((), ())), preferred_element_type=jnp.float32)


def nn(left, right):
    return lax.dot_general(left, right, (((1,), (0,)), ((), ())), preferred_element_type=jnp.float32)


def head_lanes(values, head):
    lane = lax.broadcasted_iota(jnp.int32, values.shape, 1)
    mine = (lane < DH) if head == 0 else (lane >= DH)
    return jnp.where(mine, values, jnp.zeros_like(values))


def unit(reverse):
    row = lax.broadcasted_iota(jnp.int32, (TILE, TILE), 0)
    col = lax.broadcasted_iota(jnp.int32, (TILE, TILE), 1)
    hit = (row + col == TILE - 1) if reverse else (row == col)
    return jnp.where(hit, 1.0, 0.0).astype(jnp.bfloat16)


def attend_back_kernel(
    q_ref, k_ref, v_ref, grad_ref, prob_ref, relk_ref, relq_ref,
    dq_ref, dk_ref, dv_ref, drelk_ref, drelq_ref, qt_ref, kt_ref,
):
    swap = unit(True)
    for source, result in ((q_ref, qt_ref), (k_ref, kt_ref)):
        for at in range(0, source.shape[0], TILE):
            flipped = nn(swap, source[pl.ds(at, TILE), :])
            result[:, pl.ds(at, TILE)] = flipped.T.astype(jnp.bfloat16)
    row = lax.broadcasted_iota(jnp.int32, (TILE, TILE), 0)
    col = lax.broadcasted_iota(jnp.int32, (TILE, TILE), 1)
    parts = REACH // TILE
    tiles = q_ref.shape[0] // TILE
    dk_ref[...] = jnp.zeros_like(dk_ref)
    dv_ref[...] = jnp.zeros_like(dv_ref)
    drelk_ref[...] = jnp.zeros_like(drelk_ref)
    drelq_ref[...] = jnp.zeros_like(drelq_ref)
    for tile in range(tiles):
        first = tile * TILE
        q_tile = q_ref[pl.ds(first, TILE), :]
        grad_tile = grad_ref[pl.ds(first, TILE), :]
        v_tile = v_ref[pl.ds(first, REACH), :]
        q_heads = [head_lanes(q_tile, head) for head in range(2)]
        grad_heads = [head_lanes(grad_tile, head) for head in range(2)]
        dq_heads = []
        lefts = [[] for _ in range(parts)]
        for head in range(2):
            lanes = pl.ds(head * DH, DH)
            probs = prob_ref[head, tile].astype(jnp.float32)
            weighted = probs * nt(v_tile, grad_heads[head])
            delta = jnp.sum(weighted, axis=0, keepdims=True)
            dscore = ((weighted - probs * delta) * score_scale).astype(jnp.bfloat16)
            turned = nt(swap, dscore)
            dband = pltpu.roll(turned, REACH - TILE + 1, 1, stride=1, stride_axis=0)
            dband = dband[:, : 2 * SPAN].astype(jnp.bfloat16)
            dq_heads.append(
                nn(turned.astype(jnp.bfloat16), k_ref[pl.ds(first, REACH), :])
                + nn(dband, relk_ref[...])
            )
            drelk_ref[lanes, :] += nn(qt_ref[lanes, pl.ds(first, TILE)], dband)
            for part in range(parts):
                flipped = nn(swap, dscore[part * TILE : (part + 1) * TILE, :])
                spun = pltpu.roll(flipped, 0, 1, stride=1, stride_axis=0)
                low = jnp.where(col >= row, spun, 0.0)
                dfrom = jnp.concatenate([low, spun - low], axis=1).astype(jnp.bfloat16)
                window = pl.ds((parts - 1 - part) * TILE, 2 * TILE)
                drelq_ref[lanes, window] += nn(kt_ref[lanes, pl.ds(first + part * TILE, TILE)], dfrom)
                lefts[part] += [flipped.astype(jnp.bfloat16), dfrom]
        dq_turned = jnp.where(col < DH, dq_heads[0], dq_heads[1]).astype(jnp.bfloat16)
        dq_ref[pl.ds(first, TILE), :] = nn(swap, dq_turned).astype(dq_ref.dtype)
        dv_ref[pl.ds(first, REACH), :] += nn(
            jnp.concatenate([prob_ref[0, tile], prob_ref[1, tile]], axis=1),
            jnp.concatenate(grad_heads, axis=0),
        )
        for part in range(parts):
            window = relq_ref[pl.ds((parts - 1 - part) * TILE, 2 * TILE), :]
            right = jnp.concatenate(
                [q_heads[0], head_lanes(window, 0), q_heads[1], head_lanes(window, 1)], axis=0
            )
            dk_ref[pl.ds(first + part * TILE, TILE), :] += nn(
                jnp.concatenate(lefts[part], axis=1), right
            )


def attend_back(query, key_ext, value_ext, grad, probs, relk, relq):
    block_len, width = query.shape
    ext_len = key_ext.shape[0]
    tiles = block_len // TILE
    pairs = width // PAIR
    table = 2 * SPAN
    cols = lambda n: pl.BlockSpec((n, PAIR), lambda p: (0, p))
    rows = lambda n: pl.BlockSpec((PAIR, n), lambda p: (p, 0))
    f32 = lambda *s: jax.ShapeDtypeStruct(s, jnp.float32)
    return pl.pallas_call(
        attend_back_kernel,
        grid=(pairs,),
        in_specs=[
            cols(block_len), cols(ext_len), cols(ext_len), cols(block_len),
            pl.BlockSpec((2, tiles, REACH, TILE), lambda p: (p, 0, 0, 0)),
            cols(table), cols(table + 2 * TILE),
        ],
        out_specs=[cols(block_len), cols(ext_len), cols(ext_len), rows(table), rows(table + 2 * TILE)],
        out_shape=[
            jax.ShapeDtypeStruct((block_len, width), jnp.bfloat16),
            f32(ext_len, width), f32(ext_len, width), f32(width, table), f32(width, table + 2 * TILE),
        ],
        scratch_shapes=[
            pltpu.VMEM((PAIR, block_len), jnp.bfloat16), pltpu.VMEM((PAIR, ext_len), jnp.bfloat16),
        ],
        compiler_params=pltpu.CompilerParams(vmem_limit_bytes=48 * 2**20),
        name="attend_back",
    )(query, key_ext, value_ext, grad, probs, relk, relq)


MESH = pl.DeviceIdType.MESH
PACK = 16


norm_eps = 1e-07
masked_score = -1e30
inverse_root_two = math.sqrt(0.5)
density_at_zero = 1.0 / math.sqrt(2.0 * math.pi)


def gelu_both(values):
    size = jnp.abs(values) * inverse_root_two
    t = 1.0 / (1.0 + 0.3275911 * size)
    poly = 1.061405429 * t - 1.453152027
    poly = poly * t + 1.421413741
    poly = poly * t - 0.284496736
    poly = poly * t + 0.254829592
    bell = jnp.exp(-size * size)
    tail = 0.5 * poly * t * bell
    share = jnp.where(values >= 0.0, 1.0 - tail, tail)
    return values * share, share + values * bell * density_at_zero


def mean_of(values):
    return jnp.mean(values, axis=-1, keepdims=True)


def by_blocks(width, body, step=256):
    def one(i, carry):
        body(pl.ds(pl.multiple_of(i * step, step), step))
        return carry

    lax.fori_loop(0, width // step, one, 0)


def column_of(row_values):
    row = lax.broadcasted_iota(jnp.int32, (TILE, TILE), 0)
    col = lax.broadcasted_iota(jnp.int32, (TILE, TILE), 1)
    return jnp.sum(jnp.where(row == col, row_values, 0), axis=1, keepdims=True)


def mask_of(r, seq_count):
    ext_len, block_len = r["bias"].shape
    place = lax.axis_index("seq")
    row_len = block_len * seq_count
    ends, end = [], 0
    for number in range(r["lengths"].shape[1]):
        end = end + r["lengths"][0, number]
        ends.append(end)

    def segment(slots):
        return sum((slots >= end).astype(jnp.int32) for end in ends)

    query = place * block_len + lax.broadcasted_iota(jnp.int32, (1, block_len), 1)
    query_segment = segment(query)
    for block in range(ext_len // TILE):
        first = place * block_len - SPAN + block * TILE
        line = lax.clamp(0, place * (block_len // TILE) - SPAN // TILE + block, row_len // TILE - 1)
        keep = column_of(r["keep"][pl.ds(line, 1), :])
        key = first + lax.broadcasted_iota(jnp.int32, (TILE, 1), 0)
        key_segment = jnp.where((key >= 0) & (key < row_len), segment(key), -1)
        apart = key - query
        seen = (key_segment == query_segment) & (jnp.abs(apart) < SPAN)
        seen = seen & ((keep == 1) | (apart == 0))
        r["bias"][pl.ds(block * TILE, TILE), :] = jnp.where(seen, 0.0, masked_score)


def attend_pair(pair, buf, r):
    eye = unit(False)
    log_two = score_scale * math.log2(math.e)
    lanes = pl.ds(pl.multiple_of(pair * PAIR, PAIR), PAIR)
    tiles = r["q"].shape[0] // TILE
    parts = REACH // TILE
    for at in range(0, r["v"].shape[0], TILE):
        r["vt"][:, pl.ds(at, TILE)] = r["v"][pl.ds(at, TILE), lanes].T
    for tile in range(tiles):
        first = tile * TILE
        q_tile = r["q"][pl.ds(first, TILE), lanes]
        outs = []
        for head in range(2):
            score_ref = r["scores"].at[head]
            q_head = head_lanes(q_tile, head)
            band = nt(q_head, r["relk"][:, lanes])
            band = jnp.concatenate([band, jnp.zeros((TILE, REACH - 2 * SPAN), jnp.float32)], axis=1)
            to_term = pltpu.roll(band, 0, 1, stride=1, stride_axis=0).astype(jnp.bfloat16)
            for part in range(parts):
                at = first + part * TILE
                k_part = r["k"][pl.ds(at, TILE), lanes]
                window = r["relq"][pl.ds((parts - 1 - part) * TILE, 2 * TILE), lanes]
                from_band = nt(head_lanes(k_part, head), window)
                from_term = pltpu.roll(from_band, TILE + 1, 1, stride=1, stride_axis=0)[:, :TILE]
                left = jnp.concatenate([k_part, eye], axis=1)
                right = jnp.concatenate([q_head, to_term[:, part * TILE : (part + 1) * TILE]], axis=1)
                score_ref[pl.ds(part * TILE, TILE), :] = (
                    nt(left, right) + from_term + r["bias"][pl.ds(at, TILE), pl.ds(first, TILE)]
                )
            scores = score_ref[...]
            top = jnp.max(scores, axis=0, keepdims=True)
            weights = jnp.exp2((scores - top) * log_two)
            total = jnp.sum(weights, axis=0, keepdims=True)
            probs = (weights * (1.0 / total)).astype(jnp.bfloat16)
            r["probs"][buf, head, tile] = probs
            outs.append(nn(r["vt"][pl.ds(head * DH, DH), pl.ds(first, REACH)], probs))
        both = jnp.concatenate(outs, axis=0)
        r["attn_t"][lanes, pl.ds(first, TILE)] = both.astype(jnp.bfloat16)
        r["attn"][pl.ds(first, TILE), lanes] = both.T.astype(jnp.bfloat16)


START_HBM = (
    "tokens", "rel_table", "w_query", "w_key", "w_value", "w_output", "w_inner", "w_outer", "cotangent",
)
START_VMEM = ("rel_buckets", "mid_gain", "mid_bias", "end_gain", "end_bias", "keep")
START_IN = START_HBM + START_VMEM + ("lengths",)
START_KEPT = (
    "x", "q", "k", "v", "relk", "relq", "to_table", "from_table", "hot", "grad", "resid",
    "outer", "inner", "output",
)
START_OUT = START_KEPT + ("probs_out", "layer_out", "vectors")
START_SCRATCH = START_KEPT + (
    "rel_table", "w_query", "w_key", "w_value", "w_output", "w_inner", "w_outer", "cotangent",
    "bias", "vt", "scores", "probs", "attn", "attn_t", "mixed", "hidden", "z_mid", "root_mid", "hidden_low",
    "active", "slope", "inner_low", "sum_grad", "outer_low",
    "load_sem", "keep_sem", "probs_sem", "send_sem", "recv_sem",
)


def start_kernel(seq_count, *refs):
    given = dict(zip(START_IN, refs))
    outs = dict(zip(START_OUT, refs[len(START_IN) :]))
    r = dict(zip(START_SCRATCH, refs[len(START_IN) + len(START_OUT) :]))
    r.update((name, given[name]) for name in START_VMEM + ("lengths",))
    block_len, width = r["q"].shape
    ext_len, table_len = r["x"].shape[0], r["to_table"].shape[0]
    inner_width = r["w_inner"].shape[1]
    pairs = width // PAIR
    own = pl.ds(SPAN, block_len)

    loads = {}
    for number, name in enumerate(START_HBM):
        target = r["x"].at[own] if name == "tokens" else r[name]
        loads[name] = pltpu.make_async_copy(given[name], target, r["load_sem"].at[number])
        loads[name].start()
    row, place = lax.axis_index("rows"), lax.axis_index("seq")
    before = {"rows": row, "seq": lax.rem(place + seq_count - 1, seq_count)}
    after = {"rows": row, "seq": lax.rem(place + 1, seq_count)}
    barrier = pltpu.get_barrier_semaphore()
    for device in (before, after):
        pl.semaphore_signal(barrier, inc=1, device_id=device, device_id_type=MESH)
    pl.semaphore_wait(barrier, 2)
    halos = [
        pltpu.make_async_remote_copy(
            src_ref=given["tokens"], dst_ref=r["x"].at[pl.ds(at, SPAN)], send_sem=r["send_sem"].at[number],
            recv_sem=r["recv_sem"].at[number], device_id=device, device_id_type=MESH,
        )
        for number, (at, device) in enumerate(((0, after), (SPAN + block_len, before)))
    ]
    for copy in halos:
        copy.start()

    def keep(name):
        pltpu.make_async_copy(r[name], outs[name], r["keep_sem"].at[START_KEPT.index(name)]).start()

    def low(values):
        return values.astype(jnp.bfloat16)

    place_of = lax.broadcasted_iota(jnp.int32, (table_len, table_len), 0)
    turned_bucket = pltpu.roll(r["rel_buckets"][...].reshape(1, table_len), table_len - 1, 1)
    to_pos = jnp.clip(turned_bucket + SPAN, 0, table_len - 1)
    from_pos = jnp.clip(SPAN - turned_bucket, 0, table_len - 1)
    r["hot"][:, pl.ds(table_len, table_len)] = low(jnp.where(place_of == from_pos, 1.0, 0.0))
    to_turned = low(jnp.where(place_of == to_pos, 1.0, 0.0))
    for at in range(0, table_len, TILE):
        r["hot"][:, pl.ds(at, TILE)] = low(
            nn(to_turned[:, table_len - TILE - at : table_len - at], unit(True))
        )
    keep("hot")
    mask_of(r, seq_count)
    loads["rel_table"].wait()
    for number, name in enumerate(("to", "from")):
        hot = r["hot"][:, pl.ds(number * table_len, table_len)].T

        def table_cols(cols, hot=hot, name=name):
            r[name + "_table"][:, cols] = low(nn(hot, r["rel_table"][:, cols]))

        by_blocks(width, table_cols)
        keep(name + "_table")
    loads["w_query"].wait()
    loads["tokens"].wait()
    r["relq"][pl.ds(0, TILE), :] = jnp.zeros((TILE, width), jnp.bfloat16)
    r["relq"][pl.ds(TILE + table_len, TILE), :] = jnp.zeros((TILE, width), jnp.bfloat16)

    def query_cols(cols):
        r["q"][:, cols] = low(nn(r["x"][own, :], r["w_query"][:, cols]))
        r["relq"][pl.ds(TILE, table_len), cols] = low(nn(r["from_table"][...], r["w_query"][:, cols]))

    by_blocks(width, query_cols)
    keep("q")
    keep("relq")
    loads["w_key"].wait()

    def relk_cols(cols):
        r["relk"][:, cols] = low(nn(r["to_table"][...], r["w_key"][:, cols]))

    by_blocks(width, relk_cols)
    keep("relk")
    loads["w_value"].wait()
    for copy in halos:
        copy.wait()
    keep("x")

    def pair_cols(cols):
        r["k"][:, cols] = low(nn(r["x"][...], r["w_key"][:, cols]))
        r["v"][:, cols] = low(nn(r["x"][...], r["w_value"][:, cols]))

    by_blocks(width, pair_cols)
    keep("k")
    keep("v")

    def probs_copy(pair, buf):
        return pltpu.make_async_copy(
            r["probs"].at[buf], outs["probs_out"].at[pl.ds(2 * pair, 2)], r["probs_sem"].at[buf]
        )

    def one_pair(pair, carry):
        buf = lax.rem(pair, 2)

        @pl.when(pair >= 2)
        def _():
            probs_copy(pair - 2, buf).wait()

        attend_pair(pair, buf, r)
        probs_copy(pair, buf).start()
        return carry

    lax.fori_loop(0, pairs, one_pair, 0)

    for name in ("w_output", "w_inner", "w_outer", "cotangent"):
        loads[name].wait()

    def mixed_cols(cols):
        r["mixed"][:, cols] = nn(r["attn"][...], r["w_output"][:, cols])

    by_blocks(width, mixed_cols)
    high = 64
    mid_gain, mid_bias, end_gain, end_bias = (
        r[name][...].reshape(1, width) for name in ("mid_gain", "mid_bias", "end_gain", "end_bias")
    )

    def mid_rows(rows):
        mine = pl.ds(pl.multiple_of(SPAN + rows.start, high), high)
        values = r["x"][mine, :].astype(jnp.float32) + r["mixed"][rows, :]
        centre = values - mean_of(values)
        root = lax.rsqrt(mean_of(centre * centre) + norm_eps)
        z = centre * root
        hidden = z * mid_gain + mid_bias
        r["z_mid"][rows, :] = z
        r["root_mid"][rows, :] = jnp.broadcast_to(root, (high, TILE))
        r["hidden"][rows, :] = hidden
        r["hidden_low"][rows, :] = low(hidden)

    by_blocks(block_len, mid_rows, high)

    def active_cols(cols):
        active, slope = gelu_both(nn(r["hidden_low"][...], r["w_inner"][:, cols]))
        r["active"][:, cols] = low(active)
        r["slope"][:, cols] = low(slope)

    by_blocks(inner_width, active_cols)

    def outer_cols(cols):
        r["mixed"][:, cols] = nn(r["active"][...], r["w_outer"][:, cols])

    by_blocks(width, outer_cols)
    outs["vectors"][...] = jnp.zeros_like(outs["vectors"])

    def end_rows(rows):
        values = r["hidden"][rows, :] + r["mixed"][rows, :]
        centre = values - mean_of(values)
        root = lax.rsqrt(mean_of(centre * centre) + norm_eps)
        z = centre * root
        outs["layer_out"][rows, :] = low(z * end_gain + end_bias)
        cotangent = r["cotangent"][rows, :].astype(jnp.float32)
        outs["vectors"][pl.ds(2, 1), :] += jnp.sum(cotangent * z, axis=0, keepdims=True)
        outs["vectors"][pl.ds(3, 1), :] += jnp.sum(cotangent, axis=0, keepdims=True)
        grad = cotangent * end_gain
        sum_grad = root * (grad - mean_of(grad) - z * mean_of(grad * z))
        r["sum_grad"][rows, :] = sum_grad
        r["outer_low"][rows, :] = low(sum_grad)

    by_blocks(block_len, end_rows, high)

    def inner_cols(cols):
        grad = nt(r["outer_low"][...], r["w_outer"][cols, :])
        r["inner_low"][:, cols] = low(grad * r["slope"][:, cols].astype(jnp.float32))

    by_blocks(inner_width, inner_cols)

    def outer_part(rows):
        r["outer"][rows, :] = low(nn(r["active"][:, rows].T, r["outer_low"][...]))

    by_blocks(inner_width, outer_part)
    keep("outer")

    def hidden_cols(cols):
        r["mixed"][:, cols] = r["sum_grad"][:, cols] + nt(r["inner_low"][...], r["w_inner"][cols, :])

    by_blocks(width, hidden_cols)
    hidden_t = r["hidden_low"][...].T

    def inner_part(cols):
        r["inner"][:, cols] = low(nn(hidden_t, r["inner_low"][:, cols]))

    by_blocks(inner_width, inner_part)
    keep("inner")

    def resid_rows(rows):
        hidden_grad, z = r["mixed"][rows, :], r["z_mid"][rows, :]
        outs["vectors"][pl.ds(0, 1), :] += jnp.sum(hidden_grad * z, axis=0, keepdims=True)
        outs["vectors"][pl.ds(1, 1), :] += jnp.sum(hidden_grad, axis=0, keepdims=True)
        grad = hidden_grad * mid_gain
        root = r["root_mid"][rows, pl.ds(0, 1)]
        resid = root * (grad - mean_of(grad) - z * mean_of(grad * z))
        r["resid"][rows, :] = resid
        r["outer_low"][rows, :] = low(resid)

    by_blocks(block_len, resid_rows, high)
    keep("resid")

    def grad_cols(cols):
        r["grad"][:, cols] = low(nt(r["outer_low"][...], r["w_output"][cols, :]))
        r["output"][:, cols] = low(nn(r["attn_t"][...], r["outer_low"][:, cols]))

    by_blocks(width, grad_cols)
    keep("grad")
    keep("output")
    for pair in (pairs - 2, pairs - 1):
        probs_copy(pair, pair % 2).wait()
    for number, name in enumerate(START_KEPT):
        pltpu.make_async_copy(r[name], outs[name], r["keep_sem"].at[number]).wait()


def start(inputs, seq_count):
    block_len, width = inputs["tokens"].shape
    table_len = inputs["rel_table"].shape[0]
    inner_width = inputs["w_inner"].shape[1]
    ext_len = block_len + 2 * SPAN
    tiles = block_len // TILE
    heads = 2 * (width // PAIR)
    sizes = {
        "x": (ext_len, width), "q": (block_len, width), "k": (ext_len, width), "v": (ext_len, width),
        "relk": (table_len, width), "relq": (table_len + 2 * TILE, width), "to_table": (table_len, width),
        "from_table": (table_len, width), "hot": (table_len, 2 * table_len), "grad": (block_len, width),
        "resid": (block_len, width), "outer": (inner_width, width), "inner": (width, inner_width),
        "output": (width, width),
    }
    kinds = {name: jnp.float32 if name == "resid" else jnp.bfloat16 for name in START_KEPT}
    bf = lambda *shape: pltpu.VMEM(shape, jnp.bfloat16)
    f32 = lambda *shape: pltpu.VMEM(shape, jnp.float32)
    dma = pltpu.SemaphoreType.DMA
    any_spec = pl.BlockSpec(memory_space=pl.ANY)
    vmem = pl.BlockSpec(memory_space=pltpu.VMEM)
    smem = pl.BlockSpec(memory_space=pltpu.SMEM)
    values = pl.pallas_call(
        functools.partial(start_kernel, seq_count),
        in_specs=[any_spec] * len(START_HBM) + [vmem] * len(START_VMEM) + [smem],
        out_specs=[any_spec] * (len(START_KEPT) + 1) + [vmem] * 2,
        out_shape=[
            *(jax.ShapeDtypeStruct(sizes[name], kinds[name]) for name in START_KEPT),
            jax.ShapeDtypeStruct((heads, tiles, REACH, TILE), jnp.bfloat16),
            jax.ShapeDtypeStruct((block_len, width), jnp.bfloat16),
            jax.ShapeDtypeStruct((8, width), jnp.float32),
        ],
        scratch_shapes=[
            *(pltpu.VMEM(sizes[name], kinds[name]) for name in START_KEPT),
            *(pltpu.VMEM(inputs[name].shape, inputs[name].dtype) for name in START_HBM[1:]),
            f32(ext_len, block_len), bf(PAIR, ext_len), f32(2, REACH, TILE), bf(2, 2, tiles, REACH, TILE),
            bf(block_len, width), bf(width, block_len), f32(block_len, width), f32(block_len, width),
            f32(block_len, width), f32(block_len, TILE), bf(block_len, width),
            bf(block_len, inner_width), bf(block_len, inner_width), bf(block_len, inner_width),
            f32(block_len, width), bf(block_len, width),
            dma((len(START_HBM),)), dma((len(START_KEPT),)), dma((2,)), dma((2,)), dma((2,)),
        ],
        compiler_params=pltpu.CompilerParams(
            collective_id=1, has_side_effects=True, vmem_limit_bytes=60 * 2**20
        ),
        name="start",
    )(*(inputs[name] for name in START_IN))
    return dict(zip(START_OUT, values))


class Line:
    def __init__(self, side, row_step, seq_step):
        self.side = side
        row, place = lax.axis_index("rows"), lax.axis_index("seq")
        away = 1 - 2 * side
        self.device = {"rows": row + away * row_step, "seq": place + away * seq_step}


def lines_of():
    row, place = lax.axis_index("rows"), lax.axis_index("seq")
    first, second, third, fourth = (place // step % 2 for step in (1, 2, 4, 8))
    core = Line(row, 1, 0)
    near = Line(first + row * (second - first), 0, 1 + row)
    cross = Line(second + row * (first - second), 0, 2 - row)
    low_z, high_z = Line(third, 0, 4), Line(fourth, 0, 8)
    return (core, near, cross, low_z, high_z), (core, low_z, high_z, near, cross)


def add_rows(target, at, source, rows, out, out_at):
    step = next(s for s in (48, 32, PACK) if rows % s == 0)

    def body(i, carry):
        here = pl.multiple_of(i * step, PACK)
        mine = pl.ds(pl.multiple_of(at + here, PACK), step)
        goal = pl.ds(pl.multiple_of(out_at + here, PACK), step)
        out[goal, :] = target[mine, :] + source[pl.ds(here, step), :]
        return carry

    lax.fori_loop(0, rows // step, body, 0)


class Chunk:
    def __init__(self, index, which, start, half, base, width, z_first):
        self.index, self.which, self.start, self.half = index, which, start, half
        self.base, self.width, self.z_first = base, width, z_first

    def part(self, refs, side):
        if self.which == "inner":
            block, low_row = (self.start // 2) // self.width, (self.start // 2) % self.width
            col = (2 * block + side) * self.width
            return refs["inner"].at[pl.ds(low_row, self.half), pl.ds(pl.multiple_of(col, PAIR), self.width)]
        first = pl.multiple_of(self.start + side * self.half, PACK)
        return refs[self.which].at[pl.ds(first, self.half)]


def chunks_of(spec, unit, width):
    chunks, starts, base = [], {}, 0
    for which, units, z_first in spec:
        half = units * unit // 2
        start = starts.get(which, 0)
        chunks.append(Chunk(len(chunks), which, start, half, base, width, z_first))
        starts[which] = start + 2 * half
        base += half
    return chunks, base


class Sum:
    phases = 5
    last = 2 * phases

    def __init__(self, chunks, ins, outs, acc, recv, own_sem, send_sem, recv_sem):
        self.chunks, self.ins, self.outs = chunks, ins, outs
        self.acc, self.recv = acc, recv
        self.own_sem, self.send_sem, self.recv_sem = own_sem, send_sem, recv_sem
        self.row = lax.axis_index("rows")
        self.plane_first, self.z_first = lines_of()
        self.recv_at = [2 * chunk.base for chunk in chunks]

    def greet(self, more):
        barrier = pltpu.get_barrier_semaphore()
        devices = [line.device for line in self.plane_first] + more
        for device in devices:
            pl.semaphore_signal(barrier, inc=1, device_id=device, device_id_type=MESH)
        pl.semaphore_wait(barrier, len(devices))

    def lines(self, chunk):
        return self.z_first if chunk.z_first else self.plane_first

    def offset(self, chunk, phase):
        at, rows = chunk.base, chunk.half
        for line in self.lines(chunk)[1 : phase + 1]:
            rows //= 2
            at = at + line.side * rows
        return at

    def received(self, chunk, phase):
        at = self.recv_at[chunk.index] + sum(chunk.half >> p for p in range(phase))
        return self.recv.at[pl.ds(at, chunk.half >> phase)]

    def copies(self, chunk, stage):
        gather = stage >= self.phases
        phase = self.last - 1 - stage if gather else stage
        line, rows = self.lines(chunk)[phase], chunk.half >> phase
        local = None
        if gather:
            at = chunk.base + self.offset(chunk, phase)
            source = self.recv.at[pl.ds(pl.multiple_of(at, PACK), rows)]
            target = source
            if phase == 0:
                target = chunk.part(self.outs, self.row)
                local = (source, target)
        elif phase == 0:
            source, target = chunk.part(self.ins, 1 - self.row), self.received(chunk, 0)
            local = (chunk.part(self.ins, self.row), self.acc.at[pl.ds(chunk.base, rows)])
        else:
            at = self.offset(chunk, phase - 1) + (1 - line.side) * rows
            source = self.acc.at[pl.ds(pl.multiple_of(at, PACK), rows)]
            target = self.received(chunk, phase)
        sem = chunk.index * self.last + stage
        copies = [
            pltpu.make_async_remote_copy(
                src_ref=source, dst_ref=target, send_sem=self.send_sem.at[sem],
                recv_sem=self.recv_sem.at[sem], device_id=line.device, device_id_type=MESH,
            )
        ]
        if local is not None:
            copies.append(pltpu.make_async_copy(*local, self.own_sem.at[chunk.index]))
        return copies

    def step(self, c, stage):
        chunk = self.chunks[c]
        if stage > 0:
            for copy in self.copies(chunk, stage - 1):
                copy.wait()
        if 0 < stage <= self.phases:
            phase = stage - 1
            at, rows = self.offset(chunk, phase), chunk.half >> phase
            if stage == self.phases:
                add_rows(self.acc, at, self.received(chunk, phase), rows, self.recv, chunk.base + at)
            else:
                add_rows(self.acc, at, self.received(chunk, phase), rows, self.acc, at)
        if stage < self.last:
            for copy in self.copies(chunk, stage):
                copy.start()


class VectorSum:
    def __init__(self, lines, acc, recv, send_sem, recv_sem):
        self.lines, self.acc, self.recv, self.send_sem, self.recv_sem = lines, acc, recv, send_sem, recv_sem

    def copy(self, phase):
        return pltpu.make_async_remote_copy(
            src_ref=self.acc.at[phase], dst_ref=self.recv.at[phase], send_sem=self.send_sem.at[phase],
            recv_sem=self.recv_sem.at[phase], device_id=self.lines[phase].device, device_id_type=MESH,
        )

    def start(self, phase):
        self.copy(phase).start()

    def end(self, phase):
        self.copy(phase).wait()
        self.acc[phase + 1] = self.acc[phase] + self.recv[phase]


def back_of_pair(pair, buf, r):
    swap = unit(True)
    lanes_at = pl.multiple_of(pair * PAIR, PAIR)
    lanes_here = pl.ds(lanes_at, PAIR)
    row = lax.broadcasted_iota(jnp.int32, (TILE, TILE), 0)
    col = lax.broadcasted_iota(jnp.int32, (TILE, TILE), 1)
    parts = REACH // TILE
    block_len, ext_len = r["q"].shape[0], r["k"].shape[0]
    tiles = block_len // TILE
    qt_ref, kt_ref, dk_ref, dv_ref, drelk_ref, drelq_ref = (
        r[name] for name in ("qt", "kt", "dk_pair", "dv_pair", "drelk_t", "drelq_t")
    )
    for source, result in ((r["q"], qt_ref), (r["k"], kt_ref)):
        for at in range(0, source.shape[0], TILE):
            flipped = nn(swap, source[pl.ds(at, TILE), lanes_here])
            result[:, pl.ds(at, TILE)] = flipped.T.astype(jnp.bfloat16)
    dk_ref[...] = jnp.zeros_like(dk_ref)
    dv_ref[...] = jnp.zeros_like(dv_ref)
    drelk_ref[...] = jnp.zeros_like(drelk_ref)
    drelq_ref[...] = jnp.zeros_like(drelq_ref)
    for tile in range(tiles):
        first = tile * TILE
        q_tile = r["q"][pl.ds(first, TILE), lanes_here]
        grad_tile = r["grad"][pl.ds(first, TILE), lanes_here]
        v_tile = r["v"][pl.ds(first, REACH), lanes_here]
        q_heads = [head_lanes(q_tile, head) for head in range(2)]
        grad_heads = [head_lanes(grad_tile, head) for head in range(2)]
        dq_heads = []
        lefts = [[] for _ in range(parts)]
        for head in range(2):
            lanes = pl.ds(head * DH, DH)
            probs = r["probs"][buf, head, tile].astype(jnp.float32)
            weighted = probs * nt(v_tile, grad_heads[head])
            delta = jnp.sum(weighted, axis=0, keepdims=True)
            dscore = ((weighted - probs * delta) * score_scale).astype(jnp.bfloat16)
            turned = nt(swap, dscore)
            dband = pltpu.roll(turned, REACH - TILE + 1, 1, stride=1, stride_axis=0)
            dband = dband[:, : 2 * SPAN].astype(jnp.bfloat16)
            dq_heads.append(
                nn(turned.astype(jnp.bfloat16), r["k"][pl.ds(first, REACH), lanes_here])
                + nn(dband, r["relk"][:, lanes_here])
            )
            drelk_ref[lanes, :] += nn(qt_ref[lanes, pl.ds(first, TILE)], dband)
            for part in range(parts):
                flipped = nn(swap, dscore[part * TILE : (part + 1) * TILE, :])
                spun = pltpu.roll(flipped, 0, 1, stride=1, stride_axis=0)
                near = jnp.where(col >= row, spun, 0.0)
                dfrom = jnp.concatenate([near, spun - near], axis=1).astype(jnp.bfloat16)
                window = pl.ds((parts - 1 - part) * TILE, 2 * TILE)
                drelq_ref[lanes, window] += nn(kt_ref[lanes, pl.ds(first + part * TILE, TILE)], dfrom)
                lefts[part] += [flipped.astype(jnp.bfloat16), dfrom]
        dq_turned = jnp.where(col < DH, dq_heads[0], dq_heads[1]).astype(jnp.bfloat16)
        r["dq"][pl.ds(first, TILE), lanes_here] = nn(swap, dq_turned).astype(jnp.bfloat16)
        dv_ref[pl.ds(first, REACH), :] += nn(
            jnp.concatenate([r["probs"][buf, 0, tile], r["probs"][buf, 1, tile]], axis=1),
            jnp.concatenate(grad_heads, axis=0),
        )
        for part in range(parts):
            window = r["relq"][pl.ds((parts - 1 - part) * TILE, 2 * TILE), lanes_here]
            right = jnp.concatenate(
                [q_heads[0], head_lanes(window, 0), q_heads[1], head_lanes(window, 1)], axis=0
            )
            dk_ref[pl.ds(first + part * TILE, TILE), :] += nn(
                jnp.concatenate(lefts[part], axis=1), right
            )
    r["dv"][:, lanes_here] = dv_ref[...].astype(jnp.bfloat16)
    for at in range(0, ext_len, TILE):
        r["dk"][pl.ds(at, TILE), lanes_here] = nn(
            swap, dk_ref[pl.ds(at, TILE), :].astype(jnp.bfloat16)
        ).astype(jnp.bfloat16)
    r["dk"][pl.ds(ext_len, 2 * SPAN), lanes_here] = drelk_ref[...].T.astype(jnp.bfloat16)
    r["dq"][pl.ds(block_len, 2 * SPAN), lanes_here] = (
        drelq_ref[:, pl.ds(TILE, 2 * SPAN)].T.astype(jnp.bfloat16)
    )


SOONER = ("q", "k", "v", "grad", "relk", "relq")
LATER = ("x", "to_table", "from_table", "w_query", "w_key", "w_value", "hot", "resid")
FINISH_IN = SOONER + LATER + ("vectors", "outer", "inner", "output", "probs_in")
FINISH_OUT = ("outer", "inner", "rest", "vectors", "tokens_grad")
FINISH_SCRATCH = (
    "probs", "qt", "kt", "dk_pair", "dv_pair", "drelk_t", "drelq_t", "dq", "dk", "dv", "rest", "table",
    "xt_query", "xt_key",
    "halo", "halo_got", "own_grad", "acc", "recv", "vec_acc", "vec_recv", "own_sem", "send_sem", "recv_sem",
    "vec_send", "vec_got", "probs_sem", "halo_send", "halo_recv", "load_sem",
)


def finish_kernel(chunks, schedule, seq_count, *refs):
    r = dict(zip(FINISH_IN, refs))
    outs = dict(zip(FINISH_OUT, refs[len(FINISH_IN) :]))
    scratch = refs[len(FINISH_IN) + len(FINISH_OUT) :]
    r.update(zip(FINISH_SCRATCH, scratch))
    loads = {}
    for number, (name, held) in enumerate(zip(SOONER + LATER, scratch[len(FINISH_SCRATCH) :])):
        loads[name] = pltpu.make_async_copy(r[name], held, r["load_sem"].at[number])
        loads[name].start()
        r[name] = held
    block_len, width = r["q"].shape
    ext_len = r["k"].shape[0]
    pairs = width // PAIR
    total = Sum(chunks, r, outs, r["acc"], r["recv"], r["own_sem"], r["send_sem"], r["recv_sem"])
    row, place = lax.axis_index("rows"), lax.axis_index("seq")
    before = {"rows": row, "seq": lax.rem(place + seq_count - 1, seq_count)}
    after = {"rows": row, "seq": lax.rem(place + 1, seq_count)}
    total.greet([before, after])
    vec = VectorSum(total.plane_first, r["vec_acc"], r["vec_recv"], r["vec_send"], r["vec_got"])
    vec.acc[0] = r["vectors"][...]

    def probs_copy(pair, buf):
        return pltpu.make_async_copy(
            r["probs_in"].at[pl.ds(2 * pair, 2)], r["probs"].at[buf], r["probs_sem"].at[buf]
        )

    def between(pair):
        if 0 < pair <= total.phases:
            vec.end(pair - 1)
        if pair < total.phases:
            vec.start(pair)
        for c, stage in schedule[pair + 1]:
            total.step(c, stage)

    def one_pair(pair, carry):
        buf = lax.rem(pair, 2)

        @pl.when(pair + 1 < pairs)
        def _():
            probs_copy(pair + 1, 1 - buf).start()

        probs_copy(pair, buf).wait()
        back_of_pair(pair, buf, r)
        for at in range(pairs):
            pl.when(pair == at)(functools.partial(between, at))
        return carry

    def turn_tokens(rows):
        r["xt_key"][:, rows] = r["x"][rows, :].T

    def turn_tables(rows):
        r["xt_key"][:, pl.ds(pl.multiple_of(ext_len + rows.start, PAIR), rows.size)] = r["to_table"][rows, :].T
        r["xt_query"][:, pl.ds(pl.multiple_of(block_len + rows.start, PAIR), rows.size)] = (
            r["from_table"][rows, :].T
        )

    def turn():
        by_blocks(ext_len, turn_tokens)
        by_blocks(2 * SPAN, turn_tables)
        r["xt_query"][:, pl.ds(0, block_len)] = r["xt_key"][:, pl.ds(SPAN, block_len)]

    def query_cols(cols):
        r["rest"][pl.ds(0, width), cols] = nn(r["xt_query"][...], r["dq"][:, cols]).astype(jnp.bfloat16)

    def key_cols(cols):
        r["rest"][pl.ds(width, width), cols] = nn(r["xt_key"][...], r["dk"][:, cols]).astype(jnp.bfloat16)

    def value_cols(cols):
        r["rest"][pl.ds(2 * width, width), cols] = nn(
            r["xt_key"][:, pl.ds(0, ext_len)], r["dv"][:, cols]
        ).astype(jnp.bfloat16)

    def table_cols(cols):
        r["table"][pl.ds(0, 2 * SPAN), cols] = nt(
            r["dk"][pl.ds(ext_len, 2 * SPAN), :], r["w_key"][cols, :]
        ).astype(jnp.bfloat16)
        r["table"][pl.ds(2 * SPAN, 2 * SPAN), cols] = nt(
            r["dq"][pl.ds(block_len, 2 * SPAN), :], r["w_query"][cols, :]
        ).astype(jnp.bfloat16)

    def bucket_cols(cols):
        r["rest"][pl.ds(4 * width, 2 * SPAN), cols] = nn(r["hot"][...], r["table"][:, cols]).astype(
            jnp.bfloat16
        )

    def halo_cols(cols):
        for at in (0, ext_len - SPAN):
            rows = pl.ds(at, SPAN)
            grad = nt(r["dk"][rows, :], r["w_key"][cols, :]) + nt(r["dv"][rows, :], r["w_value"][cols, :])
            r["halo"][rows, cols] = grad.astype(jnp.bfloat16)

    def own_cols(cols):
        own, mid = pl.ds(0, block_len), pl.ds(SPAN, block_len)
        r["own_grad"][:, cols] = (
            r["resid"][:, cols]
            + nt(r["dq"][own, :], r["w_query"][cols, :])
            + nt(r["dk"][mid, :], r["w_key"][cols, :])
            + nt(r["dv"][mid, :], r["w_value"][cols, :])
        )

    output_copy = pltpu.make_async_copy(
        r["output"], r["rest"].at[pl.ds(3 * width, width)], r["own_sem"].at[len(chunks)]
    )
    halos = [
        pltpu.make_async_remote_copy(
            src_ref=r["halo"].at[pl.ds(at, SPAN)], dst_ref=r["halo_got"].at[number],
            send_sem=r["halo_send"].at[number], recv_sem=r["halo_recv"].at[number],
            device_id=device, device_id_type=MESH,
        )
        for number, (at, device) in enumerate(((0, before), (ext_len - SPAN, after)))
    ]

    probs_copy(0, 0).start()
    output_copy.start()
    for c, stage in schedule[0]:
        total.step(c, stage)
    for name in SOONER:
        loads[name].wait()
    lax.fori_loop(0, pairs, one_pair, 0)
    output_copy.wait()
    for name in LATER:
        loads[name].wait()
    turn()
    pieces = ((query_cols,), (key_cols,), (value_cols,), (table_cols, bucket_cols), (halo_cols,), (own_cols,))
    for piece, steps in zip(pieces, schedule[pairs + 1 :]):
        for body in piece:
            by_blocks(width, body)
        if piece[0] is halo_cols:
            for copy in halos:
                copy.start()
        for c, stage in steps:
            total.step(c, stage)
    for copy in halos:
        copy.wait()
    grad = r["own_grad"][...]
    for number in range(2):
        grad = grad + r["halo_got"][number].astype(jnp.float32)
    outs["tokens_grad"][...] = grad.astype(jnp.bfloat16)
    outs["vectors"][...] = vec.acc[total.phases]


CHUNKS = (
    ("outer", 2, False),
    ("outer", 2, False),
    ("outer", 2, True),
    ("inner", 3, False),
    ("inner", 3, False),
    ("rest", 2, False),
    ("rest", 2, True),
    ("rest", 2, False),
    ("rest", 1, False),
)
SCHEDULE = (
    ((4, 0), (2, 0), (1, 0),),
    ((0, 0), (4, 1), (2, 1), (3, 0),),
    ((1, 1),),
    ((4, 2), (0, 1), (3, 1), (2, 2),),
    ((4, 3),),
    ((1, 2), (4, 4),),
    ((3, 2), (2, 3), (4, 5), (1, 3),),
    (),
    ((5, 0), (4, 6), (0, 2),),
    ((2, 4), (5, 1), (6, 0), (1, 4), (3, 3), (0, 3), (4, 7),),
    ((7, 0), (6, 1), (5, 2), (7, 1), (0, 4),),
    ((8, 0), (1, 5), (6, 2), (8, 1), (1, 6), (7, 2), (2, 5), (3, 4), (5, 3), (8, 2), (0, 5), (6, 3), (1, 7), (3, 5), (0, 6), (2, 6), (7, 3), (8, 3), (4, 8), (5, 4), (7, 4), (6, 4), (8, 4), (0, 7), (3, 6), (5, 5), (1, 8), (8, 5), (6, 5), (7, 5), (3, 7), (2, 7),),
    ((7, 6), (6, 6), (8, 6), (0, 8), (5, 6), (1, 9), (6, 7), (8, 7), (7, 7), (2, 8), (5, 7), (3, 8), (6, 8), (4, 9), (8, 8), (5, 8), (1, 10), (3, 9), (0, 9), (7, 8), (2, 9), (8, 9), (5, 9), (6, 9), (0, 10), (7, 9), (5, 10), (2, 10), (8, 10), (4, 10), (6, 10), (3, 10), (7, 10),),
)

def finish(inputs, seq_count):
    unit_rows = PACK * 2 * seq_count
    width = inputs["q"].shape[1]
    block_len, ext_len = inputs["q"].shape[0], inputs["k"].shape[0]
    chunks, rows = chunks_of(CHUNKS, unit_rows, width)
    sems = len(chunks) * Sum.last
    rest_rows = 4 * width + 2 * SPAN
    bf = lambda *shape: pltpu.VMEM(shape, jnp.bfloat16)
    f32 = lambda *shape: pltpu.VMEM(shape, jnp.float32)
    dma = pltpu.SemaphoreType.DMA
    vec_shape = inputs["vectors"].shape
    any_spec = pl.BlockSpec(memory_space=pl.ANY)
    vmem = pl.BlockSpec(memory_space=pltpu.VMEM)
    tiles = block_len // TILE
    return pl.pallas_call(
        functools.partial(finish_kernel, chunks, SCHEDULE, seq_count),
        in_specs=[vmem if name == "vectors" else any_spec for name in FINISH_IN],
        out_specs=[any_spec] * 3 + [vmem] * 2,
        out_shape=[
            jax.ShapeDtypeStruct(inputs["outer"].shape, jnp.bfloat16),
            jax.ShapeDtypeStruct(inputs["inner"].shape, jnp.bfloat16),
            jax.ShapeDtypeStruct((rest_rows, width), jnp.bfloat16),
            jax.ShapeDtypeStruct(vec_shape, jnp.float32),
            jax.ShapeDtypeStruct((block_len, width), jnp.bfloat16),
        ],
        scratch_shapes=[
            bf(2, 2, tiles, REACH, TILE), bf(PAIR, block_len), bf(PAIR, ext_len),
            f32(ext_len, PAIR), f32(ext_len, PAIR), f32(PAIR, 2 * SPAN), f32(PAIR, 2 * SPAN + 2 * TILE),
            bf(block_len + 2 * SPAN, width), bf(ext_len + 2 * SPAN, width), bf(ext_len, width),
            bf(rest_rows, width), bf(4 * SPAN, width),
            bf(width, block_len + 2 * SPAN), bf(width, ext_len + 2 * SPAN), bf(ext_len, width), bf(2, SPAN, width), f32(block_len, width),
            bf(rows, width), bf(2 * rows, width),
            f32(Sum.phases + 1, *vec_shape), f32(Sum.phases, *vec_shape),
            dma((len(chunks) + 1,)), dma((sems,)), dma((sems,)), dma((Sum.phases,)), dma((Sum.phases,)),
            dma((2,)), dma((2,)), dma((2,)), dma((len(SOONER + LATER),)),
            *(pltpu.VMEM(inputs[name].shape, inputs[name].dtype) for name in SOONER + LATER),
        ],
        compiler_params=pltpu.CompilerParams(
            collective_id=0, has_side_effects=True, vmem_limit_bytes=60 * 2**20
        ),
        name="finish",
    )(*(inputs[name] for name in FINISH_IN))


def shifted(shard, axis, by):
    count = lax.axis_size(axis)
    pairs = [(i, i + by) for i in range(count) if 0 <= i + by < count]
    return lax.ppermute(shard, axis, pairs)


def f32dot(spec, left, right):
    return jnp.einsum(spec, left, right, preferred_element_type=jnp.float32)


def low(values):
    return values.astype(jnp.bfloat16)

def finish_plain(inputs):
    query, key_ext, value_ext = inputs["q"], inputs["k"], inputs["v"]
    block_len, width = query.shape
    w_query, w_key, w_value, hot = (inputs[name] for name in ("w_query", "w_key", "w_value", "hot"))
    dquery, dkey, dvalue, drelk, drelq = attend_back(
        query, key_ext, value_ext, inputs["grad"], inputs["probs_in"], inputs["relk"], inputs["relq"]
    )
    dkey = low(f32dot("ab,nbd->nad", unit(True), low(dkey).reshape(-1, TILE, width))).reshape(-1, width)
    dvalue = low(dvalue)
    drelk = low(drelk).T
    drelq = low(drelq[:, TILE : TILE + 2 * SPAN]).T
    query_part = f32dot("em,md->ed", jnp.concatenate([inputs["x"][SPAN : SPAN + block_len], inputs["from_table"]]).T, jnp.concatenate([dquery, drelq]))
    key_part = f32dot("em,md->ed", jnp.concatenate([inputs["x"], inputs["to_table"]]).T, jnp.concatenate([dkey, drelk]))
    value_part = f32dot("em,md->ed", inputs["x"].T, dvalue)
    table = jnp.concatenate(
        [low(f32dot("md,ed->me", drelk, w_key)), low(f32dot("md,ed->me", drelq, w_query))]
    )
    table_part = f32dot("rm,me->re", hot, table)
    rest = jnp.concatenate(
        [low(query_part), low(key_part), low(value_part), inputs["output"], low(table_part)]
    )
    ext_grad = f32dot("td,ed->te", dkey, w_key) + f32dot("td,ed->te", dvalue, w_value)
    tokens_grad = (
        inputs["resid"]
        + f32dot("td,ed->te", dquery, w_query)
        + ext_grad[SPAN : SPAN + block_len]
        + shifted(low(ext_grad[:SPAN]), "seq", -1).astype(jnp.float32)
        + shifted(low(ext_grad[SPAN + block_len :]), "seq", 1).astype(jnp.float32)
    )
    both = ("rows", "seq")
    sums = [
        lax.all_gather(
            lax.psum_scatter(part, both, scatter_dimension=0, tiled=True), both, axis=0, tiled=True
        )
        for part in (inputs["outer"], inputs["inner"], rest)
    ]
    return (*sums, lax.psum(inputs["vectors"], both), low(tokens_grad))


def finish_of(inputs):
    seq_count, rows_count = lax.axis_size("seq"), lax.axis_size("rows")
    if rows_count == 2 and seq_count == 16:
        return finish(inputs, seq_count)
    return finish_plain(inputs)

def shards(
    tokens, cotangent, w_query, w_key, w_value, w_output, w_inner, w_outer, rel_table,
    mid_gain, mid_bias, end_gain, end_bias, seq_lengths, pad_mask, rel_buckets,
):
    width = tokens.shape[-1]
    inputs = {
        "tokens": tokens[0], "cotangent": cotangent[0], "rel_table": rel_table, "w_query": w_query,
        "w_key": w_key, "w_value": w_value, "w_output": w_output, "w_inner": w_inner, "w_outer": w_outer,
        "rel_buckets": rel_buckets, "mid_gain": mid_gain, "mid_bias": mid_bias, "end_gain": end_gain,
        "end_bias": end_bias, "keep": pad_mask.reshape(-1, TILE), "lengths": seq_lengths,
    }
    kept = start(inputs, lax.axis_size("seq"))
    layer_out = kept.pop("layer_out")
    inputs.update(kept, probs_in=kept["probs_out"])
    outer_w, inner_w, rest_w, norm_parts, tokens_grad = finish_of(inputs)
    query_w, key_w, value_w, output_w = (rest_w[at * width : (at + 1) * width] for at in range(4))
    table_w = rest_w[4 * width :]
    return (
        layer_out[None], tokens_grad[None],
        *(w.astype(jnp.float32) for w in (query_w, key_w, value_w, output_w, inner_w, outer_w, table_w)),
        *(norm_parts[at] for at in range(4)),
    )


def solution(mesh):
    split = P("rows", "seq", None)
    return jax.shard_map(
        shards,
        mesh=mesh,
        in_specs=(split, split) + (P(),) * 11 + (P("rows", None), P("rows", None), P()),
        out_specs=(split, split) + (P(),) * 11,
        check_vma=False,
    )
```

```python
import functools
import math

import jax
import jax.numpy as jnp
from jax import lax
from jax.experimental import pallas as pl
from jax.experimental.pallas import tpu as pltpu
from jax.sharding import PartitionSpec as P

H = 12
DH = 64
SPAN = 256
TILE = 128
REACH = 640
PAIR = 128
score_scale = 1.0 / math.sqrt(3 * DH)


def nt(left, right):
    return lax.dot_general(left, right, (((1,), (1,)), ((), ())), preferred_element_type=jnp.float32)


def nn(left, right):
    return lax.dot_general(left, right, (((1,), (0,)), ((), ())), preferred_element_type=jnp.float32)


def head_lanes(values, head):
    lane = lax.broadcasted_iota(jnp.int32, values.shape, 1)
    mine = (lane < DH) if head == 0 else (lane >= DH)
    return jnp.where(mine, values, jnp.zeros_like(values))


def unit(reverse):
    row = lax.broadcasted_iota(jnp.int32, (TILE, TILE), 0)
    col = lax.broadcasted_iota(jnp.int32, (TILE, TILE), 1)
    hit = (row + col == TILE - 1) if reverse else (row == col)
    return jnp.where(hit, 1.0, 0.0).astype(jnp.bfloat16)


def attend_back_kernel(
    q_ref, k_ref, v_ref, grad_ref, prob_ref, relk_ref, relq_ref,
    dq_ref, dk_ref, dv_ref, drelk_ref, drelq_ref, qt_ref, kt_ref,
):
    swap = unit(True)
    for source, result in ((q_ref, qt_ref), (k_ref, kt_ref)):
        for at in range(0, source.shape[0], TILE):
            flipped = nn(swap, source[pl.ds(at, TILE), :])
            result[:, pl.ds(at, TILE)] = flipped.T.astype(jnp.bfloat16)
    row = lax.broadcasted_iota(jnp.int32, (TILE, TILE), 0)
    col = lax.broadcasted_iota(jnp.int32, (TILE, TILE), 1)
    parts = REACH // TILE
    tiles = q_ref.shape[0] // TILE
    dk_ref[...] = jnp.zeros_like(dk_ref)
    dv_ref[...] = jnp.zeros_like(dv_ref)
    drelk_ref[...] = jnp.zeros_like(drelk_ref)
    drelq_ref[...] = jnp.zeros_like(drelq_ref)
    for tile in range(tiles):
        first = tile * TILE
        q_tile = q_ref[pl.ds(first, TILE), :]
        grad_tile = grad_ref[pl.ds(first, TILE), :]
        v_tile = v_ref[pl.ds(first, REACH), :]
        q_heads = [head_lanes(q_tile, head) for head in range(2)]
        grad_heads = [head_lanes(grad_tile, head) for head in range(2)]
        dq_heads = []
        lefts = [[] for _ in range(parts)]
        for head in range(2):
            lanes = pl.ds(head * DH, DH)
            probs = prob_ref[head, tile].astype(jnp.float32)
            weighted = probs * nt(v_tile, grad_heads[head])
            delta = jnp.sum(weighted, axis=0, keepdims=True)
            dscore = ((weighted - probs * delta) * score_scale).astype(jnp.bfloat16)
            turned = nt(swap, dscore)
            dband = pltpu.roll(turned, REACH - TILE + 1, 1, stride=1, stride_axis=0)
            dband = dband[:, : 2 * SPAN].astype(jnp.bfloat16)
            dq_heads.append(
                nn(turned.astype(jnp.bfloat16), k_ref[pl.ds(first, REACH), :])
                + nn(dband, relk_ref[...])
            )
            drelk_ref[lanes, :] += nn(qt_ref[lanes, pl.ds(first, TILE)], dband)
            for part in range(parts):
                flipped = nn(swap, dscore[part * TILE : (part + 1) * TILE, :])
                spun = pltpu.roll(flipped, 0, 1, stride=1, stride_axis=0)
                low = jnp.where(col >= row, spun, 0.0)
                dfrom = jnp.concatenate([low, spun - low], axis=1).astype(jnp.bfloat16)
                window = pl.ds((parts - 1 - part) * TILE, 2 * TILE)
                drelq_ref[lanes, window] += nn(kt_ref[lanes, pl.ds(first + part * TILE, TILE)], dfrom)
                lefts[part] += [flipped.astype(jnp.bfloat16), dfrom]
        dq_turned = jnp.where(col < DH, dq_heads[0], dq_heads[1]).astype(jnp.bfloat16)
        dq_ref[pl.ds(first, TILE), :] = nn(swap, dq_turned).astype(dq_ref.dtype)
        dv_ref[pl.ds(first, REACH), :] += nn(
            jnp.concatenate([prob_ref[0, tile], prob_ref[1, tile]], axis=1),
            jnp.concatenate(grad_heads, axis=0),
        )
        for part in range(parts):
            window = relq_ref[pl.ds((parts - 1 - part) * TILE, 2 * TILE), :]
            right = jnp.concatenate(
                [q_heads[0], head_lanes(window, 0), q_heads[1], head_lanes(window, 1)], axis=0
            )
            dk_ref[pl.ds(first + part * TILE, TILE), :] += nn(
                jnp.concatenate(lefts[part], axis=1), right
            )


def attend_back(query, key_ext, value_ext, grad, probs, relk, relq):
    block_len, width = query.shape
    ext_len = key_ext.shape[0]
    tiles = block_len // TILE
    pairs = width // PAIR
    table = 2 * SPAN
    cols = lambda n: pl.BlockSpec((n, PAIR), lambda p: (0, p))
    rows = lambda n: pl.BlockSpec((PAIR, n), lambda p: (p, 0))
    f32 = lambda *s: jax.ShapeDtypeStruct(s, jnp.float32)
    return pl.pallas_call(
        attend_back_kernel,
        grid=(pairs,),
        in_specs=[
            cols(block_len), cols(ext_len), cols(ext_len), cols(block_len),
            pl.BlockSpec((2, tiles, REACH, TILE), lambda p: (p, 0, 0, 0)),
            cols(table), cols(table + 2 * TILE),
        ],
        out_specs=[cols(block_len), cols(ext_len), cols(ext_len), rows(table), rows(table + 2 * TILE)],
        out_shape=[
            jax.ShapeDtypeStruct((block_len, width), jnp.bfloat16),
            f32(ext_len, width), f32(ext_len, width), f32(width, table), f32(width, table + 2 * TILE),
        ],
        scratch_shapes=[
            pltpu.VMEM((PAIR, block_len), jnp.bfloat16), pltpu.VMEM((PAIR, ext_len), jnp.bfloat16),
        ],
        compiler_params=pltpu.CompilerParams(vmem_limit_bytes=48 * 2**20),
        name="attend_back",
    )(query, key_ext, value_ext, grad, probs, relk, relq)


MESH = pl.DeviceIdType.MESH
PACK = 16


norm_eps = 1e-07
masked_score = -1e30
inverse_root_two = math.sqrt(0.5)
density_at_zero = 1.0 / math.sqrt(2.0 * math.pi)


def gelu_both(values):
    size = jnp.abs(values) * inverse_root_two
    t = 1.0 / (1.0 + 0.3275911 * size)
    poly = 1.061405429 * t - 1.453152027
    poly = poly * t + 1.421413741
    poly = poly * t - 0.284496736
    poly = poly * t + 0.254829592
    bell = jnp.exp(-size * size)
    tail = 0.5 * poly * t * bell
    share = jnp.where(values >= 0.0, 1.0 - tail, tail)
    return values * share, share + values * bell * density_at_zero


def mean_of(values):
    return jnp.mean(values, axis=-1, keepdims=True)


def by_blocks(width, body, step=256):
    def one(i, carry):
        body(pl.ds(pl.multiple_of(i * step, step), step))
        return carry

    lax.fori_loop(0, width // step, one, 0)


def column_of(row_values):
    row = lax.broadcasted_iota(jnp.int32, (TILE, TILE), 0)
    col = lax.broadcasted_iota(jnp.int32, (TILE, TILE), 1)
    return jnp.sum(jnp.where(row == col, row_values, 0), axis=1, keepdims=True)


def mask_of(r, seq_count):
    ext_len, block_len = r["bias"].shape
    place = lax.axis_index("seq")
    row_len = block_len * seq_count
    ends, end = [], 0
    for number in range(r["lengths"].shape[1]):
        end = end + r["lengths"][0, number]
        ends.append(end)

    def segment(slots):
        return sum((slots >= end).astype(jnp.int32) for end in ends)

    query = place * block_len + lax.broadcasted_iota(jnp.int32, (1, block_len), 1)
    query_segment = segment(query)
    for block in range(ext_len // TILE):
        first = place * block_len - SPAN + block * TILE
        line = lax.clamp(0, place * (block_len // TILE) - SPAN // TILE + block, row_len // TILE - 1)
        keep = column_of(r["keep"][pl.ds(line, 1), :])
        key = first + lax.broadcasted_iota(jnp.int32, (TILE, 1), 0)
        key_segment = jnp.where((key >= 0) & (key < row_len), segment(key), -1)
        apart = key - query
        seen = (key_segment == query_segment) & (jnp.abs(apart) < SPAN)
        seen = seen & ((keep == 1) | (apart == 0))
        r["bias"][pl.ds(block * TILE, TILE), :] = jnp.where(seen, 0.0, masked_score)


def attend_pair(pair, buf, r):
    eye = unit(False)
    log_two = score_scale * math.log2(math.e)
    lanes = pl.ds(pl.multiple_of(pair * PAIR, PAIR), PAIR)
    tiles = r["q"].shape[0] // TILE
    parts = REACH // TILE
    for at in range(0, r["v"].shape[0], TILE):
        r["vt"][:, pl.ds(at, TILE)] = r["v"][pl.ds(at, TILE), lanes].T
    for tile in range(tiles):
        first = tile * TILE
        q_tile = r["q"][pl.ds(first, TILE), lanes]
        outs = []
        for head in range(2):
            score_ref = r["scores"].at[head]
            q_head = head_lanes(q_tile, head)
            band = nt(q_head, r["relk"][:, lanes])
            band = jnp.concatenate([band, jnp.zeros((TILE, REACH - 2 * SPAN), jnp.float32)], axis=1)
            to_term = pltpu.roll(band, 0, 1, stride=1, stride_axis=0).astype(jnp.bfloat16)
            for part in range(parts):
                at = first + part * TILE
                k_part = r["k"][pl.ds(at, TILE), lanes]
                window = r["relq"][pl.ds((parts - 1 - part) * TILE, 2 * TILE), lanes]
                from_band = nt(head_lanes(k_part, head), window)
                from_term = pltpu.roll(from_band, TILE + 1, 1, stride=1, stride_axis=0)[:, :TILE]
                left = jnp.concatenate([k_part, eye], axis=1)
                right = jnp.concatenate([q_head, to_term[:, part * TILE : (part + 1) * TILE]], axis=1)
                score_ref[pl.ds(part * TILE, TILE), :] = (
                    nt(left, right) + from_term + r["bias"][pl.ds(at, TILE), pl.ds(first, TILE)]
                )
            scores = score_ref[...]
            top = jnp.max(scores, axis=0, keepdims=True)
            weights = jnp.exp2((scores - top) * log_two)
            total = jnp.sum(weights, axis=0, keepdims=True)
            probs = (weights * (1.0 / total)).astype(jnp.bfloat16)
            r["probs"][buf, head, tile] = probs
            outs.append(nn(r["vt"][pl.ds(head * DH, DH), pl.ds(first, REACH)], probs))
        both = jnp.concatenate(outs, axis=0)
        r["attn_t"][lanes, pl.ds(first, TILE)] = both.astype(jnp.bfloat16)
        r["attn"][pl.ds(first, TILE), lanes] = both.T.astype(jnp.bfloat16)


START_HBM = (
    "tokens", "rel_table", "w_query", "w_key", "w_value", "w_output", "w_inner", "w_outer", "cotangent",
)
START_VMEM = ("rel_buckets", "mid_gain", "mid_bias", "end_gain", "end_bias", "keep")
START_IN = START_HBM + START_VMEM + ("lengths",)
START_KEPT = (
    "x", "q", "k", "v", "relk", "relq", "to_table", "from_table", "hot", "grad", "resid",
    "active", "inner_low", "outer_low", "hidden_low", "mixed_low", "attn_t",
)
START_OUT = START_KEPT + ("probs_out", "layer_out", "vectors")
START_SCRATCH = START_KEPT + (
    "rel_table", "w_query", "w_key", "w_value", "w_output", "w_inner", "w_outer", "cotangent",
    "bias", "vt", "scores", "probs", "attn", "mixed", "hidden", "z_mid", "root_mid", "slope", "sum_grad",
    "load_sem", "keep_sem", "probs_sem", "send_sem", "recv_sem",
)


def start_kernel(seq_count, *refs):
    given = dict(zip(START_IN, refs))
    outs = dict(zip(START_OUT, refs[len(START_IN) :]))
    r = dict(zip(START_SCRATCH, refs[len(START_IN) + len(START_OUT) :]))
    r.update((name, given[name]) for name in START_VMEM + ("lengths",))
    block_len, width = r["q"].shape
    ext_len, table_len = r["x"].shape[0], r["to_table"].shape[0]
    inner_width = r["w_inner"].shape[1]
    pairs = width // PAIR
    own = pl.ds(SPAN, block_len)

    loads = {}
    for number, name in enumerate(START_HBM):
        target = r["x"].at[own] if name == "tokens" else r[name]
        loads[name] = pltpu.make_async_copy(given[name], target, r["load_sem"].at[number])
        loads[name].start()
    row, place = lax.axis_index("rows"), lax.axis_index("seq")
    before = {"rows": row, "seq": lax.rem(place + seq_count - 1, seq_count)}
    after = {"rows": row, "seq": lax.rem(place + 1, seq_count)}
    barrier = pltpu.get_barrier_semaphore()
    for device in (before, after):
        pl.semaphore_signal(barrier, inc=1, device_id=device, device_id_type=MESH)
    pl.semaphore_wait(barrier, 2)
    halos = [
        pltpu.make_async_remote_copy(
            src_ref=given["tokens"], dst_ref=r["x"].at[pl.ds(at, SPAN)], send_sem=r["send_sem"].at[number],
            recv_sem=r["recv_sem"].at[number], device_id=device, device_id_type=MESH,
        )
        for number, (at, device) in enumerate(((0, after), (SPAN + block_len, before)))
    ]
    for copy in halos:
        copy.start()

    def keep(name):
        pltpu.make_async_copy(r[name], outs[name], r["keep_sem"].at[START_KEPT.index(name)]).start()

    def low(values):
        return values.astype(jnp.bfloat16)

    place_of = lax.broadcasted_iota(jnp.int32, (table_len, table_len), 0)
    turned_bucket = pltpu.roll(r["rel_buckets"][...].reshape(1, table_len), table_len - 1, 1)
    to_pos = jnp.clip(turned_bucket + SPAN, 0, table_len - 1)
    from_pos = jnp.clip(SPAN - turned_bucket, 0, table_len - 1)
    r["hot"][:, pl.ds(table_len, table_len)] = low(jnp.where(place_of == from_pos, 1.0, 0.0))
    to_turned = low(jnp.where(place_of == to_pos, 1.0, 0.0))
    for at in range(0, table_len, TILE):
        r["hot"][:, pl.ds(at, TILE)] = low(
            nn(to_turned[:, table_len - TILE - at : table_len - at], unit(True))
        )
    keep("hot")
    mask_of(r, seq_count)
    loads["rel_table"].wait()
    for number, name in enumerate(("to", "from")):
        hot = r["hot"][:, pl.ds(number * table_len, table_len)].T

        def table_cols(cols, hot=hot, name=name):
            r[name + "_table"][:, cols] = low(nn(hot, r["rel_table"][:, cols]))

        by_blocks(width, table_cols)
        keep(name + "_table")
    loads["w_query"].wait()
    loads["tokens"].wait()
    r["relq"][pl.ds(0, TILE), :] = jnp.zeros((TILE, width), jnp.bfloat16)
    r["relq"][pl.ds(TILE + table_len, TILE), :] = jnp.zeros((TILE, width), jnp.bfloat16)

    def query_cols(cols):
        r["q"][:, cols] = low(nn(r["x"][own, :], r["w_query"][:, cols]))
        r["relq"][pl.ds(TILE, table_len), cols] = low(nn(r["from_table"][...], r["w_query"][:, cols]))

    by_blocks(width, query_cols)
    keep("q")
    keep("relq")
    loads["w_key"].wait()

    def relk_cols(cols):
        r["relk"][:, cols] = low(nn(r["to_table"][...], r["w_key"][:, cols]))

    by_blocks(width, relk_cols)
    keep("relk")
    loads["w_value"].wait()
    for copy in halos:
        copy.wait()
    keep("x")

    def pair_cols(cols):
        r["k"][:, cols] = low(nn(r["x"][...], r["w_key"][:, cols]))
        r["v"][:, cols] = low(nn(r["x"][...], r["w_value"][:, cols]))

    by_blocks(width, pair_cols)
    keep("k")
    keep("v")

    def probs_copy(pair, buf):
        return pltpu.make_async_copy(
            r["probs"].at[buf], outs["probs_out"].at[pl.ds(2 * pair, 2)], r["probs_sem"].at[buf]
        )

    def one_pair(pair, carry):
        buf = lax.rem(pair, 2)

        @pl.when(pair >= 2)
        def _():
            probs_copy(pair - 2, buf).wait()

        attend_pair(pair, buf, r)
        probs_copy(pair, buf).start()
        return carry

    lax.fori_loop(0, pairs, one_pair, 0)

    keep("attn_t")
    for name in ("w_output", "w_inner", "w_outer", "cotangent"):
        loads[name].wait()

    def mixed_cols(cols):
        r["mixed"][:, cols] = nn(r["attn"][...], r["w_output"][:, cols])

    by_blocks(width, mixed_cols)
    high = 64
    mid_gain, mid_bias, end_gain, end_bias = (
        r[name][...].reshape(1, width) for name in ("mid_gain", "mid_bias", "end_gain", "end_bias")
    )

    def mid_rows(rows):
        mine = pl.ds(pl.multiple_of(SPAN + rows.start, high), high)
        values = r["x"][mine, :].astype(jnp.float32) + r["mixed"][rows, :]
        centre = values - mean_of(values)
        root = lax.rsqrt(mean_of(centre * centre) + norm_eps)
        z = centre * root
        hidden = z * mid_gain + mid_bias
        r["z_mid"][rows, :] = z
        r["root_mid"][rows, :] = jnp.broadcast_to(root, (high, TILE))
        r["hidden"][rows, :] = hidden
        r["hidden_low"][rows, :] = low(hidden)

    by_blocks(block_len, mid_rows, high)
    keep("hidden_low")

    def active_cols(cols):
        active, slope = gelu_both(nn(r["hidden_low"][...], r["w_inner"][:, cols]))
        r["active"][:, cols] = low(active)
        r["slope"][:, cols] = low(slope)

    by_blocks(inner_width, active_cols)
    keep("active")

    def outer_cols(cols):
        r["mixed"][:, cols] = nn(r["active"][...], r["w_outer"][:, cols])

    by_blocks(width, outer_cols)
    outs["vectors"][...] = jnp.zeros_like(outs["vectors"])

    def end_rows(rows):
        values = r["hidden"][rows, :] + r["mixed"][rows, :]
        centre = values - mean_of(values)
        root = lax.rsqrt(mean_of(centre * centre) + norm_eps)
        z = centre * root
        outs["layer_out"][rows, :] = low(z * end_gain + end_bias)
        cotangent = r["cotangent"][rows, :].astype(jnp.float32)
        outs["vectors"][pl.ds(2, 1), :] += jnp.sum(cotangent * z, axis=0, keepdims=True)
        outs["vectors"][pl.ds(3, 1), :] += jnp.sum(cotangent, axis=0, keepdims=True)
        grad = cotangent * end_gain
        sum_grad = root * (grad - mean_of(grad) - z * mean_of(grad * z))
        r["sum_grad"][rows, :] = sum_grad
        r["outer_low"][rows, :] = low(sum_grad)

    by_blocks(block_len, end_rows, high)
    keep("outer_low")

    def inner_cols(cols):
        grad = nt(r["outer_low"][...], r["w_outer"][cols, :])
        r["inner_low"][:, cols] = low(grad * r["slope"][:, cols].astype(jnp.float32))

    by_blocks(inner_width, inner_cols)
    keep("inner_low")

    def hidden_cols(cols):
        r["mixed"][:, cols] = r["sum_grad"][:, cols] + nt(r["inner_low"][...], r["w_inner"][cols, :])

    by_blocks(width, hidden_cols)

    def resid_rows(rows):
        hidden_grad, z = r["mixed"][rows, :], r["z_mid"][rows, :]
        outs["vectors"][pl.ds(0, 1), :] += jnp.sum(hidden_grad * z, axis=0, keepdims=True)
        outs["vectors"][pl.ds(1, 1), :] += jnp.sum(hidden_grad, axis=0, keepdims=True)
        grad = hidden_grad * mid_gain
        root = r["root_mid"][rows, pl.ds(0, 1)]
        resid = root * (grad - mean_of(grad) - z * mean_of(grad * z))
        r["resid"][rows, :] = resid
        r["mixed_low"][rows, :] = low(resid)

    by_blocks(block_len, resid_rows, high)
    keep("resid")
    keep("mixed_low")

    def grad_cols(cols):
        r["grad"][:, cols] = low(nt(r["mixed_low"][...], r["w_output"][cols, :]))

    by_blocks(width, grad_cols)
    keep("grad")
    for pair in (pairs - 2, pairs - 1):
        probs_copy(pair, pair % 2).wait()
    for number, name in enumerate(START_KEPT):
        pltpu.make_async_copy(r[name], outs[name], r["keep_sem"].at[number]).wait()


def start(inputs, seq_count):
    block_len, width = inputs["tokens"].shape
    table_len = inputs["rel_table"].shape[0]
    inner_width = inputs["w_inner"].shape[1]
    ext_len = block_len + 2 * SPAN
    tiles = block_len // TILE
    heads = 2 * (width // PAIR)
    sizes = {
        "x": (ext_len, width), "q": (block_len, width), "k": (ext_len, width), "v": (ext_len, width),
        "relk": (table_len, width), "relq": (table_len + 2 * TILE, width), "to_table": (table_len, width),
        "from_table": (table_len, width), "hot": (table_len, 2 * table_len), "grad": (block_len, width),
        "resid": (block_len, width), "active": (block_len, inner_width),
        "inner_low": (block_len, inner_width), "outer_low": (block_len, width),
        "hidden_low": (block_len, width), "mixed_low": (block_len, width), "attn_t": (width, block_len),
    }
    kinds = {name: jnp.float32 if name == "resid" else jnp.bfloat16 for name in START_KEPT}
    bf = lambda *shape: pltpu.VMEM(shape, jnp.bfloat16)
    f32 = lambda *shape: pltpu.VMEM(shape, jnp.float32)
    dma = pltpu.SemaphoreType.DMA
    any_spec = pl.BlockSpec(memory_space=pl.ANY)
    vmem = pl.BlockSpec(memory_space=pltpu.VMEM)
    smem = pl.BlockSpec(memory_space=pltpu.SMEM)
    values = pl.pallas_call(
        functools.partial(start_kernel, seq_count),
        in_specs=[any_spec] * len(START_HBM) + [vmem] * len(START_VMEM) + [smem],
        out_specs=[any_spec] * (len(START_KEPT) + 1) + [vmem] * 2,
        out_shape=[
            *(jax.ShapeDtypeStruct(sizes[name], kinds[name]) for name in START_KEPT),
            jax.ShapeDtypeStruct((heads, tiles, REACH, TILE), jnp.bfloat16),
            jax.ShapeDtypeStruct((block_len, width), jnp.bfloat16),
            jax.ShapeDtypeStruct((8, width), jnp.float32),
        ],
        scratch_shapes=[
            *(pltpu.VMEM(sizes[name], kinds[name]) for name in START_KEPT),
            *(pltpu.VMEM(inputs[name].shape, inputs[name].dtype) for name in START_HBM[1:]),
            f32(ext_len, block_len), bf(PAIR, ext_len), f32(2, REACH, TILE), bf(2, 2, tiles, REACH, TILE),
            bf(block_len, width), f32(block_len, width), f32(block_len, width), f32(block_len, width),
            f32(block_len, TILE), bf(block_len, inner_width), f32(block_len, width),
            dma((len(START_HBM),)), dma((len(START_KEPT),)), dma((2,)), dma((2,)), dma((2,)),
        ],
        compiler_params=pltpu.CompilerParams(
            collective_id=1, has_side_effects=True, vmem_limit_bytes=60 * 2**20
        ),
        name="start",
    )(*(inputs[name] for name in START_IN))
    return dict(zip(START_OUT, values))


class Line:
    def __init__(self, side, row_step, seq_step):
        self.side = side
        row, place = lax.axis_index("rows"), lax.axis_index("seq")
        away = 1 - 2 * side
        self.device = {"rows": row + away * row_step, "seq": place + away * seq_step}


def lines_of():
    row, place = lax.axis_index("rows"), lax.axis_index("seq")
    first, second, third, fourth = (place // step % 2 for step in (1, 2, 4, 8))
    core = Line(row, 1, 0)
    near = Line(first + row * (second - first), 0, 1 + row)
    cross = Line(second + row * (first - second), 0, 2 - row)
    low_z, high_z = Line(third, 0, 4), Line(fourth, 0, 8)
    return (core, near, cross, low_z, high_z), (core, low_z, high_z, near, cross)


def add_rows(left, right, out):
    rows = out.shape[0]
    step = next(s for s in (48, 32, PACK) if rows % s == 0)

    def body(i, carry):
        here = pl.ds(pl.multiple_of(i * step, PACK), step)
        out[here, :] = left[here, :] + right[here, :]
        return carry

    lax.fori_loop(0, rows // step, body, 0)


class Chunk:
    def __init__(self, index, which, start, half, base, width, z_first):
        self.index, self.which, self.start, self.half = index, which, start, half
        self.base, self.width, self.z_first = base, width, z_first

    def out(self, refs, side):
        if self.which == "inner":
            col = (self.start // self.width + side) * self.width
            return refs["inner"].at[:, pl.ds(pl.multiple_of(col, PAIR), self.width)]
        first = pl.multiple_of(self.start + side * self.half, PACK)
        return refs[self.which].at[pl.ds(first, self.half)]


def chunks_of(spec, unit, width):
    chunks, starts, base = [], {}, 0
    for which, units, z_first in spec:
        start = starts.get(which, 0)
        chunks.append(Chunk(len(chunks), which, start, units * unit // 2, base, width, z_first))
        starts[which] = start + units * unit
        base += units * unit
    return chunks, base


class Sum:
    phases = 5
    last = 2 * phases

    def __init__(self, chunks, outs, work, recv, own_sem, send_sem, recv_sem):
        self.chunks, self.outs, self.work, self.recv = chunks, outs, work, recv
        self.own_sem, self.send_sem, self.recv_sem = own_sem, send_sem, recv_sem
        self.row = lax.axis_index("rows")
        self.plane_first, self.z_first = lines_of()

    def greet(self, more):
        barrier = pltpu.get_barrier_semaphore()
        devices = [line.device for line in self.plane_first] + more
        for device in devices:
            pl.semaphore_signal(barrier, inc=1, device_id=device, device_id_type=MESH)
        pl.semaphore_wait(barrier, len(devices))

    def lines(self, chunk):
        return self.z_first if chunk.z_first else self.plane_first

    def offset(self, chunk, phase):
        at, rows = 0, chunk.half
        for line in self.lines(chunk)[1 : phase + 1]:
            rows //= 2
            at = at + line.side * rows
        return at

    def working(self, chunk, at, rows):
        return self.work.at[pl.ds(pl.multiple_of(chunk.base + self.row * chunk.half + at, PACK), rows)]

    def received(self, chunk, phase):
        at = chunk.base + sum(chunk.half >> p for p in range(phase))
        return self.recv.at[pl.ds(at, chunk.half >> phase)]

    def summed(self, chunk, phase):
        at = pl.multiple_of(chunk.base + self.offset(chunk, phase), PACK)
        return self.recv.at[pl.ds(at, chunk.half >> phase)]

    def copies(self, chunk, stage):
        gather = stage >= self.phases
        phase = self.last - 1 - stage if gather else stage
        line, rows = self.lines(chunk)[phase], chunk.half >> phase
        local = None
        if gather:
            source = target = self.summed(chunk, phase)
            if phase == 0:
                target = chunk.out(self.outs, self.row)
                local = (source, target)
        else:
            target = self.received(chunk, phase)
            if phase == 0:
                other = chunk.base + (1 - self.row) * chunk.half
                source = self.work.at[pl.ds(pl.multiple_of(other, PACK), rows)]
            else:
                source = self.working(chunk, self.offset(chunk, phase - 1) + (1 - line.side) * rows, rows)
        sem = chunk.index * self.last + stage
        copies = [
            pltpu.make_async_remote_copy(
                src_ref=source, dst_ref=target, send_sem=self.send_sem.at[sem],
                recv_sem=self.recv_sem.at[sem], device_id=line.device, device_id_type=MESH,
            )
        ]
        if local is not None:
            copies.append(pltpu.make_async_copy(*local, self.own_sem.at[chunk.index]))
        return copies

    def step(self, c, stage):
        chunk = self.chunks[c]
        if stage > 0:
            for copy in self.copies(chunk, stage - 1):
                copy.wait()
        if 0 < stage <= self.phases:
            phase = stage - 1
            mine = self.working(chunk, self.offset(chunk, phase), chunk.half >> phase)
            add_rows(mine, self.received(chunk, phase), self.summed(chunk, phase) if stage == self.phases else mine)
        if stage < self.last:
            for copy in self.copies(chunk, stage):
                copy.start()


class VectorSum:
    def __init__(self, lines, acc, recv, send_sem, recv_sem):
        self.lines, self.acc, self.recv, self.send_sem, self.recv_sem = lines, acc, recv, send_sem, recv_sem

    def copy(self, phase):
        return pltpu.make_async_remote_copy(
            src_ref=self.acc.at[phase], dst_ref=self.recv.at[phase], send_sem=self.send_sem.at[phase],
            recv_sem=self.recv_sem.at[phase], device_id=self.lines[phase].device, device_id_type=MESH,
        )

    def start(self, phase):
        self.copy(phase).start()

    def end(self, phase):
        self.copy(phase).wait()
        self.acc[phase + 1] = self.acc[phase] + self.recv[phase]


def back_of_pair(pair, buf, r):
    swap = unit(True)
    lanes_at = pl.multiple_of(pair * PAIR, PAIR)
    lanes_here = pl.ds(lanes_at, PAIR)
    row = lax.broadcasted_iota(jnp.int32, (TILE, TILE), 0)
    col = lax.broadcasted_iota(jnp.int32, (TILE, TILE), 1)
    parts = REACH // TILE
    block_len, ext_len = r["q"].shape[0], r["k"].shape[0]
    tiles = block_len // TILE
    qt_ref, kt_ref, dk_ref, dv_ref, drelk_ref, drelq_ref = (
        r[name] for name in ("qt", "kt", "dk_pair", "dv_pair", "drelk_t", "drelq_t")
    )
    for source, result in ((r["q"], qt_ref), (r["k"], kt_ref)):
        for at in range(0, source.shape[0], TILE):
            flipped = nn(swap, source[pl.ds(at, TILE), lanes_here])
            result[:, pl.ds(at, TILE)] = flipped.T.astype(jnp.bfloat16)
    dk_ref[...] = jnp.zeros_like(dk_ref)
    dv_ref[...] = jnp.zeros_like(dv_ref)
    drelk_ref[...] = jnp.zeros_like(drelk_ref)
    drelq_ref[...] = jnp.zeros_like(drelq_ref)
    for tile in range(tiles):
        first = tile * TILE
        q_tile = r["q"][pl.ds(first, TILE), lanes_here]
        grad_tile = r["grad"][pl.ds(first, TILE), lanes_here]
        v_tile = r["v"][pl.ds(first, REACH), lanes_here]
        q_heads = [head_lanes(q_tile, head) for head in range(2)]
        grad_heads = [head_lanes(grad_tile, head) for head in range(2)]
        dq_heads = []
        lefts = [[] for _ in range(parts)]
        for head in range(2):
            lanes = pl.ds(head * DH, DH)
            probs = r["probs"][buf, head, tile].astype(jnp.float32)
            weighted = probs * nt(v_tile, grad_heads[head])
            delta = jnp.sum(weighted, axis=0, keepdims=True)
            dscore = ((weighted - probs * delta) * score_scale).astype(jnp.bfloat16)
            turned = nt(swap, dscore)
            dband = pltpu.roll(turned, REACH - TILE + 1, 1, stride=1, stride_axis=0)
            dband = dband[:, : 2 * SPAN].astype(jnp.bfloat16)
            dq_heads.append(
                nn(turned.astype(jnp.bfloat16), r["k"][pl.ds(first, REACH), lanes_here])
                + nn(dband, r["relk"][:, lanes_here])
            )
            drelk_ref[lanes, :] += nn(qt_ref[lanes, pl.ds(first, TILE)], dband)
            for part in range(parts):
                flipped = nn(swap, dscore[part * TILE : (part + 1) * TILE, :])
                spun = pltpu.roll(flipped, 0, 1, stride=1, stride_axis=0)
                near = jnp.where(col >= row, spun, 0.0)
                dfrom = jnp.concatenate([near, spun - near], axis=1).astype(jnp.bfloat16)
                window = pl.ds((parts - 1 - part) * TILE, 2 * TILE)
                drelq_ref[lanes, window] += nn(kt_ref[lanes, pl.ds(first + part * TILE, TILE)], dfrom)
                lefts[part] += [flipped.astype(jnp.bfloat16), dfrom]
        dq_turned = jnp.where(col < DH, dq_heads[0], dq_heads[1]).astype(jnp.bfloat16)
        r["dq"][pl.ds(first, TILE), lanes_here] = nn(swap, dq_turned).astype(jnp.bfloat16)
        dv_ref[pl.ds(first, REACH), :] += nn(
            jnp.concatenate([r["probs"][buf, 0, tile], r["probs"][buf, 1, tile]], axis=1),
            jnp.concatenate(grad_heads, axis=0),
        )
        for part in range(parts):
            window = r["relq"][pl.ds((parts - 1 - part) * TILE, 2 * TILE), lanes_here]
            right = jnp.concatenate(
                [q_heads[0], head_lanes(window, 0), q_heads[1], head_lanes(window, 1)], axis=0
            )
            dk_ref[pl.ds(first + part * TILE, TILE), :] += nn(
                jnp.concatenate(lefts[part], axis=1), right
            )
    r["dv"][:, lanes_here] = dv_ref[...].astype(jnp.bfloat16)
    for at in range(0, ext_len, TILE):
        r["dk"][pl.ds(at, TILE), lanes_here] = nn(
            swap, dk_ref[pl.ds(at, TILE), :].astype(jnp.bfloat16)
        ).astype(jnp.bfloat16)
    r["dk"][pl.ds(ext_len, 2 * SPAN), lanes_here] = drelk_ref[...].T.astype(jnp.bfloat16)
    r["dq"][pl.ds(block_len, 2 * SPAN), lanes_here] = (
        drelq_ref[:, pl.ds(TILE, 2 * SPAN)].T.astype(jnp.bfloat16)
    )


SOONEST = ("outer_low", "hidden_low", "mixed_low", "attn_t")
SOONER = ("q", "k", "v", "grad", "relk", "relq")
LATER = ("x", "to_table", "from_table", "w_query", "w_key", "w_value", "hot", "resid")
FINISH_IN = ("active", "inner_low") + SOONEST + SOONER + LATER + ("vectors", "probs_out")
FINISH_OUT = ("outer", "inner", "rest", "vectors", "tokens_grad")
FINISH_SCRATCH = (
    "probs", "qt", "kt", "dk_pair", "dv_pair", "drelk_t", "drelq_t", "wide", "dv", "work", "table",
    "xt_query", "xt_key", "hidden_t", "halo", "halo_got", "own_grad", "recv", "vec_acc", "vec_recv", "own_sem",
    "send_sem", "recv_sem", "vec_send", "vec_got", "probs_sem", "halo_send", "halo_recv", "load_sem", "wide_sem",
)


def finish_kernel(chunks, schedule, seq_count, *refs):
    given = dict(zip(FINISH_IN, refs))
    outs = dict(zip(FINISH_OUT, refs[len(FINISH_IN) :]))
    scratch = refs[len(FINISH_IN) + len(FINISH_OUT) :]
    r = dict(zip(FINISH_SCRATCH, scratch))
    block_len, width = given["q"].shape
    ext_len = given["k"].shape[0]
    folds = given["active"].shape[1] // width
    wide_loads = {}
    for number, name in enumerate(("active", "inner_low")):
        wide_loads[name] = [
            pltpu.make_async_copy(
                given[name].at[:, pl.ds(fold * width, width)],
                r["wide"].at[pl.ds((number * folds + fold) * block_len, block_len)],
                r["wide_sem"].at[number * folds + fold],
            )
            for fold in range(folds)
        ]
    r["dk"] = r["wide"].at[pl.ds(0, ext_len + 2 * SPAN)]
    r["dq"] = r["wide"].at[pl.ds(ext_len + 2 * SPAN, block_len + 2 * SPAN)]
    loads = {}
    for number, (name, held) in enumerate(
        zip(SOONEST + SOONER + LATER, scratch[len(FINISH_SCRATCH) :])
    ):
        loads[name] = pltpu.make_async_copy(given[name], held, r["load_sem"].at[number])
        r[name] = held
    loads["outer_low"].start()
    for copy in wide_loads["active"] + wide_loads["inner_low"]:
        copy.start()
    for name in SOONEST[1:] + SOONER + LATER:
        loads[name].start()
    pairs = width // PAIR
    total = Sum(chunks, outs, r["work"], r["recv"], r["own_sem"], r["send_sem"], r["recv_sem"])
    row, place = lax.axis_index("rows"), lax.axis_index("seq")
    before = {"rows": row, "seq": lax.rem(place + seq_count - 1, seq_count)}
    after = {"rows": row, "seq": lax.rem(place + 1, seq_count)}
    total.greet([before, after])
    vec = VectorSum(total.plane_first, r["vec_acc"], r["vec_recv"], r["vec_send"], r["vec_got"])
    vec.acc[0] = given["vectors"][...]

    def probs_copy(pair, buf):
        return pltpu.make_async_copy(
            given["probs_out"].at[pl.ds(2 * pair, 2)], r["probs"].at[buf], r["probs_sem"].at[buf]
        )

    probs_copy(0, 0).start()
    inner_base = folds * width
    rest_base = 2 * folds * width

    def outer_piece(chunk):
        def body(i, carry):
            at = pl.multiple_of(chunk.start + i * 256, 256)
            fold, col = at // width, pl.multiple_of(at % width, 256)
            active = r["wide"][pl.ds(pl.multiple_of(fold * block_len, block_len), block_len), pl.ds(col, 256)]
            r["work"][pl.ds(at, 256), :] = nn(active.T, r["outer_low"][...]).astype(jnp.bfloat16)
            return carry

        lax.fori_loop(0, 2 * chunk.half // 256, body, 0)

    def inner_piece(chunk):
        for fold in range(chunk.start // width, (chunk.start + 2 * chunk.half) // width):

            def inner_cols(cols, fold=fold):
                inner_low = r["wide"][pl.ds((folds + fold) * block_len, block_len), cols]
                r["work"][pl.ds(inner_base + fold * width, width), cols] = nn(
                    r["hidden_t"][...], inner_low
                ).astype(jnp.bfloat16)

            by_blocks(width, inner_cols)

    def output_piece():
        def output_cols(cols):
            r["work"][pl.ds(rest_base, width), cols] = nn(r["attn_t"][...], r["mixed_low"][:, cols]).astype(
                jnp.bfloat16
            )

        by_blocks(width, output_cols)

    def between(pair):
        if 0 < pair <= total.phases:
            vec.end(pair - 1)
        if pair < total.phases:
            vec.start(pair)
        for c, stage in later[pair]:
            total.step(c, stage)

    def one_pair(pair, carry):
        buf = lax.rem(pair, 2)

        @pl.when(pair + 1 < pairs)
        def _():
            probs_copy(pair + 1, 1 - buf).start()

        probs_copy(pair, buf).wait()
        back_of_pair(pair, buf, r)
        for at in range(pairs):
            pl.when(pair == at)(functools.partial(between, at))
        return carry

    def turn_tokens(rows):
        r["xt_key"][:, rows] = r["x"][rows, :].T

    def turn_tables(rows):
        r["xt_key"][:, pl.ds(pl.multiple_of(ext_len + rows.start, PAIR), rows.size)] = r["to_table"][rows, :].T
        r["xt_query"][:, pl.ds(pl.multiple_of(block_len + rows.start, PAIR), rows.size)] = (
            r["from_table"][rows, :].T
        )

    def turn():
        by_blocks(ext_len, turn_tokens)
        by_blocks(2 * SPAN, turn_tables)
        r["xt_query"][:, pl.ds(0, block_len)] = r["xt_key"][:, pl.ds(SPAN, block_len)]

    def query_cols(cols):
        r["work"][pl.ds(rest_base + width, width), cols] = nn(r["xt_query"][...], r["dq"][:, cols]).astype(jnp.bfloat16)

    def key_cols(cols):
        r["work"][pl.ds(rest_base + 2 * width, width), cols] = nn(
            r["xt_key"][...], r["dk"][:, cols]
        ).astype(jnp.bfloat16)

    def value_cols(cols):
        r["work"][pl.ds(rest_base + 3 * width, width), cols] = nn(
            r["xt_key"][:, pl.ds(0, ext_len)], r["dv"][:, cols]
        ).astype(jnp.bfloat16)

    def table_cols(cols):
        r["table"][pl.ds(0, 2 * SPAN), cols] = nt(
            r["dk"][pl.ds(ext_len, 2 * SPAN), :], r["w_key"][cols, :]
        ).astype(jnp.bfloat16)
        r["table"][pl.ds(2 * SPAN, 2 * SPAN), cols] = nt(
            r["dq"][pl.ds(block_len, 2 * SPAN), :], r["w_query"][cols, :]
        ).astype(jnp.bfloat16)

    def bucket_cols(cols):
        r["work"][pl.ds(rest_base + 4 * width, 2 * SPAN), cols] = nn(
            r["hot"][...], r["table"][:, cols]
        ).astype(jnp.bfloat16)

    def halo_cols(cols):
        for at in (0, ext_len - SPAN):
            rows = pl.ds(at, SPAN)
            grad = nt(r["dk"][rows, :], r["w_key"][cols, :]) + nt(r["dv"][rows, :], r["w_value"][cols, :])
            r["halo"][rows, cols] = grad.astype(jnp.bfloat16)

    def own_cols(cols):
        own, mid = pl.ds(0, block_len), pl.ds(SPAN, block_len)
        r["own_grad"][:, cols] = (
            r["resid"][:, cols]
            + nt(r["dq"][own, :], r["w_query"][cols, :])
            + nt(r["dk"][mid, :], r["w_key"][cols, :])
            + nt(r["dv"][mid, :], r["w_value"][cols, :])
        )

    halos = [
        pltpu.make_async_remote_copy(
            src_ref=r["halo"].at[pl.ds(at, SPAN)], dst_ref=r["halo_got"].at[number],
            send_sem=r["halo_send"].at[number], recv_sem=r["halo_recv"].at[number],
            device_id=device, device_id_type=MESH,
        )
        for number, (at, device) in enumerate(((0, before), (ext_len - SPAN, after)))
    ]

    early = [chunk for chunk in chunks if chunk.which != "rest"]
    later = schedule[len(early) + 2 :]

    def advance(steps):
        for c, stage in steps:
            total.step(c, stage)

    advance(schedule[0])
    for name in ("outer_low", "hidden_low"):
        loads[name].wait()
    for copy in wide_loads["active"]:
        copy.wait()
    r["hidden_t"][...] = r["hidden_low"][...].T
    fresh = True
    for number, chunk in enumerate(early):
        if chunk.which == "inner" and fresh:
            for copy in wide_loads["inner_low"]:
                copy.wait()
            fresh = False
        (inner_piece if chunk.which == "inner" else outer_piece)(chunk)
        advance(schedule[number + 1])
    for name in ("mixed_low", "attn_t"):
        loads[name].wait()
    output_piece()
    advance(schedule[len(early) + 1])
    for name in SOONER:
        loads[name].wait()
    lax.fori_loop(0, pairs, one_pair, 0)
    for name in LATER:
        loads[name].wait()
    turn()
    pieces = ((query_cols,), (key_cols,), (value_cols,), (table_cols, bucket_cols), (halo_cols,), (own_cols,))
    for piece, steps in zip(pieces, later[pairs:]):
        for body in piece:
            by_blocks(width, body)
        if piece[0] is halo_cols:
            for copy in halos:
                copy.start()
        advance(steps)
    for copy in halos:
        copy.wait()
    grad = r["own_grad"][...]
    for number in range(2):
        grad = grad + r["halo_got"][number].astype(jnp.float32)
    outs["tokens_grad"][...] = grad.astype(jnp.bfloat16)
    outs["vectors"][...] = vec.acc[total.phases]


CHUNKS = (
    ("outer", 2, False),
    ("outer", 2, False),
    ("outer", 2, True),
    ("inner", 3, False),
    ("inner", 3, False),
    ("rest", 1, True),
    ("rest", 2, False),
    ("rest", 1, True),
    ("rest", 1, False),
    ("rest", 1, True),
    ("rest", 1, False),
)
SCHEDULE = (
    (),
    ((0, 0),),
    ((1, 0),),
    ((0, 1), (2, 0),),
    ((3, 0),),
    (),
    ((2, 1), (4, 0), (0, 2), (5, 0), (3, 1),),
    ((0, 3), (1, 1), (5, 1),),
    ((0, 4), (3, 2),),
    ((1, 2), (0, 5), (3, 3), (4, 1), (5, 2),),
    ((3, 4), (0, 6), (1, 3),),
    ((4, 2), (3, 5), (2, 2), (0, 7),),
    ((4, 3),),
    ((0, 8), (6, 0), (3, 6),),
    ((7, 0), (1, 4), (6, 1), (4, 4), (7, 1),),
    ((1, 5), (8, 0), (3, 7), (9, 0), (5, 3), (2, 3), (9, 1), (6, 2),),
    ((8, 1), (10, 0), (5, 4), (7, 2), (4, 5), (10, 1), (1, 6), (6, 3), (8, 2), (5, 5), (2, 4), (7, 3), (10, 2), (3, 8), (8, 3), (9, 2), (7, 4), (6, 4), (10, 3), (8, 4), (5, 6), (0, 9), (2, 5), (1, 7), (9, 3), (4, 6), (10, 4), (6, 5), (2, 6), (5, 7), (7, 5), (1, 8), (9, 4), (6, 6), (7, 6), (4, 7), (8, 5), (2, 7), (8, 6), (9, 5), (10, 5), (1, 9), (6, 7), (0, 10), (5, 8), (9, 6), (4, 8), (8, 7), (9, 7), (6, 8), (1, 10), (10, 6), (3, 9), (5, 9), (7, 7), (2, 8), (9, 8), (10, 7), (8, 8), (7, 8), (10, 8), (5, 10),),
    ((6, 9), (10, 9), (6, 10), (10, 10), (2, 9), (2, 10), (8, 9), (8, 10), (4, 9), (9, 9), (4, 10), (7, 9),),
    ((7, 10), (3, 10), (9, 10),),
)

def finish(inputs, seq_count):
    width = inputs["q"].shape[1]
    block_len, ext_len = inputs["q"].shape[0], inputs["k"].shape[0]
    inner_width = inputs["active"].shape[1]
    chunks, rows = chunks_of(CHUNKS, PACK * 2 * seq_count, width)
    sems = len(chunks) * Sum.last
    rest_rows = rows - 2 * inner_width
    bf = lambda *shape: pltpu.VMEM(shape, jnp.bfloat16)
    f32 = lambda *shape: pltpu.VMEM(shape, jnp.float32)
    dma = pltpu.SemaphoreType.DMA
    vec_shape = inputs["vectors"].shape
    any_spec = pl.BlockSpec(memory_space=pl.ANY)
    vmem = pl.BlockSpec(memory_space=pltpu.VMEM)
    tiles = block_len // TILE
    held = SOONEST + SOONER + LATER
    return pl.pallas_call(
        functools.partial(finish_kernel, chunks, SCHEDULE, seq_count),
        in_specs=[vmem if name == "vectors" else any_spec for name in FINISH_IN],
        out_specs=[any_spec] * 3 + [vmem] * 2,
        out_shape=[
            jax.ShapeDtypeStruct((inner_width, width), jnp.bfloat16),
            jax.ShapeDtypeStruct((width, inner_width), jnp.bfloat16),
            jax.ShapeDtypeStruct((rest_rows, width), jnp.bfloat16),
            jax.ShapeDtypeStruct(vec_shape, jnp.float32),
            jax.ShapeDtypeStruct((block_len, width), jnp.bfloat16),
        ],
        scratch_shapes=[
            bf(2, 2, tiles, REACH, TILE), bf(PAIR, block_len), bf(PAIR, ext_len),
            f32(ext_len, PAIR), f32(ext_len, PAIR), f32(PAIR, 2 * SPAN), f32(PAIR, 2 * SPAN + 2 * TILE),
            bf(2 * block_len * (inner_width // width), width), bf(ext_len, width), bf(rows, width),
            bf(4 * SPAN, width), bf(width, block_len + 2 * SPAN), bf(width, ext_len + 2 * SPAN),
            bf(width, block_len), bf(ext_len, width), bf(2, SPAN, width), f32(block_len, width), bf(rows, width),
            f32(Sum.phases + 1, *vec_shape), f32(Sum.phases, *vec_shape),
            dma((len(chunks),)), dma((sems,)), dma((sems,)), dma((Sum.phases,)), dma((Sum.phases,)),
            dma((2,)), dma((2,)), dma((2,)), dma((len(held),)), dma((2 * (inner_width // width),)),
            *(pltpu.VMEM(inputs[name].shape, inputs[name].dtype) for name in held),
        ],
        compiler_params=pltpu.CompilerParams(
            collective_id=0, has_side_effects=True, vmem_limit_bytes=61 * 2**20
        ),
        name="finish",
    )(*(inputs[name] for name in FINISH_IN))


def shifted(shard, axis, by):
    count = lax.axis_size(axis)
    pairs = [(i, i + by) for i in range(count) if 0 <= i + by < count]
    return lax.ppermute(shard, axis, pairs)


def f32dot(spec, left, right):
    return jnp.einsum(spec, left, right, preferred_element_type=jnp.float32)


def low(values):
    return values.astype(jnp.bfloat16)

def finish_plain(inputs):
    query, key_ext, value_ext = inputs["q"], inputs["k"], inputs["v"]
    block_len, width = query.shape
    w_query, w_key, w_value, hot = (inputs[name] for name in ("w_query", "w_key", "w_value", "hot"))
    dquery, dkey, dvalue, drelk, drelq = attend_back(
        query, key_ext, value_ext, inputs["grad"], inputs["probs_out"], inputs["relk"], inputs["relq"]
    )
    dkey = low(f32dot("ab,nbd->nad", unit(True), low(dkey).reshape(-1, TILE, width))).reshape(-1, width)
    dvalue = low(dvalue)
    drelk = low(drelk).T
    drelq = low(drelq[:, TILE : TILE + 2 * SPAN]).T
    query_part = f32dot("em,md->ed", jnp.concatenate([inputs["x"][SPAN : SPAN + block_len], inputs["from_table"]]).T, jnp.concatenate([dquery, drelq]))
    key_part = f32dot("em,md->ed", jnp.concatenate([inputs["x"], inputs["to_table"]]).T, jnp.concatenate([dkey, drelk]))
    value_part = f32dot("em,md->ed", inputs["x"].T, dvalue)
    table = jnp.concatenate(
        [low(f32dot("md,ed->me", drelk, w_key)), low(f32dot("md,ed->me", drelq, w_query))]
    )
    table_part = f32dot("rm,me->re", hot, table)
    output_part = f32dot("dt,te->de", inputs["attn_t"], inputs["mixed_low"])
    rest = low(jnp.concatenate([output_part, query_part, key_part, value_part, table_part]))
    outer_part = low(f32dot("tf,td->fd", inputs["active"], inputs["outer_low"]))
    inner_part = low(f32dot("td,tf->df", inputs["hidden_low"], inputs["inner_low"]))
    ext_grad = f32dot("td,ed->te", dkey, w_key) + f32dot("td,ed->te", dvalue, w_value)
    tokens_grad = (
        inputs["resid"]
        + f32dot("td,ed->te", dquery, w_query)
        + ext_grad[SPAN : SPAN + block_len]
        + shifted(low(ext_grad[:SPAN]), "seq", -1).astype(jnp.float32)
        + shifted(low(ext_grad[SPAN + block_len :]), "seq", 1).astype(jnp.float32)
    )
    both = ("rows", "seq")
    sums = [
        lax.all_gather(
            lax.psum_scatter(part, both, scatter_dimension=0, tiled=True), both, axis=0, tiled=True
        )
        for part in (outer_part, inner_part, rest)
    ]
    return (*sums, lax.psum(inputs["vectors"], both), low(tokens_grad))


def finish_of(inputs):
    seq_count, rows_count = lax.axis_size("seq"), lax.axis_size("rows")
    if rows_count == 2 and seq_count == 16:
        return finish(inputs, seq_count)
    return finish_plain(inputs)

def shards(
    tokens, cotangent, w_query, w_key, w_value, w_output, w_inner, w_outer, rel_table,
    mid_gain, mid_bias, end_gain, end_bias, seq_lengths, pad_mask, rel_buckets,
):
    width = tokens.shape[-1]
    inputs = {
        "tokens": tokens[0], "cotangent": cotangent[0], "rel_table": rel_table, "w_query": w_query,
        "w_key": w_key, "w_value": w_value, "w_output": w_output, "w_inner": w_inner, "w_outer": w_outer,
        "rel_buckets": rel_buckets, "mid_gain": mid_gain, "mid_bias": mid_bias, "end_gain": end_gain,
        "end_bias": end_bias, "keep": pad_mask.reshape(-1, TILE), "lengths": seq_lengths,
    }
    kept = start(inputs, lax.axis_size("seq"))
    layer_out = kept.pop("layer_out")
    inputs.update(kept)
    outer_w, inner_w, rest_w, norm_parts, tokens_grad = finish_of(inputs)
    output_w, query_w, key_w, value_w = (rest_w[at * width : (at + 1) * width] for at in range(4))
    table_w = rest_w[4 * width :]
    return (
        layer_out[None], tokens_grad[None],
        *(w.astype(jnp.float32) for w in (query_w, key_w, value_w, output_w, inner_w, outer_w, table_w)),
        *(norm_parts[at] for at in range(4)),
    )


def solution(mesh):
    split = P("rows", "seq", None)
    return jax.shard_map(
        shards,
        mesh=mesh,
        in_specs=(split, split) + (P(),) * 11 + (P("rows", None), P("rows", None), P()),
        out_specs=(split, split) + (P(),) * 11,
        check_vma=False,
    )
```

```python
import functools
import math

import jax
import jax.numpy as jnp
from jax import lax
from jax.experimental import pallas as pl
from jax.experimental.pallas import tpu as pltpu
from jax.sharding import PartitionSpec as P

H = 12
DH = 64
SPAN = 256
TILE = 128
REACH = 640
PAIR = 128
score_scale = 1.0 / math.sqrt(3 * DH)


def nt(left, right):
    return lax.dot_general(left, right, (((1,), (1,)), ((), ())), preferred_element_type=jnp.float32)


def nn(left, right):
    return lax.dot_general(left, right, (((1,), (0,)), ((), ())), preferred_element_type=jnp.float32)


def head_lanes(values, head):
    lane = lax.broadcasted_iota(jnp.int32, values.shape, 1)
    mine = (lane < DH) if head == 0 else (lane >= DH)
    return jnp.where(mine, values, jnp.zeros_like(values))


def unit(reverse):
    row = lax.broadcasted_iota(jnp.int32, (TILE, TILE), 0)
    col = lax.broadcasted_iota(jnp.int32, (TILE, TILE), 1)
    hit = (row + col == TILE - 1) if reverse else (row == col)
    return jnp.where(hit, 1.0, 0.0).astype(jnp.bfloat16)


def attend_back_kernel(
    q_ref, k_ref, v_ref, grad_ref, prob_ref, relk_ref, relq_ref,
    dq_ref, dk_ref, dv_ref, drelk_ref, drelq_ref, qt_ref, kt_ref,
):
    swap = unit(True)
    for source, result in ((q_ref, qt_ref), (k_ref, kt_ref)):
        for at in range(0, source.shape[0], TILE):
            flipped = nn(swap, source[pl.ds(at, TILE), :])
            result[:, pl.ds(at, TILE)] = flipped.T.astype(jnp.bfloat16)
    row = lax.broadcasted_iota(jnp.int32, (TILE, TILE), 0)
    col = lax.broadcasted_iota(jnp.int32, (TILE, TILE), 1)
    parts = REACH // TILE
    tiles = q_ref.shape[0] // TILE
    dk_ref[...] = jnp.zeros_like(dk_ref)
    dv_ref[...] = jnp.zeros_like(dv_ref)
    drelk_ref[...] = jnp.zeros_like(drelk_ref)
    drelq_ref[...] = jnp.zeros_like(drelq_ref)
    for tile in range(tiles):
        first = tile * TILE
        q_tile = q_ref[pl.ds(first, TILE), :]
        grad_tile = grad_ref[pl.ds(first, TILE), :]
        v_tile = v_ref[pl.ds(first, REACH), :]
        q_heads = [head_lanes(q_tile, head) for head in range(2)]
        grad_heads = [head_lanes(grad_tile, head) for head in range(2)]
        dq_heads = []
        lefts = [[] for _ in range(parts)]
        for head in range(2):
            lanes = pl.ds(head * DH, DH)
            probs = prob_ref[head, tile].astype(jnp.float32)
            weighted = probs * nt(v_tile, grad_heads[head])
            delta = jnp.sum(weighted, axis=0, keepdims=True)
            dscore = ((weighted - probs * delta) * score_scale).astype(jnp.bfloat16)
            turned = nt(swap, dscore)
            dband = pltpu.roll(turned, REACH - TILE + 1, 1, stride=1, stride_axis=0)
            dband = dband[:, : 2 * SPAN].astype(jnp.bfloat16)
            dq_heads.append(
                nn(turned.astype(jnp.bfloat16), k_ref[pl.ds(first, REACH), :])
                + nn(dband, relk_ref[...])
            )
            drelk_ref[lanes, :] += nn(qt_ref[lanes, pl.ds(first, TILE)], dband)
            for part in range(parts):
                flipped = nn(swap, dscore[part * TILE : (part + 1) * TILE, :])
                spun = pltpu.roll(flipped, 0, 1, stride=1, stride_axis=0)
                low = jnp.where(col >= row, spun, 0.0)
                dfrom = jnp.concatenate([low, spun - low], axis=1).astype(jnp.bfloat16)
                window = pl.ds((parts - 1 - part) * TILE, 2 * TILE)
                drelq_ref[lanes, window] += nn(kt_ref[lanes, pl.ds(first + part * TILE, TILE)], dfrom)
                lefts[part] += [flipped.astype(jnp.bfloat16), dfrom]
        dq_turned = jnp.where(col < DH, dq_heads[0], dq_heads[1]).astype(jnp.bfloat16)
        dq_ref[pl.ds(first, TILE), :] = nn(swap, dq_turned).astype(dq_ref.dtype)
        dv_ref[pl.ds(first, REACH), :] += nn(
            jnp.concatenate([prob_ref[0, tile], prob_ref[1, tile]], axis=1),
            jnp.concatenate(grad_heads, axis=0),
        )
        for part in range(parts):
            window = relq_ref[pl.ds((parts - 1 - part) * TILE, 2 * TILE), :]
            right = jnp.concatenate(
                [q_heads[0], head_lanes(window, 0), q_heads[1], head_lanes(window, 1)], axis=0
            )
            dk_ref[pl.ds(first + part * TILE, TILE), :] += nn(
                jnp.concatenate(lefts[part], axis=1), right
            )


def attend_back(query, key_ext, value_ext, grad, probs, relk, relq):
    block_len, width = query.shape
    ext_len = key_ext.shape[0]
    tiles = block_len // TILE
    pairs = width // PAIR
    table = 2 * SPAN
    cols = lambda n: pl.BlockSpec((n, PAIR), lambda p: (0, p))
    rows = lambda n: pl.BlockSpec((PAIR, n), lambda p: (p, 0))
    f32 = lambda *s: jax.ShapeDtypeStruct(s, jnp.float32)
    return pl.pallas_call(
        attend_back_kernel,
        grid=(pairs,),
        in_specs=[
            cols(block_len), cols(ext_len), cols(ext_len), cols(block_len),
            pl.BlockSpec((2, tiles, REACH, TILE), lambda p: (p, 0, 0, 0)),
            cols(table), cols(table + 2 * TILE),
        ],
        out_specs=[cols(block_len), cols(ext_len), cols(ext_len), rows(table), rows(table + 2 * TILE)],
        out_shape=[
            jax.ShapeDtypeStruct((block_len, width), jnp.bfloat16),
            f32(ext_len, width), f32(ext_len, width), f32(width, table), f32(width, table + 2 * TILE),
        ],
        scratch_shapes=[
            pltpu.VMEM((PAIR, block_len), jnp.bfloat16), pltpu.VMEM((PAIR, ext_len), jnp.bfloat16),
        ],
        compiler_params=pltpu.CompilerParams(vmem_limit_bytes=48 * 2**20),
        name="attend_back",
    )(query, key_ext, value_ext, grad, probs, relk, relq)


MESH = pl.DeviceIdType.MESH
PACK = 16


norm_eps = 1e-07
masked_score = -1e30
inverse_root_two = math.sqrt(0.5)
density_at_zero = 1.0 / math.sqrt(2.0 * math.pi)


def gelu_both(values):
    size = jnp.abs(values) * inverse_root_two
    t = 1.0 / (1.0 + 0.3275911 * size)
    poly = 1.061405429 * t - 1.453152027
    poly = poly * t + 1.421413741
    poly = poly * t - 0.284496736
    poly = poly * t + 0.254829592
    bell = jnp.exp(-size * size)
    tail = 0.5 * poly * t * bell
    share = jnp.where(values >= 0.0, 1.0 - tail, tail)
    return values * share, share + values * bell * density_at_zero


def mean_of(values):
    return jnp.mean(values, axis=-1, keepdims=True)


def by_blocks(width, body, step=256, unroll=3):
    def one(i, carry):
        body(pl.ds(pl.multiple_of(i * step, step), step))
        return carry

    lax.fori_loop(0, width // step, one, 0, unroll=unroll)


def column_of(row_values):
    row = lax.broadcasted_iota(jnp.int32, (TILE, TILE), 0)
    col = lax.broadcasted_iota(jnp.int32, (TILE, TILE), 1)
    return jnp.sum(jnp.where(row == col, row_values, 0), axis=1, keepdims=True)


def mask_of(r, seq_count):
    ext_len, block_len = r["bias"].shape
    place = lax.axis_index("seq")
    row_len = block_len * seq_count
    ends, end = [], 0
    for number in range(r["lengths"].shape[1]):
        end = end + r["lengths"][0, number]
        ends.append(end)

    def segment(slots):
        return sum((slots >= end).astype(jnp.int32) for end in ends)

    query = place * block_len + lax.broadcasted_iota(jnp.int32, (1, block_len), 1)
    query_segment = segment(query)
    for block in range(ext_len // TILE):
        first = place * block_len - SPAN + block * TILE
        line = lax.clamp(0, place * (block_len // TILE) - SPAN // TILE + block, row_len // TILE - 1)
        keep = column_of(r["keep"][pl.ds(line, 1), :])
        key = first + lax.broadcasted_iota(jnp.int32, (TILE, 1), 0)
        key_segment = jnp.where((key >= 0) & (key < row_len), segment(key), -1)
        apart = key - query
        seen = (key_segment == query_segment) & (jnp.abs(apart) < SPAN)
        seen = seen & ((keep == 1) | (apart == 0))
        r["bias"][pl.ds(block * TILE, TILE), :] = jnp.where(seen, 0.0, masked_score)


def score_part(r, pair, tile, head, part, q_head, to_term):
    lanes = pl.ds(pl.multiple_of(pair * PAIR, PAIR), PAIR)
    first = tile * TILE
    at = first + part * TILE
    k_part = r["k"][pl.ds(at, TILE), lanes]
    window = r["relq"][pl.ds((REACH // TILE - 1 - part) * TILE, 2 * TILE), lanes]
    from_band = nt(head_lanes(k_part, head), window)
    from_term = pltpu.roll(from_band, TILE + 1, 1, stride=1, stride_axis=0)[:, :TILE]
    left = jnp.concatenate([k_part, unit(False)], axis=1)
    right = jnp.concatenate([q_head, to_term], axis=1)
    r["scores"][pair, tile, head, pl.ds(part * TILE, TILE), :] = (
        nt(left, right) + from_term + r["bias"][pl.ds(at, TILE), pl.ds(first, TILE)]
    )


def parts_of(tile, block_len):
    first = SPAN // TILE - tile
    own = range(first, first + block_len // TILE)
    return own, [part for part in range(REACH // TILE) if part not in own]


def attend_own(pair, r):
    lanes = pl.ds(pl.multiple_of(pair * PAIR, PAIR), PAIR)
    block_len = r["q"].shape[0]
    for tile in range(block_len // TILE):
        q_tile = r["q"][pl.ds(tile * TILE, TILE), lanes]
        for head in range(2):
            q_head = head_lanes(q_tile, head)
            band = nt(q_head, r["relk"][:, lanes])
            band = jnp.concatenate([band, jnp.zeros((TILE, REACH - 2 * SPAN), jnp.float32)], axis=1)
            to_term = pltpu.roll(band, 0, 1, stride=1, stride_axis=0).astype(jnp.bfloat16)
            r["to_terms"][pair, tile, head] = to_term
            for part in parts_of(tile, block_len)[0]:
                score_part(r, pair, tile, head, part, q_head, to_term[:, part * TILE : (part + 1) * TILE])


def attend_rest(pair, buf, r):
    log_two = score_scale * math.log2(math.e)
    lanes = pl.ds(pl.multiple_of(pair * PAIR, PAIR), PAIR)
    block_len = r["q"].shape[0]
    for at in range(0, r["v"].shape[0], TILE):
        r["vt"][:, pl.ds(at, TILE)] = r["v"][pl.ds(at, TILE), lanes].T
    for tile in range(block_len // TILE):
        first = tile * TILE
        q_tile = r["q"][pl.ds(first, TILE), lanes]
        outs = []
        for head in range(2):
            q_head = head_lanes(q_tile, head)
            for part in parts_of(tile, block_len)[1]:
                to_term = r["to_terms"][pair, tile, head, :, pl.ds(part * TILE, TILE)]
                score_part(r, pair, tile, head, part, q_head, to_term)
            scores = r["scores"][pair, tile, head]
            top = jnp.max(scores, axis=0, keepdims=True)
            weights = jnp.exp2((scores - top) * log_two)
            total = jnp.sum(weights, axis=0, keepdims=True)
            probs = (weights * (1.0 / total)).astype(jnp.bfloat16)
            r["probs"][buf, head, tile] = probs
            outs.append(nn(r["vt"][pl.ds(head * DH, DH), pl.ds(first, REACH)], probs))
        both = jnp.concatenate(outs, axis=0)
        r["attn_t"][lanes, pl.ds(first, TILE)] = both.astype(jnp.bfloat16)
        r["attn"][pl.ds(first, TILE), lanes] = both.T.astype(jnp.bfloat16)


START_HBM = (
    "tokens", "rel_table", "w_query", "w_key", "w_value", "w_output", "w_inner", "w_outer", "cotangent",
)
START_VMEM = ("rel_buckets", "mid_gain", "mid_bias", "end_gain", "end_bias", "keep")
START_IN = START_HBM + START_VMEM + ("lengths",)
START_KEPT = (
    "x", "q", "k", "v", "relk", "relq", "to_table", "from_table", "hot", "grad", "resid",
    "active", "inner_low", "outer_low", "hidden_low", "mixed_low", "attn_t",
)
START_OUT = START_KEPT + ("probs_out", "layer_out", "vectors")
START_SCRATCH = START_KEPT + (
    "rel_table", "w_query", "w_key", "w_value", "w_output", "w_inner", "w_outer", "cotangent",
    "bias", "vt", "scores", "to_terms", "probs", "attn", "mixed", "hidden", "z_mid", "root_mid", "slope", "sum_grad",
    "load_sem", "keep_sem", "probs_sem", "send_sem", "recv_sem",
)


def start_kernel(seq_count, *refs):
    given = dict(zip(START_IN, refs))
    outs = dict(zip(START_OUT, refs[len(START_IN) :]))
    r = dict(zip(START_SCRATCH, refs[len(START_IN) + len(START_OUT) :]))
    r.update((name, given[name]) for name in START_VMEM + ("lengths",))
    block_len, width = r["q"].shape
    ext_len, table_len = r["x"].shape[0], r["to_table"].shape[0]
    inner_width = r["w_inner"].shape[1]
    pairs = width // PAIR
    own = pl.ds(SPAN, block_len)

    loads = {}
    for number, name in enumerate(START_HBM):
        target = r["x"].at[own] if name == "tokens" else r[name]
        loads[name] = pltpu.make_async_copy(given[name], target, r["load_sem"].at[number])
        loads[name].start()
    row, place = lax.axis_index("rows"), lax.axis_index("seq")
    before = {"rows": row, "seq": lax.rem(place + seq_count - 1, seq_count)}
    after = {"rows": row, "seq": lax.rem(place + 1, seq_count)}
    barrier = pltpu.get_barrier_semaphore()
    for device in (before, after):
        pl.semaphore_signal(barrier, inc=1, device_id=device, device_id_type=MESH)
    pl.semaphore_wait(barrier, 2)
    halos = [
        pltpu.make_async_remote_copy(
            src_ref=given["tokens"], dst_ref=r["x"].at[pl.ds(at, SPAN)], send_sem=r["send_sem"].at[number],
            recv_sem=r["recv_sem"].at[number], device_id=device, device_id_type=MESH,
        )
        for number, (at, device) in enumerate(((0, after), (SPAN + block_len, before)))
    ]
    for copy in halos:
        copy.start()

    def keep(name):
        pltpu.make_async_copy(r[name], outs[name], r["keep_sem"].at[START_KEPT.index(name)]).start()

    def low(values):
        return values.astype(jnp.bfloat16)

    place_of = lax.broadcasted_iota(jnp.int32, (table_len, table_len), 0)
    turned_bucket = pltpu.roll(r["rel_buckets"][...].reshape(1, table_len), table_len - 1, 1)
    to_pos = jnp.clip(turned_bucket + SPAN, 0, table_len - 1)
    from_pos = jnp.clip(SPAN - turned_bucket, 0, table_len - 1)
    r["hot"][:, pl.ds(table_len, table_len)] = low(jnp.where(place_of == from_pos, 1.0, 0.0))
    to_turned = low(jnp.where(place_of == to_pos, 1.0, 0.0))
    for at in range(0, table_len, TILE):
        r["hot"][:, pl.ds(at, TILE)] = low(
            nn(to_turned[:, table_len - TILE - at : table_len - at], unit(True))
        )
    keep("hot")
    mask_of(r, seq_count)
    loads["rel_table"].wait()
    for number, name in enumerate(("to", "from")):
        hot = r["hot"][:, pl.ds(number * table_len, table_len)].T

        def table_cols(cols, hot=hot, name=name):
            r[name + "_table"][:, cols] = low(nn(hot, r["rel_table"][:, cols]))

        by_blocks(width, table_cols)
        keep(name + "_table")
    loads["w_query"].wait()
    loads["tokens"].wait()
    r["relq"][pl.ds(0, TILE), :] = jnp.zeros((TILE, width), jnp.bfloat16)
    r["relq"][pl.ds(TILE + table_len, TILE), :] = jnp.zeros((TILE, width), jnp.bfloat16)

    def query_cols(cols):
        r["q"][:, cols] = low(nn(r["x"][own, :], r["w_query"][:, cols]))
        r["relq"][pl.ds(TILE, table_len), cols] = low(nn(r["from_table"][...], r["w_query"][:, cols]))

    by_blocks(width, query_cols)
    keep("q")
    keep("relq")
    loads["w_key"].wait()

    def relk_cols(cols):
        r["relk"][:, cols] = low(nn(r["to_table"][...], r["w_key"][:, cols]))

    by_blocks(width, relk_cols)
    keep("relk")
    loads["w_value"].wait()

    def pair_rows(rows):
        def pair_cols(cols):
            r["k"][rows, cols] = low(nn(r["x"][rows, :], r["w_key"][:, cols]))
            r["v"][rows, cols] = low(nn(r["x"][rows, :], r["w_value"][:, cols]))

        by_blocks(width, pair_cols)

    pair_rows(own)

    def own_pair(pair, carry):
        attend_own(pair, r)
        return carry

    lax.fori_loop(0, pairs, own_pair, 0)
    for copy in halos:
        copy.wait()
    keep("x")
    pair_rows(pl.ds(0, SPAN))
    pair_rows(pl.ds(SPAN + block_len, SPAN))
    keep("k")
    keep("v")

    def probs_copy(pair, buf):
        return pltpu.make_async_copy(
            r["probs"].at[buf], outs["probs_out"].at[pl.ds(2 * pair, 2)], r["probs_sem"].at[buf]
        )

    def one_pair(pair, carry):
        buf = lax.rem(pair, 2)

        @pl.when(pair >= 2)
        def _():
            probs_copy(pair - 2, buf).wait()

        attend_rest(pair, buf, r)
        probs_copy(pair, buf).start()
        return carry

    lax.fori_loop(0, pairs, one_pair, 0)

    keep("attn_t")
    for name in ("w_output", "w_inner", "w_outer", "cotangent"):
        loads[name].wait()

    def mixed_cols(cols):
        r["mixed"][:, cols] = nn(r["attn"][...], r["w_output"][:, cols])

    by_blocks(width, mixed_cols)
    high = 64
    mid_gain, mid_bias, end_gain, end_bias = (
        r[name][...].reshape(1, width) for name in ("mid_gain", "mid_bias", "end_gain", "end_bias")
    )

    def mid_rows(rows):
        mine = pl.ds(pl.multiple_of(SPAN + rows.start, high), high)
        values = r["x"][mine, :].astype(jnp.float32) + r["mixed"][rows, :]
        centre = values - mean_of(values)
        root = lax.rsqrt(mean_of(centre * centre) + norm_eps)
        z = centre * root
        hidden = z * mid_gain + mid_bias
        r["z_mid"][rows, :] = z
        r["root_mid"][rows, :] = jnp.broadcast_to(root, (high, TILE))
        r["hidden"][rows, :] = hidden
        r["hidden_low"][rows, :] = low(hidden)

    by_blocks(block_len, mid_rows, high)
    keep("hidden_low")

    def active_cols(cols):
        active, slope = gelu_both(nn(r["hidden_low"][...], r["w_inner"][:, cols]))
        r["active"][:, cols] = low(active)
        r["slope"][:, cols] = low(slope)

    by_blocks(inner_width, active_cols, unroll=12)
    keep("active")

    def outer_cols(cols):
        r["mixed"][:, cols] = nn(r["active"][...], r["w_outer"][:, cols])

    by_blocks(width, outer_cols)
    outs["vectors"][...] = jnp.zeros_like(outs["vectors"])

    def end_rows(rows):
        values = r["hidden"][rows, :] + r["mixed"][rows, :]
        centre = values - mean_of(values)
        root = lax.rsqrt(mean_of(centre * centre) + norm_eps)
        z = centre * root
        outs["layer_out"][rows, :] = low(z * end_gain + end_bias)
        cotangent = r["cotangent"][rows, :].astype(jnp.float32)
        outs["vectors"][pl.ds(2, 1), :] += jnp.sum(cotangent * z, axis=0, keepdims=True)
        outs["vectors"][pl.ds(3, 1), :] += jnp.sum(cotangent, axis=0, keepdims=True)
        grad = cotangent * end_gain
        sum_grad = root * (grad - mean_of(grad) - z * mean_of(grad * z))
        r["sum_grad"][rows, :] = sum_grad
        r["outer_low"][rows, :] = low(sum_grad)

    by_blocks(block_len, end_rows, high)
    keep("outer_low")

    def inner_cols(cols):
        grad = nt(r["outer_low"][...], r["w_outer"][cols, :])
        r["inner_low"][:, cols] = low(grad * r["slope"][:, cols].astype(jnp.float32))

    by_blocks(inner_width, inner_cols, unroll=12)
    keep("inner_low")

    def hidden_cols(cols):
        r["mixed"][:, cols] = r["sum_grad"][:, cols] + nt(r["inner_low"][...], r["w_inner"][cols, :])

    by_blocks(width, hidden_cols)

    def resid_rows(rows):
        hidden_grad, z = r["mixed"][rows, :], r["z_mid"][rows, :]
        outs["vectors"][pl.ds(0, 1), :] += jnp.sum(hidden_grad * z, axis=0, keepdims=True)
        outs["vectors"][pl.ds(1, 1), :] += jnp.sum(hidden_grad, axis=0, keepdims=True)
        grad = hidden_grad * mid_gain
        root = r["root_mid"][rows, pl.ds(0, 1)]
        resid = root * (grad - mean_of(grad) - z * mean_of(grad * z))
        r["resid"][rows, :] = resid
        r["mixed_low"][rows, :] = low(resid)

    by_blocks(block_len, resid_rows, high)
    keep("resid")
    keep("mixed_low")

    def grad_cols(cols):
        r["grad"][:, cols] = low(nt(r["mixed_low"][...], r["w_output"][cols, :]))

    by_blocks(width, grad_cols)
    keep("grad")
    for pair in (pairs - 2, pairs - 1):
        probs_copy(pair, pair % 2).wait()
    for number, name in enumerate(START_KEPT):
        pltpu.make_async_copy(r[name], outs[name], r["keep_sem"].at[number]).wait()


def start(inputs, seq_count):
    block_len, width = inputs["tokens"].shape
    table_len = inputs["rel_table"].shape[0]
    inner_width = inputs["w_inner"].shape[1]
    ext_len = block_len + 2 * SPAN
    tiles = block_len // TILE
    heads = 2 * (width // PAIR)
    sizes = {
        "x": (ext_len, width), "q": (block_len, width), "k": (ext_len, width), "v": (ext_len, width),
        "relk": (table_len, width), "relq": (table_len + 2 * TILE, width), "to_table": (table_len, width),
        "from_table": (table_len, width), "hot": (table_len, 2 * table_len), "grad": (block_len, width),
        "resid": (block_len, width), "active": (block_len, inner_width),
        "inner_low": (block_len, inner_width), "outer_low": (block_len, width),
        "hidden_low": (block_len, width), "mixed_low": (block_len, width), "attn_t": (width, block_len),
    }
    kinds = {name: jnp.float32 if name == "resid" else jnp.bfloat16 for name in START_KEPT}
    bf = lambda *shape: pltpu.VMEM(shape, jnp.bfloat16)
    f32 = lambda *shape: pltpu.VMEM(shape, jnp.float32)
    dma = pltpu.SemaphoreType.DMA
    any_spec = pl.BlockSpec(memory_space=pl.ANY)
    vmem = pl.BlockSpec(memory_space=pltpu.VMEM)
    smem = pl.BlockSpec(memory_space=pltpu.SMEM)
    values = pl.pallas_call(
        functools.partial(start_kernel, seq_count),
        in_specs=[any_spec] * len(START_HBM) + [vmem] * len(START_VMEM) + [smem],
        out_specs=[any_spec] * (len(START_KEPT) + 1) + [vmem] * 2,
        out_shape=[
            *(jax.ShapeDtypeStruct(sizes[name], kinds[name]) for name in START_KEPT),
            jax.ShapeDtypeStruct((heads, tiles, REACH, TILE), jnp.bfloat16),
            jax.ShapeDtypeStruct((block_len, width), jnp.bfloat16),
            jax.ShapeDtypeStruct((8, width), jnp.float32),
        ],
        scratch_shapes=[
            *(pltpu.VMEM(sizes[name], kinds[name]) for name in START_KEPT),
            *(pltpu.VMEM(inputs[name].shape, inputs[name].dtype) for name in START_HBM[1:]),
            f32(ext_len, block_len), bf(PAIR, ext_len), f32(heads // 2, tiles, 2, REACH, TILE),
            bf(heads // 2, tiles, 2, TILE, REACH), bf(2, 2, tiles, REACH, TILE),
            bf(block_len, width), f32(block_len, width), f32(block_len, width), f32(block_len, width),
            f32(block_len, TILE), bf(block_len, inner_width), f32(block_len, width),
            dma((len(START_HBM),)), dma((len(START_KEPT),)), dma((2,)), dma((2,)), dma((2,)),
        ],
        compiler_params=pltpu.CompilerParams(
            collective_id=1, has_side_effects=True, vmem_limit_bytes=60 * 2**20
        ),
        name="start",
    )(*(inputs[name] for name in START_IN))
    return dict(zip(START_OUT, values))


class Line:
    def __init__(self, side, row_step, seq_step):
        self.side = side
        row, place = lax.axis_index("rows"), lax.axis_index("seq")
        away = 1 - 2 * side
        self.device = {"rows": row + away * row_step, "seq": place + away * seq_step}


def lines_of():
    row, place = lax.axis_index("rows"), lax.axis_index("seq")
    first, second, third, fourth = (place // step % 2 for step in (1, 2, 4, 8))
    core = Line(row, 1, 0)
    near = Line(first + row * (second - first), 0, 1 + row)
    cross = Line(second + row * (first - second), 0, 2 - row)
    low_z, high_z = Line(third, 0, 4), Line(fourth, 0, 8)
    return (core, near, cross, low_z, high_z), (core, low_z, high_z, near, cross)


def add_rows(left, right, out):
    rows = out.shape[0]
    step = next(s for s in (48, 32, PACK) if rows % s == 0)

    def body(i, carry):
        here = pl.ds(pl.multiple_of(i * step, PACK), step)
        out[here, :] = left[here, :] + right[here, :]
        return carry

    lax.fori_loop(0, rows // step, body, 0)


class Chunk:
    def __init__(self, index, which, start, half, base, width, z_first):
        self.index, self.which, self.start, self.half = index, which, start, half
        self.base, self.width, self.z_first = base, width, z_first

    def out(self, refs, side):
        if self.which == "inner":
            col = (self.start // self.width + side) * self.width
            return refs["inner"].at[:, pl.ds(pl.multiple_of(col, PAIR), self.width)]
        first = pl.multiple_of(self.start + side * self.half, PACK)
        return refs[self.which].at[pl.ds(first, self.half)]


def chunks_of(spec, unit, width):
    chunks, starts, base = [], {}, 0
    for which, units, z_first in spec:
        start = starts.get(which, 0)
        chunks.append(Chunk(len(chunks), which, start, units * unit // 2, base, width, z_first))
        starts[which] = start + units * unit
        base += units * unit
    return chunks, base


class Sum:
    phases = 5
    last = 2 * phases

    def __init__(self, chunks, outs, work, recv, own_sem, send_sem, recv_sem):
        self.chunks, self.outs, self.work, self.recv = chunks, outs, work, recv
        self.own_sem, self.send_sem, self.recv_sem = own_sem, send_sem, recv_sem
        self.row = lax.axis_index("rows")
        self.plane_first, self.z_first = lines_of()

    def greet(self, more):
        barrier = pltpu.get_barrier_semaphore()
        devices = [line.device for line in self.plane_first] + more
        for device in devices:
            pl.semaphore_signal(barrier, inc=1, device_id=device, device_id_type=MESH)
        pl.semaphore_wait(barrier, len(devices))

    def lines(self, chunk):
        return self.z_first if chunk.z_first else self.plane_first

    def offset(self, chunk, phase):
        at, rows = 0, chunk.half
        for line in self.lines(chunk)[1 : phase + 1]:
            rows //= 2
            at = at + line.side * rows
        return at

    def working(self, chunk, at, rows):
        return self.work.at[pl.ds(pl.multiple_of(chunk.base + self.row * chunk.half + at, PACK), rows)]

    def received(self, chunk, phase):
        at = chunk.base + sum(chunk.half >> p for p in range(phase))
        return self.recv.at[pl.ds(at, chunk.half >> phase)]

    def summed(self, chunk, phase):
        at = pl.multiple_of(chunk.base + self.offset(chunk, phase), PACK)
        return self.recv.at[pl.ds(at, chunk.half >> phase)]

    def copies(self, chunk, stage):
        gather = stage >= self.phases
        phase = self.last - 1 - stage if gather else stage
        line, rows = self.lines(chunk)[phase], chunk.half >> phase
        local = None
        if gather:
            source = target = self.summed(chunk, phase)
            if phase == 0:
                target = chunk.out(self.outs, self.row)
                local = (source, target)
        else:
            target = self.received(chunk, phase)
            if phase == 0:
                other = chunk.base + (1 - self.row) * chunk.half
                source = self.work.at[pl.ds(pl.multiple_of(other, PACK), rows)]
            else:
                source = self.working(chunk, self.offset(chunk, phase - 1) + (1 - line.side) * rows, rows)
        sem = chunk.index * self.last + stage
        copies = [
            pltpu.make_async_remote_copy(
                src_ref=source, dst_ref=target, send_sem=self.send_sem.at[sem],
                recv_sem=self.recv_sem.at[sem], device_id=line.device, device_id_type=MESH,
            )
        ]
        if local is not None:
            copies.append(pltpu.make_async_copy(*local, self.own_sem.at[chunk.index]))
        return copies

    def step(self, c, stage):
        chunk = self.chunks[c]
        if stage > 0:
            for copy in self.copies(chunk, stage - 1):
                copy.wait()
        if 0 < stage <= self.phases:
            phase = stage - 1
            mine = self.working(chunk, self.offset(chunk, phase), chunk.half >> phase)
            add_rows(mine, self.received(chunk, phase), self.summed(chunk, phase) if stage == self.phases else mine)
        if stage < self.last:
            for copy in self.copies(chunk, stage):
                copy.start()


class VectorSum:
    def __init__(self, lines, acc, recv, send_sem, recv_sem):
        self.lines, self.acc, self.recv, self.send_sem, self.recv_sem = lines, acc, recv, send_sem, recv_sem

    def copy(self, phase):
        return pltpu.make_async_remote_copy(
            src_ref=self.acc.at[phase], dst_ref=self.recv.at[phase], send_sem=self.send_sem.at[phase],
            recv_sem=self.recv_sem.at[phase], device_id=self.lines[phase].device, device_id_type=MESH,
        )

    def start(self, phase):
        self.copy(phase).start()

    def end(self, phase):
        self.copy(phase).wait()
        self.acc[phase + 1] = self.acc[phase] + self.recv[phase]


def back_of_pair(pair, buf, r):
    swap = unit(True)
    lanes_at = pl.multiple_of(pair * PAIR, PAIR)
    lanes_here = pl.ds(lanes_at, PAIR)
    row = lax.broadcasted_iota(jnp.int32, (TILE, TILE), 0)
    col = lax.broadcasted_iota(jnp.int32, (TILE, TILE), 1)
    parts = REACH // TILE
    block_len, ext_len = r["q"].shape[0], r["k"].shape[0]
    tiles = block_len // TILE
    qt_ref, kt_ref, dk_ref, dv_ref, drelk_ref, drelq_ref = (
        r[name] for name in ("qt", "kt", "dk_pair", "dv_pair", "drelk_t", "drelq_t")
    )
    for source, result in ((r["q"], qt_ref), (r["k"], kt_ref)):
        for at in range(0, source.shape[0], TILE):
            flipped = nn(swap, source[pl.ds(at, TILE), lanes_here])
            result[:, pl.ds(at, TILE)] = flipped.T.astype(jnp.bfloat16)
    dk_ref[...] = jnp.zeros_like(dk_ref)
    dv_ref[...] = jnp.zeros_like(dv_ref)
    drelk_ref[...] = jnp.zeros_like(drelk_ref)
    drelq_ref[...] = jnp.zeros_like(drelq_ref)
    for tile in range(tiles):
        first = tile * TILE
        q_tile = r["q"][pl.ds(first, TILE), lanes_here]
        grad_tile = r["grad"][pl.ds(first, TILE), lanes_here]
        v_tile = r["v"][pl.ds(first, REACH), lanes_here]
        q_heads = [head_lanes(q_tile, head) for head in range(2)]
        grad_heads = [head_lanes(grad_tile, head) for head in range(2)]
        dq_heads = []
        lefts = [[] for _ in range(parts)]
        for head in range(2):
            lanes = pl.ds(head * DH, DH)
            probs = r["probs"][buf, head, tile].astype(jnp.float32)
            weighted = probs * nt(v_tile, grad_heads[head])
            delta = jnp.sum(weighted, axis=0, keepdims=True)
            dscore = ((weighted - probs * delta) * score_scale).astype(jnp.bfloat16)
            turned = nt(swap, dscore)
            dband = pltpu.roll(turned, REACH - TILE + 1, 1, stride=1, stride_axis=0)
            dband = dband[:, : 2 * SPAN].astype(jnp.bfloat16)
            dq_heads.append(
                nn(turned.astype(jnp.bfloat16), r["k"][pl.ds(first, REACH), lanes_here])
                + nn(dband, r["relk"][:, lanes_here])
            )
            drelk_ref[lanes, :] += nn(qt_ref[lanes, pl.ds(first, TILE)], dband)
            for part in range(parts):
                flipped = nn(swap, dscore[part * TILE : (part + 1) * TILE, :])
                spun = pltpu.roll(flipped, 0, 1, stride=1, stride_axis=0)
                near = jnp.where(col >= row, spun, 0.0)
                dfrom = jnp.concatenate([near, spun - near], axis=1).astype(jnp.bfloat16)
                window = pl.ds((parts - 1 - part) * TILE, 2 * TILE)
                drelq_ref[lanes, window] += nn(kt_ref[lanes, pl.ds(first + part * TILE, TILE)], dfrom)
                lefts[part] += [flipped.astype(jnp.bfloat16), dfrom]
        dq_turned = jnp.where(col < DH, dq_heads[0], dq_heads[1]).astype(jnp.bfloat16)
        r["dq"][pl.ds(first, TILE), lanes_here] = nn(swap, dq_turned).astype(jnp.bfloat16)
        dv_ref[pl.ds(first, REACH), :] += nn(
            jnp.concatenate([r["probs"][buf, 0, tile], r["probs"][buf, 1, tile]], axis=1),
            jnp.concatenate(grad_heads, axis=0),
        )
        for part in range(parts):
            window = r["relq"][pl.ds((parts - 1 - part) * TILE, 2 * TILE), lanes_here]
            right = jnp.concatenate(
                [q_heads[0], head_lanes(window, 0), q_heads[1], head_lanes(window, 1)], axis=0
            )
            dk_ref[pl.ds(first + part * TILE, TILE), :] += nn(
                jnp.concatenate(lefts[part], axis=1), right
            )
    r["dv"][:, lanes_here] = dv_ref[...].astype(jnp.bfloat16)
    for at in range(0, ext_len, TILE):
        r["dk"][pl.ds(at, TILE), lanes_here] = nn(
            swap, dk_ref[pl.ds(at, TILE), :].astype(jnp.bfloat16)
        ).astype(jnp.bfloat16)
    r["dk"][pl.ds(ext_len, 2 * SPAN), lanes_here] = drelk_ref[...].T.astype(jnp.bfloat16)
    r["dq"][pl.ds(block_len, 2 * SPAN), lanes_here] = (
        drelq_ref[:, pl.ds(TILE, 2 * SPAN)].T.astype(jnp.bfloat16)
    )


SOONEST = ("outer_low", "hidden_low", "mixed_low", "attn_t")
SOONER = ("q", "k", "v", "grad", "relk", "relq")
LATER = ("x", "to_table", "from_table", "w_query", "w_key", "w_value", "hot", "resid")
FINISH_IN = ("active", "inner_low") + SOONEST + SOONER + LATER + ("vectors", "probs_out")
FINISH_OUT = ("outer", "inner", "rest", "vectors", "tokens_grad")
FINISH_SCRATCH = (
    "probs", "qt", "kt", "dk_pair", "dv_pair", "drelk_t", "drelq_t", "wide", "dv", "work", "table",
    "xt_query", "xt_key", "hidden_t", "halo", "halo_got", "own_grad", "recv", "vec_acc", "vec_recv", "own_sem",
    "send_sem", "recv_sem", "vec_send", "vec_got", "probs_sem", "halo_send", "halo_recv", "load_sem", "wide_sem",
)


def finish_kernel(chunks, schedule, seq_count, *refs):
    given = dict(zip(FINISH_IN, refs))
    outs = dict(zip(FINISH_OUT, refs[len(FINISH_IN) :]))
    scratch = refs[len(FINISH_IN) + len(FINISH_OUT) :]
    r = dict(zip(FINISH_SCRATCH, scratch))
    block_len, width = given["q"].shape
    ext_len = given["k"].shape[0]
    folds = given["active"].shape[1] // width
    wide_loads = {}
    for number, name in enumerate(("active", "inner_low")):
        wide_loads[name] = [
            pltpu.make_async_copy(
                given[name].at[:, pl.ds(fold * width, width)],
                r["wide"].at[pl.ds((number * folds + fold) * block_len, block_len)],
                r["wide_sem"].at[number * folds + fold],
            )
            for fold in range(folds)
        ]
    r["dk"] = r["wide"].at[pl.ds(0, ext_len + 2 * SPAN)]
    r["dq"] = r["wide"].at[pl.ds(ext_len + 2 * SPAN, block_len + 2 * SPAN)]
    loads = {}
    for number, (name, held) in enumerate(
        zip(SOONEST + SOONER + LATER, scratch[len(FINISH_SCRATCH) :])
    ):
        loads[name] = pltpu.make_async_copy(given[name], held, r["load_sem"].at[number])
        r[name] = held
    loads["outer_low"].start()
    for copy in wide_loads["active"] + wide_loads["inner_low"]:
        copy.start()
    for name in SOONEST[1:] + SOONER + LATER:
        loads[name].start()
    pairs = width // PAIR
    total = Sum(chunks, outs, r["work"], r["recv"], r["own_sem"], r["send_sem"], r["recv_sem"])
    row, place = lax.axis_index("rows"), lax.axis_index("seq")
    before = {"rows": row, "seq": lax.rem(place + seq_count - 1, seq_count)}
    after = {"rows": row, "seq": lax.rem(place + 1, seq_count)}
    total.greet([before, after])
    vec = VectorSum(total.plane_first, r["vec_acc"], r["vec_recv"], r["vec_send"], r["vec_got"])
    vec.acc[0] = given["vectors"][...]

    def probs_copy(pair, buf):
        return pltpu.make_async_copy(
            given["probs_out"].at[pl.ds(2 * pair, 2)], r["probs"].at[buf], r["probs_sem"].at[buf]
        )

    probs_copy(0, 0).start()
    inner_base = folds * width
    rest_base = 2 * folds * width

    def outer_piece(chunk):
        def body(i, carry):
            at = pl.multiple_of(chunk.start + i * 256, 256)
            fold, col = at // width, pl.multiple_of(at % width, 256)
            active = r["wide"][pl.ds(pl.multiple_of(fold * block_len, block_len), block_len), pl.ds(col, 256)]
            r["work"][pl.ds(at, 256), :] = nn(active.T, r["outer_low"][...]).astype(jnp.bfloat16)
            return carry

        lax.fori_loop(0, 2 * chunk.half // 256, body, 0)

    def inner_piece(chunk):
        for fold in range(chunk.start // width, (chunk.start + 2 * chunk.half) // width):

            def inner_cols(cols, fold=fold):
                inner_low = r["wide"][pl.ds((folds + fold) * block_len, block_len), cols]
                r["work"][pl.ds(inner_base + fold * width, width), cols] = nn(
                    r["hidden_t"][...], inner_low
                ).astype(jnp.bfloat16)

            by_blocks(width, inner_cols)

    def output_piece():
        def output_cols(cols):
            r["work"][pl.ds(rest_base, width), cols] = nn(r["attn_t"][...], r["mixed_low"][:, cols]).astype(
                jnp.bfloat16
            )

        by_blocks(width, output_cols)

    def between(pair):
        if 0 < pair <= total.phases:
            vec.end(pair - 1)
        if pair < total.phases:
            vec.start(pair)
        for c, stage in later[pair]:
            total.step(c, stage)

    def one_pair(pair, carry):
        buf = lax.rem(pair, 2)

        @pl.when(pair + 1 < pairs)
        def _():
            probs_copy(pair + 1, 1 - buf).start()

        probs_copy(pair, buf).wait()
        back_of_pair(pair, buf, r)
        for at in range(pairs):
            pl.when(pair == at)(functools.partial(between, at))
        return carry

    def turn_tokens(rows):
        r["xt_key"][:, rows] = r["x"][rows, :].T

    def turn_tables(rows):
        r["xt_key"][:, pl.ds(pl.multiple_of(ext_len + rows.start, PAIR), rows.size)] = r["to_table"][rows, :].T
        r["xt_query"][:, pl.ds(pl.multiple_of(block_len + rows.start, PAIR), rows.size)] = (
            r["from_table"][rows, :].T
        )

    def turn():
        by_blocks(ext_len, turn_tokens)
        by_blocks(2 * SPAN, turn_tables)
        r["xt_query"][:, pl.ds(0, block_len)] = r["xt_key"][:, pl.ds(SPAN, block_len)]

    def query_cols(cols):
        r["work"][pl.ds(rest_base + width, width), cols] = nn(r["xt_query"][...], r["dq"][:, cols]).astype(jnp.bfloat16)

    def key_cols(cols):
        r["work"][pl.ds(rest_base + 2 * width, width), cols] = nn(
            r["xt_key"][...], r["dk"][:, cols]
        ).astype(jnp.bfloat16)

    def value_cols(cols):
        r["work"][pl.ds(rest_base + 3 * width, width), cols] = nn(
            r["xt_key"][:, pl.ds(0, ext_len)], r["dv"][:, cols]
        ).astype(jnp.bfloat16)

    def table_cols(cols):
        r["table"][pl.ds(0, 2 * SPAN), cols] = nt(
            r["dk"][pl.ds(ext_len, 2 * SPAN), :], r["w_key"][cols, :]
        ).astype(jnp.bfloat16)
        r["table"][pl.ds(2 * SPAN, 2 * SPAN), cols] = nt(
            r["dq"][pl.ds(block_len, 2 * SPAN), :], r["w_query"][cols, :]
        ).astype(jnp.bfloat16)

    def bucket_cols(cols):
        r["work"][pl.ds(rest_base + 4 * width, 2 * SPAN), cols] = nn(
            r["hot"][...], r["table"][:, cols]
        ).astype(jnp.bfloat16)

    def halo_cols(cols):
        for at in (0, ext_len - SPAN):
            rows = pl.ds(at, SPAN)
            grad = nt(r["dk"][rows, :], r["w_key"][cols, :]) + nt(r["dv"][rows, :], r["w_value"][cols, :])
            r["halo"][rows, cols] = grad.astype(jnp.bfloat16)

    def own_cols(cols):
        own, mid = pl.ds(0, block_len), pl.ds(SPAN, block_len)
        r["own_grad"][:, cols] = (
            r["resid"][:, cols]
            + nt(r["dq"][own, :], r["w_query"][cols, :])
            + nt(r["dk"][mid, :], r["w_key"][cols, :])
            + nt(r["dv"][mid, :], r["w_value"][cols, :])
        )

    halos = [
        pltpu.make_async_remote_copy(
            src_ref=r["halo"].at[pl.ds(at, SPAN)], dst_ref=r["halo_got"].at[number],
            send_sem=r["halo_send"].at[number], recv_sem=r["halo_recv"].at[number],
            device_id=device, device_id_type=MESH,
        )
        for number, (at, device) in enumerate(((0, before), (ext_len - SPAN, after)))
    ]

    early = [chunk for chunk in chunks if chunk.which != "rest"]
    later = schedule[len(early) + 2 :]

    def advance(steps):
        for c, stage in steps:
            total.step(c, stage)

    advance(schedule[0])
    for name in ("outer_low", "hidden_low"):
        loads[name].wait()
    for copy in wide_loads["active"]:
        copy.wait()
    r["hidden_t"][...] = r["hidden_low"][...].T
    fresh = True
    for number, chunk in enumerate(early):
        if chunk.which == "inner" and fresh:
            for copy in wide_loads["inner_low"]:
                copy.wait()
            fresh = False
        (inner_piece if chunk.which == "inner" else outer_piece)(chunk)
        advance(schedule[number + 1])
    for name in ("mixed_low", "attn_t"):
        loads[name].wait()
    output_piece()
    advance(schedule[len(early) + 1])
    for name in SOONER:
        loads[name].wait()
    lax.fori_loop(0, pairs, one_pair, 0)
    for name in LATER:
        loads[name].wait()
    turn()
    pieces = ((query_cols,), (key_cols,), (value_cols,), (table_cols, bucket_cols), (halo_cols,), (own_cols,))
    for piece, steps in zip(pieces, later[pairs:]):
        for body in piece:
            by_blocks(width, body)
        if piece[0] is halo_cols:
            for copy in halos:
                copy.start()
        advance(steps)
    for copy in halos:
        copy.wait()
    grad = r["own_grad"][...]
    for number in range(2):
        grad = grad + r["halo_got"][number].astype(jnp.float32)
    outs["tokens_grad"][...] = grad.astype(jnp.bfloat16)
    outs["vectors"][...] = vec.acc[total.phases]


CHUNKS = (
    ("outer", 2, False),
    ("outer", 2, False),
    ("outer", 2, True),
    ("inner", 3, False),
    ("inner", 3, False),
    ("rest", 1, True),
    ("rest", 2, False),
    ("rest", 1, True),
    ("rest", 1, False),
    ("rest", 1, True),
    ("rest", 1, False),
)
SCHEDULE = (
    (),
    ((0, 0),),
    ((1, 0),),
    ((0, 1), (2, 0),),
    ((3, 0),),
    (),
    ((2, 1), (4, 0), (0, 2), (5, 0), (3, 1),),
    ((0, 3), (1, 1), (5, 1),),
    ((0, 4), (3, 2),),
    ((1, 2), (0, 5), (3, 3), (4, 1), (5, 2),),
    ((3, 4), (0, 6), (1, 3),),
    ((4, 2), (3, 5), (2, 2), (0, 7),),
    ((4, 3),),
    ((0, 8), (6, 0), (3, 6),),
    ((7, 0), (1, 4), (6, 1), (4, 4), (7, 1),),
    ((1, 5), (8, 0), (3, 7), (9, 0), (5, 3), (2, 3), (9, 1), (6, 2),),
    ((8, 1), (10, 0), (5, 4), (7, 2), (4, 5), (10, 1), (1, 6), (6, 3), (8, 2), (5, 5), (2, 4), (7, 3), (10, 2), (3, 8), (8, 3), (9, 2), (7, 4), (6, 4), (10, 3), (8, 4), (5, 6), (0, 9), (2, 5), (1, 7), (9, 3), (4, 6), (10, 4), (6, 5), (2, 6), (5, 7), (7, 5), (1, 8), (9, 4), (6, 6), (7, 6), (4, 7), (8, 5), (2, 7), (8, 6), (9, 5), (10, 5), (1, 9), (6, 7), (0, 10), (5, 8), (9, 6), (4, 8), (8, 7), (9, 7), (6, 8), (1, 10), (10, 6), (3, 9), (5, 9), (7, 7), (2, 8), (9, 8), (10, 7), (8, 8), (7, 8), (10, 8), (5, 10),),
    ((6, 9), (10, 9), (6, 10), (10, 10), (2, 9), (2, 10), (8, 9), (8, 10), (4, 9), (9, 9), (4, 10), (7, 9),),
    ((7, 10), (3, 10), (9, 10),),
)

def finish(inputs, seq_count):
    width = inputs["q"].shape[1]
    block_len, ext_len = inputs["q"].shape[0], inputs["k"].shape[0]
    inner_width = inputs["active"].shape[1]
    chunks, rows = chunks_of(CHUNKS, PACK * 2 * seq_count, width)
    sems = len(chunks) * Sum.last
    rest_rows = rows - 2 * inner_width
    bf = lambda *shape: pltpu.VMEM(shape, jnp.bfloat16)
    f32 = lambda *shape: pltpu.VMEM(shape, jnp.float32)
    dma = pltpu.SemaphoreType.DMA
    vec_shape = inputs["vectors"].shape
    any_spec = pl.BlockSpec(memory_space=pl.ANY)
    vmem = pl.BlockSpec(memory_space=pltpu.VMEM)
    tiles = block_len // TILE
    held = SOONEST + SOONER + LATER
    return pl.pallas_call(
        functools.partial(finish_kernel, chunks, SCHEDULE, seq_count),
        in_specs=[vmem if name == "vectors" else any_spec for name in FINISH_IN],
        out_specs=[any_spec] * 3 + [vmem] * 2,
        out_shape=[
            jax.ShapeDtypeStruct((inner_width, width), jnp.bfloat16),
            jax.ShapeDtypeStruct((width, inner_width), jnp.bfloat16),
            jax.ShapeDtypeStruct((rest_rows, width), jnp.bfloat16),
            jax.ShapeDtypeStruct(vec_shape, jnp.float32),
            jax.ShapeDtypeStruct((block_len, width), jnp.bfloat16),
        ],
        scratch_shapes=[
            bf(2, 2, tiles, REACH, TILE), bf(PAIR, block_len), bf(PAIR, ext_len),
            f32(ext_len, PAIR), f32(ext_len, PAIR), f32(PAIR, 2 * SPAN), f32(PAIR, 2 * SPAN + 2 * TILE),
            bf(2 * block_len * (inner_width // width), width), bf(ext_len, width), bf(rows, width),
            bf(4 * SPAN, width), bf(width, block_len + 2 * SPAN), bf(width, ext_len + 2 * SPAN),
            bf(width, block_len), bf(ext_len, width), bf(2, SPAN, width), f32(block_len, width), bf(rows, width),
            f32(Sum.phases + 1, *vec_shape), f32(Sum.phases, *vec_shape),
            dma((len(chunks),)), dma((sems,)), dma((sems,)), dma((Sum.phases,)), dma((Sum.phases,)),
            dma((2,)), dma((2,)), dma((2,)), dma((len(held),)), dma((2 * (inner_width // width),)),
            *(pltpu.VMEM(inputs[name].shape, inputs[name].dtype) for name in held),
        ],
        compiler_params=pltpu.CompilerParams(
            collective_id=0, has_side_effects=True, vmem_limit_bytes=61 * 2**20
        ),
        name="finish",
    )(*(inputs[name] for name in FINISH_IN))


WIDEN_STEP = 512


def widen_pieces(shapes):
    pieces = []
    for number, (rows, cols) in enumerate(shapes):
        step = WIDEN_STEP * shapes[0][1] // cols
        pieces += [(number, at, min(step, rows - at)) for at in range(0, rows, step)]
    return pieces


def widen_kernel(shapes, splits, vec_rows, kept, *refs):
    count, total = len(shapes), len(splits)
    ins, vec_in, kept_in = refs[:count], refs[count], refs[count + 1 : count + 1 + kept]
    refs = refs[count + 1 + kept :]
    outs, vec_outs, kept_outs = refs[:total], refs[total : total + vec_rows], refs[total + vec_rows :][:kept]
    scratch = refs[total + vec_rows + kept :]
    narrow, wide = scratch[:count], scratch[count : 2 * count]
    held, (load_sem, store_sem, kept_sem) = scratch[2 * count : 2 * count + kept], scratch[2 * count + kept :]
    pieces = widen_pieces(shapes)
    loads = [
        pltpu.make_async_copy(
            ins[number].at[pl.ds(at, rows)], narrow[number].at[pl.ds(at, rows)], load_sem.at[i]
        )
        for i, (number, at, rows) in enumerate(pieces)
    ]
    for load in loads:
        load.start()
    fetches = [pltpu.make_async_copy(kept_in[i], held[i], kept_sem.at[i]) for i in range(kept)]
    stores = [pltpu.make_async_copy(held[i], kept_outs[i], kept_sem.at[i]) for i in range(kept)]
    for fetch in fetches:
        fetch.start()
    for number in range(vec_rows):
        vec_outs[number][...] = vec_in[number, :]
    for fetch, store in zip(fetches, stores):
        fetch.wait()
        store.start()
    for load, (number, at, rows) in zip(loads, pieces):
        load.wait()
        cols = shapes[number][1]
        step = 32 if cols <= 1024 else 16

        def body(i, carry, number=number, at=at, step=step):
            here = pl.ds(pl.multiple_of(at + i * step, PACK), step)
            wide[number][here, :] = narrow[number][here, :].astype(jnp.float32)
            return carry

        lax.fori_loop(0, rows // step, body, 0)
        for out, (source, first, high) in enumerate(splits):
            low_row, high_row = max(at, first), min(at + rows, first + high)
            if source == number and low_row < high_row:
                store = pltpu.make_async_copy(
                    wide[number].at[pl.ds(low_row, high_row - low_row)],
                    outs[out].at[pl.ds(low_row - first, high_row - low_row)],
                    store_sem.at[len(stores) - kept],
                )
                store.start()
                stores.append(store)
    for store in stores:
        store.wait()


def widen(arrays, splits, vectors, vec_rows, kept):
    shapes = [a.shape for a in arrays]
    pieces = widen_pieces(shapes)
    any_spec = pl.BlockSpec(memory_space=pl.ANY)
    vmem = pl.BlockSpec(memory_space=pltpu.VMEM)
    dma = pltpu.SemaphoreType.DMA
    width = vectors.shape[1]
    return pl.pallas_call(
        functools.partial(widen_kernel, shapes, splits, vec_rows, len(kept)),
        in_specs=[any_spec] * len(arrays) + [vmem] + [any_spec] * len(kept),
        out_specs=[any_spec] * len(splits) + [vmem] * vec_rows + [any_spec] * len(kept),
        out_shape=[
            *(jax.ShapeDtypeStruct((rows, shapes[number][1]), jnp.float32) for number, _, rows in splits),
            *(jax.ShapeDtypeStruct((width,), jnp.float32) for _ in range(vec_rows)),
            *(jax.ShapeDtypeStruct(a.shape, a.dtype) for a in kept),
        ],
        scratch_shapes=[
            *(pltpu.VMEM(shape, jnp.bfloat16) for shape in shapes),
            *(pltpu.VMEM(shape, jnp.float32) for shape in shapes),
            *(pltpu.VMEM(a.shape, a.dtype) for a in kept),
            dma((len(pieces),)), dma((len(pieces) + len(splits),)), dma((len(kept),)),
        ],
        compiler_params=pltpu.CompilerParams(vmem_limit_bytes=60 * 2**20),
        name="widen",
    )(*arrays, vectors, *kept)


def shifted(shard, axis, by):
    count = lax.axis_size(axis)
    pairs = [(i, i + by) for i in range(count) if 0 <= i + by < count]
    return lax.ppermute(shard, axis, pairs)


def f32dot(spec, left, right):
    return jnp.einsum(spec, left, right, preferred_element_type=jnp.float32)


def low(values):
    return values.astype(jnp.bfloat16)

def finish_plain(inputs):
    query, key_ext, value_ext = inputs["q"], inputs["k"], inputs["v"]
    block_len, width = query.shape
    w_query, w_key, w_value, hot = (inputs[name] for name in ("w_query", "w_key", "w_value", "hot"))
    dquery, dkey, dvalue, drelk, drelq = attend_back(
        query, key_ext, value_ext, inputs["grad"], inputs["probs_out"], inputs["relk"], inputs["relq"]
    )
    dkey = low(f32dot("ab,nbd->nad", unit(True), low(dkey).reshape(-1, TILE, width))).reshape(-1, width)
    dvalue = low(dvalue)
    drelk = low(drelk).T
    drelq = low(drelq[:, TILE : TILE + 2 * SPAN]).T
    query_part = f32dot("em,md->ed", jnp.concatenate([inputs["x"][SPAN : SPAN + block_len], inputs["from_table"]]).T, jnp.concatenate([dquery, drelq]))
    key_part = f32dot("em,md->ed", jnp.concatenate([inputs["x"], inputs["to_table"]]).T, jnp.concatenate([dkey, drelk]))
    value_part = f32dot("em,md->ed", inputs["x"].T, dvalue)
    table = jnp.concatenate(
        [low(f32dot("md,ed->me", drelk, w_key)), low(f32dot("md,ed->me", drelq, w_query))]
    )
    table_part = f32dot("rm,me->re", hot, table)
    output_part = f32dot("dt,te->de", inputs["attn_t"], inputs["mixed_low"])
    rest = low(jnp.concatenate([output_part, query_part, key_part, value_part, table_part]))
    outer_part = low(f32dot("tf,td->fd", inputs["active"], inputs["outer_low"]))
    inner_part = low(f32dot("td,tf->df", inputs["hidden_low"], inputs["inner_low"]))
    ext_grad = f32dot("td,ed->te", dkey, w_key) + f32dot("td,ed->te", dvalue, w_value)
    tokens_grad = (
        inputs["resid"]
        + f32dot("td,ed->te", dquery, w_query)
        + ext_grad[SPAN : SPAN + block_len]
        + shifted(low(ext_grad[:SPAN]), "seq", -1).astype(jnp.float32)
        + shifted(low(ext_grad[SPAN + block_len :]), "seq", 1).astype(jnp.float32)
    )
    both = ("rows", "seq")
    sums = [
        lax.all_gather(
            lax.psum_scatter(part, both, scatter_dimension=0, tiled=True), both, axis=0, tiled=True
        )
        for part in (outer_part, inner_part, rest)
    ]
    return (*sums, lax.psum(inputs["vectors"], both), low(tokens_grad))


def finish_of(inputs):
    seq_count, rows_count = lax.axis_size("seq"), lax.axis_size("rows")
    if rows_count == 2 and seq_count == 16:
        return finish(inputs, seq_count)
    return finish_plain(inputs)

def shards(
    tokens, cotangent, w_query, w_key, w_value, w_output, w_inner, w_outer, rel_table,
    mid_gain, mid_bias, end_gain, end_bias, seq_lengths, pad_mask, rel_buckets,
):
    width = tokens.shape[-1]
    inputs = {
        "tokens": tokens[0], "cotangent": cotangent[0], "rel_table": rel_table, "w_query": w_query,
        "w_key": w_key, "w_value": w_value, "w_output": w_output, "w_inner": w_inner, "w_outer": w_outer,
        "rel_buckets": rel_buckets, "mid_gain": mid_gain, "mid_bias": mid_bias, "end_gain": end_gain,
        "end_bias": end_bias, "keep": pad_mask.reshape(-1, TILE), "lengths": seq_lengths,
    }
    kept = start(inputs, lax.axis_size("seq"))
    layer_out = kept.pop("layer_out")
    inputs.update(kept)
    outer_w, inner_w, rest_w, norm_parts, tokens_grad = finish_of(inputs)
    splits = [(0, 0, outer_w.shape[0]), (1, 0, width)]
    splits += [(2, at * width, width) for at in range(4)] + [(2, 4 * width, rest_w.shape[0] - 4 * width)]
    values = widen([outer_w, inner_w, rest_w], splits, norm_parts, 4, [layer_out, tokens_grad])
    outer_w, inner_w, output_w, query_w, key_w, value_w, table_w, *norms = values
    *norms, layer_out, tokens_grad = norms
    return (
        layer_out[None], tokens_grad[None], query_w, key_w, value_w, output_w, inner_w, outer_w, table_w,
        *norms,
    )


def solution(mesh):
    split = P("rows", "seq", None)
    return jax.shard_map(
        shards,
        mesh=mesh,
        in_specs=(split, split) + (P(),) * 11 + (P("rows", None), P("rows", None), P()),
        out_specs=(split, split) + (P(),) * 11,
        check_vma=False,
    )
```

```python
import functools
import math

import jax
import jax.numpy as jnp
from jax import lax
from jax.experimental import pallas as pl
from jax.experimental.pallas import tpu as pltpu
from jax.sharding import PartitionSpec as P

H = 12
DH = 64
SPAN = 256
TILE = 128
REACH = 640
PAIR = 128
score_scale = 1.0 / math.sqrt(3 * DH)


def nt(left, right):
    return lax.dot_general(left, right, (((1,), (1,)), ((), ())), preferred_element_type=jnp.float32)


def nn(left, right):
    return lax.dot_general(left, right, (((1,), (0,)), ((), ())), preferred_element_type=jnp.float32)


def head_lanes(values, head):
    lane = lax.broadcasted_iota(jnp.int32, values.shape, 1)
    mine = (lane < DH) if head == 0 else (lane >= DH)
    return jnp.where(mine, values, jnp.zeros_like(values))


def unit(reverse):
    row = lax.broadcasted_iota(jnp.int32, (TILE, TILE), 0)
    col = lax.broadcasted_iota(jnp.int32, (TILE, TILE), 1)
    hit = (row + col == TILE - 1) if reverse else (row == col)
    return jnp.where(hit, 1.0, 0.0).astype(jnp.bfloat16)


def attend_back_kernel(
    q_ref, k_ref, v_ref, grad_ref, prob_ref, relk_ref, relq_ref,
    dq_ref, dk_ref, dv_ref, drelk_ref, drelq_ref, qt_ref, kt_ref,
):
    swap = unit(True)
    for source, result in ((q_ref, qt_ref), (k_ref, kt_ref)):
        for at in range(0, source.shape[0], TILE):
            flipped = nn(swap, source[pl.ds(at, TILE), :])
            result[:, pl.ds(at, TILE)] = flipped.T.astype(jnp.bfloat16)
    row = lax.broadcasted_iota(jnp.int32, (TILE, TILE), 0)
    col = lax.broadcasted_iota(jnp.int32, (TILE, TILE), 1)
    parts = REACH // TILE
    tiles = q_ref.shape[0] // TILE
    dk_ref[...] = jnp.zeros_like(dk_ref)
    dv_ref[...] = jnp.zeros_like(dv_ref)
    drelk_ref[...] = jnp.zeros_like(drelk_ref)
    drelq_ref[...] = jnp.zeros_like(drelq_ref)
    for tile in range(tiles):
        first = tile * TILE
        q_tile = q_ref[pl.ds(first, TILE), :]
        grad_tile = grad_ref[pl.ds(first, TILE), :]
        v_tile = v_ref[pl.ds(first, REACH), :]
        q_heads = [head_lanes(q_tile, head) for head in range(2)]
        grad_heads = [head_lanes(grad_tile, head) for head in range(2)]
        dq_heads = []
        lefts = [[] for _ in range(parts)]
        for head in range(2):
            lanes = pl.ds(head * DH, DH)
            probs = prob_ref[head, tile].astype(jnp.float32)
            weighted = probs * nt(v_tile, grad_heads[head])
            delta = jnp.sum(weighted, axis=0, keepdims=True)
            dscore = ((weighted - probs * delta) * score_scale).astype(jnp.bfloat16)
            turned = nt(swap, dscore)
            dband = pltpu.roll(turned, REACH - TILE + 1, 1, stride=1, stride_axis=0)
            dband = dband[:, : 2 * SPAN].astype(jnp.bfloat16)
            dq_heads.append(
                nn(turned.astype(jnp.bfloat16), k_ref[pl.ds(first, REACH), :])
                + nn(dband, relk_ref[...])
            )
            drelk_ref[lanes, :] += nn(qt_ref[lanes, pl.ds(first, TILE)], dband)
            for part in range(parts):
                flipped = nn(swap, dscore[part * TILE : (part + 1) * TILE, :])
                spun = pltpu.roll(flipped, 0, 1, stride=1, stride_axis=0)
                low = jnp.where(col >= row, spun, 0.0)
                dfrom = jnp.concatenate([low, spun - low], axis=1).astype(jnp.bfloat16)
                window = pl.ds((parts - 1 - part) * TILE, 2 * TILE)
                drelq_ref[lanes, window] += nn(kt_ref[lanes, pl.ds(first + part * TILE, TILE)], dfrom)
                lefts[part] += [flipped.astype(jnp.bfloat16), dfrom]
        dq_turned = jnp.where(col < DH, dq_heads[0], dq_heads[1]).astype(jnp.bfloat16)
        dq_ref[pl.ds(first, TILE), :] = nn(swap, dq_turned).astype(dq_ref.dtype)
        dv_ref[pl.ds(first, REACH), :] += nn(
            jnp.concatenate([prob_ref[0, tile], prob_ref[1, tile]], axis=1),
            jnp.concatenate(grad_heads, axis=0),
        )
        for part in range(parts):
            window = relq_ref[pl.ds((parts - 1 - part) * TILE, 2 * TILE), :]
            right = jnp.concatenate(
                [q_heads[0], head_lanes(window, 0), q_heads[1], head_lanes(window, 1)], axis=0
            )
            dk_ref[pl.ds(first + part * TILE, TILE), :] += nn(
                jnp.concatenate(lefts[part], axis=1), right
            )


def attend_back(query, key_ext, value_ext, grad, probs, relk, relq):
    block_len, width = query.shape
    ext_len = key_ext.shape[0]
    tiles = block_len // TILE
    pairs = width // PAIR
    table = 2 * SPAN
    cols = lambda n: pl.BlockSpec((n, PAIR), lambda p: (0, p))
    rows = lambda n: pl.BlockSpec((PAIR, n), lambda p: (p, 0))
    f32 = lambda *s: jax.ShapeDtypeStruct(s, jnp.float32)
    return pl.pallas_call(
        attend_back_kernel,
        grid=(pairs,),
        in_specs=[
            cols(block_len), cols(ext_len), cols(ext_len), cols(block_len),
            pl.BlockSpec((2, tiles, REACH, TILE), lambda p: (p, 0, 0, 0)),
            cols(table), cols(table + 2 * TILE),
        ],
        out_specs=[cols(block_len), cols(ext_len), cols(ext_len), rows(table), rows(table + 2 * TILE)],
        out_shape=[
            jax.ShapeDtypeStruct((block_len, width), jnp.bfloat16),
            f32(ext_len, width), f32(ext_len, width), f32(width, table), f32(width, table + 2 * TILE),
        ],
        scratch_shapes=[
            pltpu.VMEM((PAIR, block_len), jnp.bfloat16), pltpu.VMEM((PAIR, ext_len), jnp.bfloat16),
        ],
        compiler_params=pltpu.CompilerParams(vmem_limit_bytes=48 * 2**20),
        name="attend_back",
    )(query, key_ext, value_ext, grad, probs, relk, relq)


MESH = pl.DeviceIdType.MESH
PACK = 16


norm_eps = 1e-07
masked_score = -1e30
inverse_root_two = math.sqrt(0.5)
density_at_zero = 1.0 / math.sqrt(2.0 * math.pi)


def gelu_both(values):
    size = jnp.abs(values) * inverse_root_two
    t = 1.0 / (1.0 + 0.3275911 * size)
    poly = 1.061405429 * t - 1.453152027
    poly = poly * t + 1.421413741
    poly = poly * t - 0.284496736
    poly = poly * t + 0.254829592
    bell = jnp.exp(-size * size)
    tail = 0.5 * poly * t * bell
    share = jnp.where(values >= 0.0, 1.0 - tail, tail)
    return values * share, share + values * bell * density_at_zero


def mean_of(values):
    return jnp.mean(values, axis=-1, keepdims=True)


def by_blocks(width, body, step=256, unroll=3):
    def one(i, carry):
        body(pl.ds(pl.multiple_of(i * step, step), step))
        return carry

    lax.fori_loop(0, width // step, one, 0, unroll=unroll)


def column_of(row_values):
    row = lax.broadcasted_iota(jnp.int32, (TILE, TILE), 0)
    col = lax.broadcasted_iota(jnp.int32, (TILE, TILE), 1)
    return jnp.sum(jnp.where(row == col, row_values, 0), axis=1, keepdims=True)


def mask_of(r, seq_count):
    ext_len, block_len = r["bias"].shape
    place = lax.axis_index("seq")
    row_len = block_len * seq_count
    ends, end = [], 0
    for number in range(r["lengths"].shape[1]):
        end = end + r["lengths"][0, number]
        ends.append(end)

    def segment(slots):
        return sum((slots >= end).astype(jnp.int32) for end in ends)

    query = place * block_len + lax.broadcasted_iota(jnp.int32, (1, block_len), 1)
    query_segment = segment(query)
    for block in range(ext_len // TILE):
        first = place * block_len - SPAN + block * TILE
        line = lax.clamp(0, place * (block_len // TILE) - SPAN // TILE + block, row_len // TILE - 1)
        keep = column_of(r["keep"][pl.ds(line, 1), :])
        key = first + lax.broadcasted_iota(jnp.int32, (TILE, 1), 0)
        key_segment = jnp.where((key >= 0) & (key < row_len), segment(key), -1)
        apart = key - query
        seen = (key_segment == query_segment) & (jnp.abs(apart) < SPAN)
        seen = seen & ((keep == 1) | (apart == 0))
        r["bias"][pl.ds(block * TILE, TILE), :] = jnp.where(seen, 0.0, masked_score)


def score_part(r, pair, tile, head, part, q_head, to_term):
    lanes = pl.ds(pl.multiple_of(pair * PAIR, PAIR), PAIR)
    first = tile * TILE
    at = first + part * TILE
    k_part = r["k"][pl.ds(at, TILE), lanes]
    window = r["relq"][pl.ds((REACH // TILE - 1 - part) * TILE, 2 * TILE), lanes]
    from_band = nt(head_lanes(k_part, head), window)
    from_term = pltpu.roll(from_band, TILE + 1, 1, stride=1, stride_axis=0)[:, :TILE]
    left = jnp.concatenate([k_part, unit(False)], axis=1)
    right = jnp.concatenate([q_head, to_term], axis=1)
    r["scores"][pair, tile, head, pl.ds(part * TILE, TILE), :] = (
        nt(left, right) + from_term + r["bias"][pl.ds(at, TILE), pl.ds(first, TILE)]
    )


def parts_of(tile, block_len):
    first = SPAN // TILE - tile
    own = range(first, first + block_len // TILE)
    return own, [part for part in range(REACH // TILE) if part not in own]


def attend_own(pair, r):
    lanes = pl.ds(pl.multiple_of(pair * PAIR, PAIR), PAIR)
    block_len = r["q"].shape[0]
    for tile in range(block_len // TILE):
        q_tile = r["q"][pl.ds(tile * TILE, TILE), lanes]
        for head in range(2):
            q_head = head_lanes(q_tile, head)
            band = nt(q_head, r["relk"][:, lanes])
            band = jnp.concatenate([band, jnp.zeros((TILE, REACH - 2 * SPAN), jnp.float32)], axis=1)
            to_term = pltpu.roll(band, 0, 1, stride=1, stride_axis=0).astype(jnp.bfloat16)
            r["to_terms"][pair, tile, head] = to_term
            for part in parts_of(tile, block_len)[0]:
                score_part(r, pair, tile, head, part, q_head, to_term[:, part * TILE : (part + 1) * TILE])


def attend_rest(pair, buf, r):
    log_two = score_scale * math.log2(math.e)
    lanes = pl.ds(pl.multiple_of(pair * PAIR, PAIR), PAIR)
    block_len = r["q"].shape[0]
    for at in range(0, r["v"].shape[0], TILE):
        r["vt"][:, pl.ds(at, TILE)] = r["v"][pl.ds(at, TILE), lanes].T
    for tile in range(block_len // TILE):
        first = tile * TILE
        q_tile = r["q"][pl.ds(first, TILE), lanes]
        outs = []
        for head in range(2):
            q_head = head_lanes(q_tile, head)
            for part in parts_of(tile, block_len)[1]:
                to_term = r["to_terms"][pair, tile, head, :, pl.ds(part * TILE, TILE)]
                score_part(r, pair, tile, head, part, q_head, to_term)
            scores = r["scores"][pair, tile, head]
            top = jnp.max(scores, axis=0, keepdims=True)
            weights = jnp.exp2((scores - top) * log_two)
            total = jnp.sum(weights, axis=0, keepdims=True)
            probs = (weights * (1.0 / total)).astype(jnp.bfloat16)
            r["probs"][buf, head, tile] = probs
            outs.append(nn(r["vt"][pl.ds(head * DH, DH), pl.ds(first, REACH)], probs))
        both = jnp.concatenate(outs, axis=0)
        r["attn_t"][lanes, pl.ds(first, TILE)] = both.astype(jnp.bfloat16)
        r["attn"][pl.ds(first, TILE), lanes] = both.T.astype(jnp.bfloat16)


START_HBM = (
    "tokens", "rel_table", "w_query", "w_key", "w_value", "w_output", "w_inner", "w_outer", "cotangent",
)
START_VMEM = ("rel_buckets", "mid_gain", "mid_bias", "end_gain", "end_bias", "keep")
START_IN = START_HBM + START_VMEM + ("lengths",)
START_KEPT = (
    "x", "q", "k", "v", "relk", "relq", "to_table", "from_table", "hot", "grad", "resid",
    "active", "inner_low", "outer_low", "hidden_low", "mixed_low", "attn_t",
)
START_OUT = START_KEPT + ("probs_out", "layer_out", "vectors")
START_SCRATCH = START_KEPT + (
    "rel_table", "w_query", "w_key", "w_value", "w_output", "w_inner", "w_outer", "cotangent",
    "bias", "vt", "scores", "to_terms", "probs", "attn", "mixed", "hidden", "z_mid", "root_mid", "slope", "sum_grad",
    "load_sem", "keep_sem", "probs_sem", "send_sem", "recv_sem",
)


def start_kernel(seq_count, *refs):
    given = dict(zip(START_IN, refs))
    outs = dict(zip(START_OUT, refs[len(START_IN) :]))
    r = dict(zip(START_SCRATCH, refs[len(START_IN) + len(START_OUT) :]))
    r.update((name, given[name]) for name in START_VMEM + ("lengths",))
    block_len, width = r["q"].shape
    ext_len, table_len = r["x"].shape[0], r["to_table"].shape[0]
    inner_width = r["w_inner"].shape[1]
    pairs = width // PAIR
    own = pl.ds(SPAN, block_len)

    loads = {}
    for number, name in enumerate(START_HBM):
        target = r["x"].at[own] if name == "tokens" else r[name]
        loads[name] = pltpu.make_async_copy(given[name], target, r["load_sem"].at[number])
        loads[name].start()
    row, place = lax.axis_index("rows"), lax.axis_index("seq")
    before = {"rows": row, "seq": lax.rem(place + seq_count - 1, seq_count)}
    after = {"rows": row, "seq": lax.rem(place + 1, seq_count)}
    barrier = pltpu.get_barrier_semaphore()
    for device in (before, after):
        pl.semaphore_signal(barrier, inc=1, device_id=device, device_id_type=MESH)
    pl.semaphore_wait(barrier, 2)
    halos = [
        pltpu.make_async_remote_copy(
            src_ref=given["tokens"], dst_ref=r["x"].at[pl.ds(at, SPAN)], send_sem=r["send_sem"].at[number],
            recv_sem=r["recv_sem"].at[number], device_id=device, device_id_type=MESH,
        )
        for number, (at, device) in enumerate(((0, after), (SPAN + block_len, before)))
    ]
    for copy in halos:
        copy.start()

    def keep(name):
        pltpu.make_async_copy(r[name], outs[name], r["keep_sem"].at[START_KEPT.index(name)]).start()

    def low(values):
        return values.astype(jnp.bfloat16)

    place_of = lax.broadcasted_iota(jnp.int32, (table_len, table_len), 0)
    turned_bucket = pltpu.roll(r["rel_buckets"][...].reshape(1, table_len), table_len - 1, 1)
    to_pos = jnp.clip(turned_bucket + SPAN, 0, table_len - 1)
    from_pos = jnp.clip(SPAN - turned_bucket, 0, table_len - 1)
    r["hot"][:, pl.ds(table_len, table_len)] = low(jnp.where(place_of == from_pos, 1.0, 0.0))
    to_turned = low(jnp.where(place_of == to_pos, 1.0, 0.0))
    for at in range(0, table_len, TILE):
        r["hot"][:, pl.ds(at, TILE)] = low(
            nn(to_turned[:, table_len - TILE - at : table_len - at], unit(True))
        )
    keep("hot")
    mask_of(r, seq_count)
    loads["rel_table"].wait()
    for number, name in enumerate(("to", "from")):
        hot = r["hot"][:, pl.ds(number * table_len, table_len)].T

        def table_cols(cols, hot=hot, name=name):
            r[name + "_table"][:, cols] = low(nn(hot, r["rel_table"][:, cols]))

        by_blocks(width, table_cols)
        keep(name + "_table")
    loads["w_query"].wait()
    loads["tokens"].wait()
    r["relq"][pl.ds(0, TILE), :] = jnp.zeros((TILE, width), jnp.bfloat16)
    r["relq"][pl.ds(TILE + table_len, TILE), :] = jnp.zeros((TILE, width), jnp.bfloat16)

    def query_cols(cols):
        r["q"][:, cols] = low(nn(r["x"][own, :], r["w_query"][:, cols]))
        r["relq"][pl.ds(TILE, table_len), cols] = low(nn(r["from_table"][...], r["w_query"][:, cols]))

    by_blocks(width, query_cols)
    keep("q")
    keep("relq")
    loads["w_key"].wait()

    def relk_cols(cols):
        r["relk"][:, cols] = low(nn(r["to_table"][...], r["w_key"][:, cols]))

    by_blocks(width, relk_cols)
    keep("relk")
    loads["w_value"].wait()

    def pair_rows(rows):
        def pair_cols(cols):
            r["k"][rows, cols] = low(nn(r["x"][rows, :], r["w_key"][:, cols]))
            r["v"][rows, cols] = low(nn(r["x"][rows, :], r["w_value"][:, cols]))

        by_blocks(width, pair_cols)

    pair_rows(own)

    def own_pair(pair, carry):
        attend_own(pair, r)
        return carry

    lax.fori_loop(0, pairs, own_pair, 0, unroll=2)
    for copy in halos:
        copy.wait()
    keep("x")
    pair_rows(pl.ds(0, SPAN))
    pair_rows(pl.ds(SPAN + block_len, SPAN))
    keep("k")
    keep("v")

    def probs_copy(pair, buf):
        return pltpu.make_async_copy(
            r["probs"].at[buf], outs["probs_out"].at[pl.ds(2 * pair, 2)], r["probs_sem"].at[buf]
        )

    def one_pair(pair, carry):
        buf = lax.rem(pair, 2)

        @pl.when(pair >= 2)
        def _():
            probs_copy(pair - 2, buf).wait()

        attend_rest(pair, buf, r)
        probs_copy(pair, buf).start()
        return carry

    lax.fori_loop(0, pairs, one_pair, 0)

    keep("attn_t")
    for name in ("w_output", "w_inner", "w_outer", "cotangent"):
        loads[name].wait()

    def mixed_cols(cols):
        r["mixed"][:, cols] = nn(r["attn"][...], r["w_output"][:, cols])

    by_blocks(width, mixed_cols)
    high = 64
    mid_gain, mid_bias, end_gain, end_bias = (
        r[name][...].reshape(1, width) for name in ("mid_gain", "mid_bias", "end_gain", "end_bias")
    )

    def mid_rows(rows):
        mine = pl.ds(pl.multiple_of(SPAN + rows.start, high), high)
        values = r["x"][mine, :].astype(jnp.float32) + r["mixed"][rows, :]
        centre = values - mean_of(values)
        root = lax.rsqrt(mean_of(centre * centre) + norm_eps)
        z = centre * root
        hidden = z * mid_gain + mid_bias
        r["z_mid"][rows, :] = z
        r["root_mid"][rows, :] = jnp.broadcast_to(root, (high, TILE))
        r["hidden"][rows, :] = hidden
        r["hidden_low"][rows, :] = low(hidden)

    by_blocks(block_len, mid_rows, high, 4)
    keep("hidden_low")

    def active_cols(cols):
        active, slope = gelu_both(nn(r["hidden_low"][...], r["w_inner"][:, cols]))
        r["active"][:, cols] = low(active)
        r["slope"][:, cols] = low(slope)

    by_blocks(inner_width, active_cols, unroll=12)
    keep("active")

    def outer_cols(cols):
        r["mixed"][:, cols] = nn(r["active"][...], r["w_outer"][:, cols])

    by_blocks(width, outer_cols)
    outs["vectors"][...] = jnp.zeros_like(outs["vectors"])

    def end_rows(rows):
        values = r["hidden"][rows, :] + r["mixed"][rows, :]
        centre = values - mean_of(values)
        root = lax.rsqrt(mean_of(centre * centre) + norm_eps)
        z = centre * root
        outs["layer_out"][rows, :] = low(z * end_gain + end_bias)
        cotangent = r["cotangent"][rows, :].astype(jnp.float32)
        outs["vectors"][pl.ds(2, 1), :] += jnp.sum(cotangent * z, axis=0, keepdims=True)
        outs["vectors"][pl.ds(3, 1), :] += jnp.sum(cotangent, axis=0, keepdims=True)
        grad = cotangent * end_gain
        sum_grad = root * (grad - mean_of(grad) - z * mean_of(grad * z))
        r["sum_grad"][rows, :] = sum_grad
        r["outer_low"][rows, :] = low(sum_grad)

    by_blocks(block_len, end_rows, high, 4)
    keep("outer_low")

    def inner_cols(cols):
        grad = nt(r["outer_low"][...], r["w_outer"][cols, :])
        r["inner_low"][:, cols] = low(grad * r["slope"][:, cols].astype(jnp.float32))

    by_blocks(inner_width, inner_cols, unroll=12)
    keep("inner_low")

    def hidden_cols(cols):
        r["mixed"][:, cols] = r["sum_grad"][:, cols] + nt(r["inner_low"][...], r["w_inner"][cols, :])

    by_blocks(width, hidden_cols)

    def resid_rows(rows):
        hidden_grad, z = r["mixed"][rows, :], r["z_mid"][rows, :]
        outs["vectors"][pl.ds(0, 1), :] += jnp.sum(hidden_grad * z, axis=0, keepdims=True)
        outs["vectors"][pl.ds(1, 1), :] += jnp.sum(hidden_grad, axis=0, keepdims=True)
        grad = hidden_grad * mid_gain
        root = r["root_mid"][rows, pl.ds(0, 1)]
        resid = root * (grad - mean_of(grad) - z * mean_of(grad * z))
        r["resid"][rows, :] = resid
        r["mixed_low"][rows, :] = low(resid)

    by_blocks(block_len, resid_rows, high, 4)
    keep("resid")
    keep("mixed_low")

    def grad_cols(cols):
        r["grad"][:, cols] = low(nt(r["mixed_low"][...], r["w_output"][cols, :]))

    by_blocks(width, grad_cols)
    keep("grad")
    for pair in (pairs - 2, pairs - 1):
        probs_copy(pair, pair % 2).wait()
    for number, name in enumerate(START_KEPT):
        pltpu.make_async_copy(r[name], outs[name], r["keep_sem"].at[number]).wait()


def start(inputs, seq_count):
    block_len, width = inputs["tokens"].shape
    table_len = inputs["rel_table"].shape[0]
    inner_width = inputs["w_inner"].shape[1]
    ext_len = block_len + 2 * SPAN
    tiles = block_len // TILE
    heads = 2 * (width // PAIR)
    sizes = {
        "x": (ext_len, width), "q": (block_len, width), "k": (ext_len, width), "v": (ext_len, width),
        "relk": (table_len, width), "relq": (table_len + 2 * TILE, width), "to_table": (table_len, width),
        "from_table": (table_len, width), "hot": (table_len, 2 * table_len), "grad": (block_len, width),
        "resid": (block_len, width), "active": (block_len, inner_width),
        "inner_low": (block_len, inner_width), "outer_low": (block_len, width),
        "hidden_low": (block_len, width), "mixed_low": (block_len, width), "attn_t": (width, block_len),
    }
    kinds = {name: jnp.float32 if name == "resid" else jnp.bfloat16 for name in START_KEPT}
    bf = lambda *shape: pltpu.VMEM(shape, jnp.bfloat16)
    f32 = lambda *shape: pltpu.VMEM(shape, jnp.float32)
    dma = pltpu.SemaphoreType.DMA
    any_spec = pl.BlockSpec(memory_space=pl.ANY)
    vmem = pl.BlockSpec(memory_space=pltpu.VMEM)
    smem = pl.BlockSpec(memory_space=pltpu.SMEM)
    values = pl.pallas_call(
        functools.partial(start_kernel, seq_count),
        in_specs=[any_spec] * len(START_HBM) + [vmem] * len(START_VMEM) + [smem],
        out_specs=[any_spec] * (len(START_KEPT) + 1) + [vmem] * 2,
        out_shape=[
            *(jax.ShapeDtypeStruct(sizes[name], kinds[name]) for name in START_KEPT),
            jax.ShapeDtypeStruct((heads, tiles, REACH, TILE), jnp.bfloat16),
            jax.ShapeDtypeStruct((block_len, width), jnp.bfloat16),
            jax.ShapeDtypeStruct((8, width), jnp.float32),
        ],
        scratch_shapes=[
            *(pltpu.VMEM(sizes[name], kinds[name]) for name in START_KEPT),
            *(pltpu.VMEM(inputs[name].shape, inputs[name].dtype) for name in START_HBM[1:]),
            f32(ext_len, block_len), bf(PAIR, ext_len), f32(heads // 2, tiles, 2, REACH, TILE),
            bf(heads // 2, tiles, 2, TILE, REACH), bf(2, 2, tiles, REACH, TILE),
            bf(block_len, width), f32(block_len, width), f32(block_len, width), f32(block_len, width),
            f32(block_len, TILE), bf(block_len, inner_width), f32(block_len, width),
            dma((len(START_HBM),)), dma((len(START_KEPT),)), dma((2,)), dma((2,)), dma((2,)),
        ],
        compiler_params=pltpu.CompilerParams(
            collective_id=1, has_side_effects=True, vmem_limit_bytes=60 * 2**20
        ),
        name="start",
    )(*(inputs[name] for name in START_IN))
    return dict(zip(START_OUT, values))


class Line:
    def __init__(self, side, row_step, seq_step):
        self.side = side
        row, place = lax.axis_index("rows"), lax.axis_index("seq")
        away = 1 - 2 * side
        self.device = {"rows": row + away * row_step, "seq": place + away * seq_step}


def lines_of():
    row, place = lax.axis_index("rows"), lax.axis_index("seq")
    first, second, third, fourth = (place // step % 2 for step in (1, 2, 4, 8))
    core = Line(row, 1, 0)
    near = Line(first + row * (second - first), 0, 1 + row)
    cross = Line(second + row * (first - second), 0, 2 - row)
    low_z, high_z = Line(third, 0, 4), Line(fourth, 0, 8)
    return (core, near, cross, low_z, high_z), (core, low_z, high_z, near, cross)


def add_rows(left, right, out):
    rows = out.shape[0]
    step = next(s for s in (48, 32, PACK) if rows % s == 0)

    def body(i, carry):
        here = pl.ds(pl.multiple_of(i * step, PACK), step)
        out[here, :] = left[here, :] + right[here, :]
        return carry

    lax.fori_loop(0, rows // step, body, 0)


class Chunk:
    def __init__(self, index, which, start, half, base, width, z_first):
        self.index, self.which, self.start, self.half = index, which, start, half
        self.base, self.width, self.z_first = base, width, z_first

    def out(self, refs, side):
        if self.which == "inner":
            col = (self.start // self.width + side) * self.width
            return refs["inner"].at[:, pl.ds(pl.multiple_of(col, PAIR), self.width)]
        first = pl.multiple_of(self.start + side * self.half, PACK)
        return refs[self.which].at[pl.ds(first, self.half)]


def chunks_of(spec, unit, width):
    chunks, starts, base = [], {}, 0
    for which, units, z_first in spec:
        start = starts.get(which, 0)
        chunks.append(Chunk(len(chunks), which, start, units * unit // 2, base, width, z_first))
        starts[which] = start + units * unit
        base += units * unit
    return chunks, base


class Sum:
    phases = 5
    last = 2 * phases

    def __init__(self, chunks, outs, work, recv, own_sem, send_sem, recv_sem):
        self.chunks, self.outs, self.work, self.recv = chunks, outs, work, recv
        self.own_sem, self.send_sem, self.recv_sem = own_sem, send_sem, recv_sem
        self.row = lax.axis_index("rows")
        self.plane_first, self.z_first = lines_of()

    def greet(self, more):
        barrier = pltpu.get_barrier_semaphore()
        devices = [line.device for line in self.plane_first] + more
        for device in devices:
            pl.semaphore_signal(barrier, inc=1, device_id=device, device_id_type=MESH)
        pl.semaphore_wait(barrier, len(devices))

    def lines(self, chunk):
        return self.z_first if chunk.z_first else self.plane_first

    def offset(self, chunk, phase):
        at, rows = 0, chunk.half
        for line in self.lines(chunk)[1 : phase + 1]:
            rows //= 2
            at = at + line.side * rows
        return at

    def working(self, chunk, at, rows):
        return self.work.at[pl.ds(pl.multiple_of(chunk.base + self.row * chunk.half + at, PACK), rows)]

    def received(self, chunk, phase):
        at = chunk.base + sum(chunk.half >> p for p in range(phase))
        return self.recv.at[pl.ds(at, chunk.half >> phase)]

    def summed(self, chunk, phase):
        at = pl.multiple_of(chunk.base + self.offset(chunk, phase), PACK)
        return self.recv.at[pl.ds(at, chunk.half >> phase)]

    def copies(self, chunk, stage):
        gather = stage >= self.phases
        phase = self.last - 1 - stage if gather else stage
        line, rows = self.lines(chunk)[phase], chunk.half >> phase
        local = None
        if gather:
            source = target = self.summed(chunk, phase)
            if phase == 0:
                target = chunk.out(self.outs, self.row)
                local = (source, target)
        else:
            target = self.received(chunk, phase)
            if phase == 0:
                other = chunk.base + (1 - self.row) * chunk.half
                source = self.work.at[pl.ds(pl.multiple_of(other, PACK), rows)]
            else:
                source = self.working(chunk, self.offset(chunk, phase - 1) + (1 - line.side) * rows, rows)
        sem = chunk.index * self.last + stage
        copies = [
            pltpu.make_async_remote_copy(
                src_ref=source, dst_ref=target, send_sem=self.send_sem.at[sem],
                recv_sem=self.recv_sem.at[sem], device_id=line.device, device_id_type=MESH,
            )
        ]
        if local is not None:
            copies.append(pltpu.make_async_copy(*local, self.own_sem.at[chunk.index]))
        return copies

    def step(self, c, stage):
        chunk = self.chunks[c]
        if stage > 0:
            for copy in self.copies(chunk, stage - 1):
                copy.wait()
        if 0 < stage <= self.phases:
            phase = stage - 1
            mine = self.working(chunk, self.offset(chunk, phase), chunk.half >> phase)
            add_rows(mine, self.received(chunk, phase), self.summed(chunk, phase) if stage == self.phases else mine)
        if stage < self.last:
            for copy in self.copies(chunk, stage):
                copy.start()


class VectorSum:
    def __init__(self, lines, acc, recv, send_sem, recv_sem):
        self.lines, self.acc, self.recv, self.send_sem, self.recv_sem = lines, acc, recv, send_sem, recv_sem

    def copy(self, phase):
        return pltpu.make_async_remote_copy(
            src_ref=self.acc.at[phase], dst_ref=self.recv.at[phase], send_sem=self.send_sem.at[phase],
            recv_sem=self.recv_sem.at[phase], device_id=self.lines[phase].device, device_id_type=MESH,
        )

    def start(self, phase):
        self.copy(phase).start()

    def end(self, phase):
        self.copy(phase).wait()
        self.acc[phase + 1] = self.acc[phase] + self.recv[phase]


def back_of_pair(pair, buf, r):
    swap = unit(True)
    lanes_at = pl.multiple_of(pair * PAIR, PAIR)
    lanes_here = pl.ds(lanes_at, PAIR)
    row = lax.broadcasted_iota(jnp.int32, (TILE, TILE), 0)
    col = lax.broadcasted_iota(jnp.int32, (TILE, TILE), 1)
    parts = REACH // TILE
    block_len, ext_len = r["q"].shape[0], r["k"].shape[0]
    tiles = block_len // TILE
    qt_ref, kt_ref, dk_ref, dv_ref, drelk_ref, drelq_ref = (
        r[name] for name in ("qt", "kt", "dk_pair", "dv_pair", "drelk_t", "drelq_t")
    )
    for source, result in ((r["q"], qt_ref), (r["k"], kt_ref)):
        for at in range(0, source.shape[0], TILE):
            flipped = nn(swap, source[pl.ds(at, TILE), lanes_here])
            result[:, pl.ds(at, TILE)] = flipped.T.astype(jnp.bfloat16)
    dk_ref[...] = jnp.zeros_like(dk_ref)
    dv_ref[...] = jnp.zeros_like(dv_ref)
    drelk_ref[...] = jnp.zeros_like(drelk_ref)
    drelq_ref[...] = jnp.zeros_like(drelq_ref)
    for tile in range(tiles):
        first = tile * TILE
        q_tile = r["q"][pl.ds(first, TILE), lanes_here]
        grad_tile = r["grad"][pl.ds(first, TILE), lanes_here]
        v_tile = r["v"][pl.ds(first, REACH), lanes_here]
        q_heads = [head_lanes(q_tile, head) for head in range(2)]
        grad_heads = [head_lanes(grad_tile, head) for head in range(2)]
        dq_heads = []
        lefts = [[] for _ in range(parts)]
        for head in range(2):
            lanes = pl.ds(head * DH, DH)
            probs = r["probs"][buf, head, tile].astype(jnp.float32)
            weighted = probs * nt(v_tile, grad_heads[head])
            delta = jnp.sum(weighted, axis=0, keepdims=True)
            dscore = ((weighted - probs * delta) * score_scale).astype(jnp.bfloat16)
            turned = nt(swap, dscore)
            dband = pltpu.roll(turned, REACH - TILE + 1, 1, stride=1, stride_axis=0)
            dband = dband[:, : 2 * SPAN].astype(jnp.bfloat16)
            dq_heads.append(
                nn(turned.astype(jnp.bfloat16), r["k"][pl.ds(first, REACH), lanes_here])
                + nn(dband, r["relk"][:, lanes_here])
            )
            drelk_ref[lanes, :] += nn(qt_ref[lanes, pl.ds(first, TILE)], dband)
            for part in range(parts):
                flipped = nn(swap, dscore[part * TILE : (part + 1) * TILE, :])
                spun = pltpu.roll(flipped, 0, 1, stride=1, stride_axis=0)
                near = jnp.where(col >= row, spun, 0.0)
                dfrom = jnp.concatenate([near, spun - near], axis=1).astype(jnp.bfloat16)
                window = pl.ds((parts - 1 - part) * TILE, 2 * TILE)
                drelq_ref[lanes, window] += nn(kt_ref[lanes, pl.ds(first + part * TILE, TILE)], dfrom)
                lefts[part] += [flipped.astype(jnp.bfloat16), dfrom]
        dq_turned = jnp.where(col < DH, dq_heads[0], dq_heads[1]).astype(jnp.bfloat16)
        r["dq"][pl.ds(first, TILE), lanes_here] = nn(swap, dq_turned).astype(jnp.bfloat16)
        dv_ref[pl.ds(first, REACH), :] += nn(
            jnp.concatenate([r["probs"][buf, 0, tile], r["probs"][buf, 1, tile]], axis=1),
            jnp.concatenate(grad_heads, axis=0),
        )
        for part in range(parts):
            window = r["relq"][pl.ds((parts - 1 - part) * TILE, 2 * TILE), lanes_here]
            right = jnp.concatenate(
                [q_heads[0], head_lanes(window, 0), q_heads[1], head_lanes(window, 1)], axis=0
            )
            dk_ref[pl.ds(first + part * TILE, TILE), :] += nn(
                jnp.concatenate(lefts[part], axis=1), right
            )
    r["dv"][:, lanes_here] = dv_ref[...].astype(jnp.bfloat16)
    for at in range(0, ext_len, TILE):
        r["dk"][pl.ds(at, TILE), lanes_here] = nn(
            swap, dk_ref[pl.ds(at, TILE), :].astype(jnp.bfloat16)
        ).astype(jnp.bfloat16)
    r["dk"][pl.ds(ext_len, 2 * SPAN), lanes_here] = drelk_ref[...].T.astype(jnp.bfloat16)
    r["dq"][pl.ds(block_len, 2 * SPAN), lanes_here] = (
        drelq_ref[:, pl.ds(TILE, 2 * SPAN)].T.astype(jnp.bfloat16)
    )


SOONEST = ("outer_low", "hidden_low", "mixed_low", "attn_t")
SOONER = ("q", "k", "v", "grad", "relk", "relq")
LATER = ("x", "to_table", "from_table", "w_query", "w_key", "w_value", "hot", "resid")
FINISH_IN = ("active", "inner_low") + SOONEST + SOONER + LATER + ("vectors", "probs_out")
FINISH_OUT = ("outer", "inner", "rest", "vectors", "tokens_grad")
FINISH_SCRATCH = (
    "probs", "qt", "kt", "dk_pair", "dv_pair", "drelk_t", "drelq_t", "wide", "dv", "work", "table",
    "xt_query", "xt_key", "hidden_t", "halo", "halo_got", "own_grad", "recv", "vec_acc", "vec_recv", "own_sem",
    "send_sem", "recv_sem", "vec_send", "vec_got", "probs_sem", "halo_send", "halo_recv", "load_sem", "wide_sem",
)


def finish_kernel(chunks, schedule, seq_count, *refs):
    given = dict(zip(FINISH_IN, refs))
    outs = dict(zip(FINISH_OUT, refs[len(FINISH_IN) :]))
    scratch = refs[len(FINISH_IN) + len(FINISH_OUT) :]
    r = dict(zip(FINISH_SCRATCH, scratch))
    block_len, width = given["q"].shape
    ext_len = given["k"].shape[0]
    folds = given["active"].shape[1] // width
    wide_loads = {}
    for number, name in enumerate(("active", "inner_low")):
        wide_loads[name] = [
            pltpu.make_async_copy(
                given[name].at[:, pl.ds(fold * width, width)],
                r["wide"].at[pl.ds((number * folds + fold) * block_len, block_len)],
                r["wide_sem"].at[number * folds + fold],
            )
            for fold in range(folds)
        ]
    r["dk"] = r["wide"].at[pl.ds(0, ext_len + 2 * SPAN)]
    r["dq"] = r["wide"].at[pl.ds(ext_len + 2 * SPAN, block_len + 2 * SPAN)]
    loads = {}
    for number, (name, held) in enumerate(
        zip(SOONEST + SOONER + LATER, scratch[len(FINISH_SCRATCH) :])
    ):
        loads[name] = pltpu.make_async_copy(given[name], held, r["load_sem"].at[number])
        r[name] = held
    loads["outer_low"].start()
    for copy in wide_loads["active"] + wide_loads["inner_low"]:
        copy.start()
    for name in SOONEST[1:] + SOONER + LATER:
        loads[name].start()
    pairs = width // PAIR
    total = Sum(chunks, outs, r["work"], r["recv"], r["own_sem"], r["send_sem"], r["recv_sem"])
    row, place = lax.axis_index("rows"), lax.axis_index("seq")
    before = {"rows": row, "seq": lax.rem(place + seq_count - 1, seq_count)}
    after = {"rows": row, "seq": lax.rem(place + 1, seq_count)}
    total.greet([before, after])
    vec = VectorSum(total.plane_first, r["vec_acc"], r["vec_recv"], r["vec_send"], r["vec_got"])
    vec.acc[0] = given["vectors"][...]

    def probs_copy(pair, buf):
        return pltpu.make_async_copy(
            given["probs_out"].at[pl.ds(2 * pair, 2)], r["probs"].at[buf], r["probs_sem"].at[buf]
        )

    probs_copy(0, 0).start()
    inner_base = folds * width
    rest_base = 2 * folds * width

    def outer_piece(chunk):
        def body(i, carry):
            at = pl.multiple_of(chunk.start + i * 256, 256)
            fold, col = at // width, pl.multiple_of(at % width, 256)
            active = r["wide"][pl.ds(pl.multiple_of(fold * block_len, block_len), block_len), pl.ds(col, 256)]
            r["work"][pl.ds(at, 256), :] = nn(active.T, r["outer_low"][...]).astype(jnp.bfloat16)
            return carry

        lax.fori_loop(0, 2 * chunk.half // 256, body, 0)

    def inner_piece(chunk):
        for fold in range(chunk.start // width, (chunk.start + 2 * chunk.half) // width):

            def inner_cols(cols, fold=fold):
                inner_low = r["wide"][pl.ds((folds + fold) * block_len, block_len), cols]
                r["work"][pl.ds(inner_base + fold * width, width), cols] = nn(
                    r["hidden_t"][...], inner_low
                ).astype(jnp.bfloat16)

            by_blocks(width, inner_cols)

    def output_piece():
        def output_cols(cols):
            r["work"][pl.ds(rest_base, width), cols] = nn(r["attn_t"][...], r["mixed_low"][:, cols]).astype(
                jnp.bfloat16
            )

        by_blocks(width, output_cols)

    def between(pair):
        if 0 < pair <= total.phases:
            vec.end(pair - 1)
        if pair < total.phases:
            vec.start(pair)
        for c, stage in later[pair]:
            total.step(c, stage)

    def one_pair(pair, carry):
        buf = lax.rem(pair, 2)

        @pl.when(pair + 1 < pairs)
        def _():
            probs_copy(pair + 1, 1 - buf).start()

        probs_copy(pair, buf).wait()
        back_of_pair(pair, buf, r)
        for at in range(pairs):
            pl.when(pair == at)(functools.partial(between, at))
        return carry

    def turn_tokens(rows):
        r["xt_key"][:, rows] = r["x"][rows, :].T

    def turn_tables(rows):
        r["xt_key"][:, pl.ds(pl.multiple_of(ext_len + rows.start, PAIR), rows.size)] = r["to_table"][rows, :].T
        r["xt_query"][:, pl.ds(pl.multiple_of(block_len + rows.start, PAIR), rows.size)] = (
            r["from_table"][rows, :].T
        )

    def turn():
        by_blocks(ext_len, turn_tokens)
        by_blocks(2 * SPAN, turn_tables)
        r["xt_query"][:, pl.ds(0, block_len)] = r["xt_key"][:, pl.ds(SPAN, block_len)]

    def query_cols(cols):
        r["work"][pl.ds(rest_base + width, width), cols] = nn(r["xt_query"][...], r["dq"][:, cols]).astype(jnp.bfloat16)

    def key_cols(cols):
        r["work"][pl.ds(rest_base + 2 * width, width), cols] = nn(
            r["xt_key"][...], r["dk"][:, cols]
        ).astype(jnp.bfloat16)

    def value_cols(cols):
        r["work"][pl.ds(rest_base + 3 * width, width), cols] = nn(
            r["xt_key"][:, pl.ds(0, ext_len)], r["dv"][:, cols]
        ).astype(jnp.bfloat16)

    def table_cols(cols):
        r["table"][pl.ds(0, 2 * SPAN), cols] = nt(
            r["dk"][pl.ds(ext_len, 2 * SPAN), :], r["w_key"][cols, :]
        ).astype(jnp.bfloat16)
        r["table"][pl.ds(2 * SPAN, 2 * SPAN), cols] = nt(
            r["dq"][pl.ds(block_len, 2 * SPAN), :], r["w_query"][cols, :]
        ).astype(jnp.bfloat16)

    def bucket_cols(cols):
        r["work"][pl.ds(rest_base + 4 * width, 2 * SPAN), cols] = nn(
            r["hot"][...], r["table"][:, cols]
        ).astype(jnp.bfloat16)

    def halo_cols(cols):
        for at in (0, ext_len - SPAN):
            rows = pl.ds(at, SPAN)
            grad = nt(r["dk"][rows, :], r["w_key"][cols, :]) + nt(r["dv"][rows, :], r["w_value"][cols, :])
            r["halo"][rows, cols] = grad.astype(jnp.bfloat16)

    def own_cols(cols):
        own, mid = pl.ds(0, block_len), pl.ds(SPAN, block_len)
        r["own_grad"][:, cols] = (
            r["resid"][:, cols]
            + nt(r["dq"][own, :], r["w_query"][cols, :])
            + nt(r["dk"][mid, :], r["w_key"][cols, :])
            + nt(r["dv"][mid, :], r["w_value"][cols, :])
        )

    halos = [
        pltpu.make_async_remote_copy(
            src_ref=r["halo"].at[pl.ds(at, SPAN)], dst_ref=r["halo_got"].at[number],
            send_sem=r["halo_send"].at[number], recv_sem=r["halo_recv"].at[number],
            device_id=device, device_id_type=MESH,
        )
        for number, (at, device) in enumerate(((0, before), (ext_len - SPAN, after)))
    ]

    early = [chunk for chunk in chunks if chunk.which != "rest"]
    later = schedule[len(early) + 2 :]

    def advance(steps):
        for c, stage in steps:
            total.step(c, stage)

    advance(schedule[0])
    loads["outer_low"].wait()
    for copy in wide_loads["active"]:
        copy.wait()
    fresh = True
    for number, chunk in enumerate(early):
        if chunk.which == "inner" and fresh:
            for copy in wide_loads["inner_low"]:
                copy.wait()
            loads["hidden_low"].wait()
            r["hidden_t"][...] = r["hidden_low"][...].T
            fresh = False
        (inner_piece if chunk.which == "inner" else outer_piece)(chunk)
        advance(schedule[number + 1])
    for name in ("mixed_low", "attn_t"):
        loads[name].wait()
    output_piece()
    advance(schedule[len(early) + 1])
    for name in SOONER:
        loads[name].wait()
    lax.fori_loop(0, pairs, one_pair, 0)
    for name in LATER:
        loads[name].wait()
    turn()
    pieces = ((query_cols,), (key_cols,), (value_cols,), (table_cols, bucket_cols), (halo_cols,), (own_cols,))
    for piece, steps in zip(pieces, later[pairs:]):
        for body in piece:
            by_blocks(width, body)
        if piece[0] is halo_cols:
            for copy in halos:
                copy.start()
        advance(steps)
    for copy in halos:
        copy.wait()
    grad = r["own_grad"][...]
    for number in range(2):
        grad = grad + r["halo_got"][number].astype(jnp.float32)
    outs["tokens_grad"][...] = grad.astype(jnp.bfloat16)
    outs["vectors"][...] = vec.acc[total.phases]


CHUNKS = (
    ("outer", 2, False),
    ("outer", 2, False),
    ("outer", 2, True),
    ("inner", 3, False),
    ("inner", 3, False),
    ("rest", 1, True),
    ("rest", 2, False),
    ("rest", 1, True),
    ("rest", 1, False),
    ("rest", 1, True),
    ("rest", 1, False),
)
SCHEDULE = (
    (),
    ((0, 0),),
    ((1, 0),),
    ((0, 1), (2, 0),),
    ((3, 0),),
    (),
    ((2, 1), (4, 0), (0, 2), (5, 0), (3, 1),),
    ((0, 3), (1, 1), (5, 1),),
    ((0, 4), (3, 2),),
    ((1, 2), (0, 5), (3, 3), (4, 1), (5, 2),),
    ((3, 4), (0, 6), (1, 3),),
    ((4, 2), (3, 5), (2, 2), (0, 7),),
    ((4, 3),),
    ((0, 8), (6, 0), (3, 6),),
    ((7, 0), (1, 4), (6, 1), (4, 4), (7, 1),),
    ((1, 5), (8, 0), (3, 7), (9, 0), (5, 3), (2, 3), (9, 1), (6, 2),),
    ((8, 1), (10, 0), (5, 4), (7, 2), (4, 5), (10, 1), (1, 6), (6, 3), (8, 2), (5, 5), (2, 4), (7, 3), (10, 2), (3, 8), (8, 3), (9, 2), (7, 4), (6, 4), (10, 3), (8, 4), (5, 6), (0, 9), (2, 5), (1, 7), (9, 3), (4, 6), (10, 4), (6, 5), (2, 6), (5, 7), (7, 5), (1, 8), (9, 4), (6, 6), (7, 6), (4, 7), (8, 5), (2, 7), (8, 6), (9, 5), (10, 5), (1, 9), (6, 7), (0, 10), (5, 8), (9, 6), (4, 8), (8, 7), (9, 7), (6, 8), (1, 10), (10, 6), (3, 9), (5, 9), (7, 7), (2, 8), (9, 8), (10, 7), (8, 8), (7, 8), (10, 8), (5, 10),),
    ((6, 9), (10, 9), (6, 10), (10, 10), (2, 9), (2, 10), (8, 9), (8, 10), (4, 9), (9, 9), (4, 10), (7, 9),),
    ((7, 10), (3, 10), (9, 10),),
)

def finish(inputs, seq_count):
    width = inputs["q"].shape[1]
    block_len, ext_len = inputs["q"].shape[0], inputs["k"].shape[0]
    inner_width = inputs["active"].shape[1]
    chunks, rows = chunks_of(CHUNKS, PACK * 2 * seq_count, width)
    sems = len(chunks) * Sum.last
    rest_rows = rows - 2 * inner_width
    bf = lambda *shape: pltpu.VMEM(shape, jnp.bfloat16)
    f32 = lambda *shape: pltpu.VMEM(shape, jnp.float32)
    dma = pltpu.SemaphoreType.DMA
    vec_shape = inputs["vectors"].shape
    any_spec = pl.BlockSpec(memory_space=pl.ANY)
    vmem = pl.BlockSpec(memory_space=pltpu.VMEM)
    tiles = block_len // TILE
    held = SOONEST + SOONER + LATER
    return pl.pallas_call(
        functools.partial(finish_kernel, chunks, SCHEDULE, seq_count),
        in_specs=[vmem if name == "vectors" else any_spec for name in FINISH_IN],
        out_specs=[any_spec] * 3 + [vmem] * 2,
        out_shape=[
            jax.ShapeDtypeStruct((inner_width, width), jnp.bfloat16),
            jax.ShapeDtypeStruct((width, inner_width), jnp.bfloat16),
            jax.ShapeDtypeStruct((rest_rows, width), jnp.bfloat16),
            jax.ShapeDtypeStruct(vec_shape, jnp.float32),
            jax.ShapeDtypeStruct((block_len, width), jnp.bfloat16),
        ],
        scratch_shapes=[
            bf(2, 2, tiles, REACH, TILE), bf(PAIR, block_len), bf(PAIR, ext_len),
            f32(ext_len, PAIR), f32(ext_len, PAIR), f32(PAIR, 2 * SPAN), f32(PAIR, 2 * SPAN + 2 * TILE),
            bf(2 * block_len * (inner_width // width), width), bf(ext_len, width), bf(rows, width),
            bf(4 * SPAN, width), bf(width, block_len + 2 * SPAN), bf(width, ext_len + 2 * SPAN),
            bf(width, block_len), bf(ext_len, width), bf(2, SPAN, width), f32(block_len, width), bf(rows, width),
            f32(Sum.phases + 1, *vec_shape), f32(Sum.phases, *vec_shape),
            dma((len(chunks),)), dma((sems,)), dma((sems,)), dma((Sum.phases,)), dma((Sum.phases,)),
            dma((2,)), dma((2,)), dma((2,)), dma((len(held),)), dma((2 * (inner_width // width),)),
            *(pltpu.VMEM(inputs[name].shape, inputs[name].dtype) for name in held),
        ],
        compiler_params=pltpu.CompilerParams(
            collective_id=0, has_side_effects=True, vmem_limit_bytes=61 * 2**20
        ),
        name="finish",
    )(*(inputs[name] for name in FINISH_IN))


WIDEN_STEP = 512


def widen_pieces(shapes):
    pieces = []
    for number, (rows, cols) in enumerate(shapes):
        step = WIDEN_STEP * shapes[0][1] // cols
        pieces += [(number, at, min(step, rows - at)) for at in range(0, rows, step)]
    return pieces


def widen_kernel(shapes, splits, vec_rows, kept, *refs):
    count, total = len(shapes), len(splits)
    ins, vec_in, kept_in = refs[:count], refs[count], refs[count + 1 : count + 1 + kept]
    refs = refs[count + 1 + kept :]
    outs, vec_outs, kept_outs = refs[:total], refs[total : total + vec_rows], refs[total + vec_rows :][:kept]
    scratch = refs[total + vec_rows + kept :]
    narrow, wide = scratch[:count], scratch[count : 2 * count]
    held, (load_sem, store_sem, kept_sem) = scratch[2 * count : 2 * count + kept], scratch[2 * count + kept :]
    pieces = widen_pieces(shapes)
    loads = [
        pltpu.make_async_copy(
            ins[number].at[pl.ds(at, rows)], narrow[number].at[pl.ds(at, rows)], load_sem.at[i]
        )
        for i, (number, at, rows) in enumerate(pieces)
    ]
    for load in loads:
        load.start()
    fetches = [pltpu.make_async_copy(kept_in[i], held[i], kept_sem.at[i]) for i in range(kept)]
    stores = [pltpu.make_async_copy(held[i], kept_outs[i], kept_sem.at[i]) for i in range(kept)]
    for fetch in fetches:
        fetch.start()
    for number in range(vec_rows):
        vec_outs[number][...] = vec_in[number, :]
    for fetch, store in zip(fetches, stores):
        fetch.wait()
        store.start()
    for load, (number, at, rows) in zip(loads, pieces):
        load.wait()
        cols = shapes[number][1]
        step = 32 if cols <= 1024 else 16

        def body(i, carry, number=number, at=at, step=step):
            here = pl.ds(pl.multiple_of(at + i * step, PACK), step)
            wide[number][here, :] = narrow[number][here, :].astype(jnp.float32)
            return carry

        lax.fori_loop(0, rows // step, body, 0)
        for out, (source, first, high) in enumerate(splits):
            low_row, high_row = max(at, first), min(at + rows, first + high)
            if source == number and low_row < high_row:
                store = pltpu.make_async_copy(
                    wide[number].at[pl.ds(low_row, high_row - low_row)],
                    outs[out].at[pl.ds(low_row - first, high_row - low_row)],
                    store_sem.at[len(stores) - kept],
                )
                store.start()
                stores.append(store)
    for store in stores:
        store.wait()


def widen(arrays, splits, vectors, vec_rows, kept):
    shapes = [a.shape for a in arrays]
    pieces = widen_pieces(shapes)
    any_spec = pl.BlockSpec(memory_space=pl.ANY)
    vmem = pl.BlockSpec(memory_space=pltpu.VMEM)
    dma = pltpu.SemaphoreType.DMA
    width = vectors.shape[1]
    return pl.pallas_call(
        functools.partial(widen_kernel, shapes, splits, vec_rows, len(kept)),
        in_specs=[any_spec] * len(arrays) + [vmem] + [any_spec] * len(kept),
        out_specs=[any_spec] * len(splits) + [vmem] * vec_rows + [any_spec] * len(kept),
        out_shape=[
            *(jax.ShapeDtypeStruct((rows, shapes[number][1]), jnp.float32) for number, _, rows in splits),
            *(jax.ShapeDtypeStruct((width,), jnp.float32) for _ in range(vec_rows)),
            *(jax.ShapeDtypeStruct(a.shape, a.dtype) for a in kept),
        ],
        scratch_shapes=[
            *(pltpu.VMEM(shape, jnp.bfloat16) for shape in shapes),
            *(pltpu.VMEM(shape, jnp.float32) for shape in shapes),
            *(pltpu.VMEM(a.shape, a.dtype) for a in kept),
            dma((len(pieces),)), dma((len(pieces) + len(splits),)), dma((len(kept),)),
        ],
        compiler_params=pltpu.CompilerParams(vmem_limit_bytes=60 * 2**20),
        name="widen",
    )(*arrays, vectors, *kept)


def shifted(shard, axis, by):
    count = lax.axis_size(axis)
    pairs = [(i, i + by) for i in range(count) if 0 <= i + by < count]
    return lax.ppermute(shard, axis, pairs)


def f32dot(spec, left, right):
    return jnp.einsum(spec, left, right, preferred_element_type=jnp.float32)


def low(values):
    return values.astype(jnp.bfloat16)

def finish_plain(inputs):
    query, key_ext, value_ext = inputs["q"], inputs["k"], inputs["v"]
    block_len, width = query.shape
    w_query, w_key, w_value, hot = (inputs[name] for name in ("w_query", "w_key", "w_value", "hot"))
    dquery, dkey, dvalue, drelk, drelq = attend_back(
        query, key_ext, value_ext, inputs["grad"], inputs["probs_out"], inputs["relk"], inputs["relq"]
    )
    dkey = low(f32dot("ab,nbd->nad", unit(True), low(dkey).reshape(-1, TILE, width))).reshape(-1, width)
    dvalue = low(dvalue)
    drelk = low(drelk).T
    drelq = low(drelq[:, TILE : TILE + 2 * SPAN]).T
    query_part = f32dot("em,md->ed", jnp.concatenate([inputs["x"][SPAN : SPAN + block_len], inputs["from_table"]]).T, jnp.concatenate([dquery, drelq]))
    key_part = f32dot("em,md->ed", jnp.concatenate([inputs["x"], inputs["to_table"]]).T, jnp.concatenate([dkey, drelk]))
    value_part = f32dot("em,md->ed", inputs["x"].T, dvalue)
    table = jnp.concatenate(
        [low(f32dot("md,ed->me", drelk, w_key)), low(f32dot("md,ed->me", drelq, w_query))]
    )
    table_part = f32dot("rm,me->re", hot, table)
    output_part = f32dot("dt,te->de", inputs["attn_t"], inputs["mixed_low"])
    rest = low(jnp.concatenate([output_part, query_part, key_part, value_part, table_part]))
    outer_part = low(f32dot("tf,td->fd", inputs["active"], inputs["outer_low"]))
    inner_part = low(f32dot("td,tf->df", inputs["hidden_low"], inputs["inner_low"]))
    ext_grad = f32dot("td,ed->te", dkey, w_key) + f32dot("td,ed->te", dvalue, w_value)
    tokens_grad = (
        inputs["resid"]
        + f32dot("td,ed->te", dquery, w_query)
        + ext_grad[SPAN : SPAN + block_len]
        + shifted(low(ext_grad[:SPAN]), "seq", -1).astype(jnp.float32)
        + shifted(low(ext_grad[SPAN + block_len :]), "seq", 1).astype(jnp.float32)
    )
    both = ("rows", "seq")
    sums = [
        lax.all_gather(
            lax.psum_scatter(part, both, scatter_dimension=0, tiled=True), both, axis=0, tiled=True
        )
        for part in (outer_part, inner_part, rest)
    ]
    return (*sums, lax.psum(inputs["vectors"], both), low(tokens_grad))


def finish_of(inputs):
    seq_count, rows_count = lax.axis_size("seq"), lax.axis_size("rows")
    if rows_count == 2 and seq_count == 16:
        return finish(inputs, seq_count)
    return finish_plain(inputs)

def shards(
    tokens, cotangent, w_query, w_key, w_value, w_output, w_inner, w_outer, rel_table,
    mid_gain, mid_bias, end_gain, end_bias, seq_lengths, pad_mask, rel_buckets,
):
    width = tokens.shape[-1]
    inputs = {
        "tokens": tokens[0], "cotangent": cotangent[0], "rel_table": rel_table, "w_query": w_query,
        "w_key": w_key, "w_value": w_value, "w_output": w_output, "w_inner": w_inner, "w_outer": w_outer,
        "rel_buckets": rel_buckets, "mid_gain": mid_gain, "mid_bias": mid_bias, "end_gain": end_gain,
        "end_bias": end_bias, "keep": pad_mask.reshape(-1, TILE), "lengths": seq_lengths,
    }
    kept = start(inputs, lax.axis_size("seq"))
    layer_out = kept.pop("layer_out")
    inputs.update(kept)
    outer_w, inner_w, rest_w, norm_parts, tokens_grad = finish_of(inputs)
    splits = [(0, 0, outer_w.shape[0]), (1, 0, width)]
    splits += [(2, at * width, width) for at in range(4)] + [(2, 4 * width, rest_w.shape[0] - 4 * width)]
    values = widen([outer_w, inner_w, rest_w], splits, norm_parts, 4, [layer_out, tokens_grad])
    outer_w, inner_w, output_w, query_w, key_w, value_w, table_w, *norms = values
    *norms, layer_out, tokens_grad = norms
    return (
        layer_out[None], tokens_grad[None], query_w, key_w, value_w, output_w, inner_w, outer_w, table_w,
        *norms,
    )


def solution(mesh):
    split = P("rows", "seq", None)
    return jax.shard_map(
        shards,
        mesh=mesh,
        in_specs=(split, split) + (P(),) * 11 + (P("rows", None), P("rows", None), P()),
        out_specs=(split, split) + (P(),) * 11,
        check_vma=False,
    )
```
